256 devices in a mesh: img: 64 (over y, z, core), mp: 4 (over x).
Axes of the slice: x: 4, y: 4, z: 8, core: 2. Of those that a mesh axis runs over, the one named last changes fastest.
Arguments:
- patches: bfloat16 [512, 96, 1024], P('img'), may hold values from -5 to 5
- encoder_proj: bfloat16 [1024, 3, 1024], P(None, None, 'mp'), may hold values from -5.125 to 5.125
- encoder_out: bfloat16 [1024, 1024], P('mp'), may hold values from -0.1875 to 0.1875
- decoder_embed: bfloat16 [1024, 768], replicated, may hold values from -0.1875 to 0.1875
- decoder_proj: bfloat16 [768, 3, 768], P(None, None, 'mp'), may hold values from -5.9178403 to 5.9178403
- decoder_out: bfloat16 [768, 768], P('mp'), may hold values from -0.21875 to 0.21875
- head_weight: bfloat16 [768, 4], replicated, may hold values from -0.21875 to 0.21875
- partners: int32 [512, 8], P('img'), may hold values from 0 to 511, as said below
- depths: float32 [512, 96], P('img', 'mp'), may hold values from 1 to 4
- camera_poses: float32 [12, 512], P(None, 'img'), may hold values from -3 to 3
- valid_mask: int32 [512, 96], P('img', 'mp'), may hold values 0 or 1
Outputs:
- pointmap: float32 [4, 4096, 96], P(None, 'img', 'mp')
- new_depths: float32 [512, 96], P('img', 'mp')
- new_poses: float32 [12, 512], P(None, 'img')
The draws below stay inside these ranges and needn't reach their ends.
Inputs may be any that keep to these rules, and one draw needn't show every extreme that they name: partners[a, k] is never a. Among the 64 partners of the images of one device, at most 2 are held by any one device (images 8 o to 8 o + 7 for device o), and exactly 2 by each of half of the devices.
All inputs are finite; a program needn't handle non-finite values. No bound on the sum of `valid_mask` on one device may be relied on, other than what follows from the above.
Results may differ from the reference program's by a relative error of at most 0.012.
Values may be sent and summed in bfloat16 or wider, within the bound.
A program may use at most 128 MiB of HBM per device.

```python
import jax
import jax.numpy as jnp
from jax import lax

D = 1024
DD = 768
HEADS_ENC = 16
HEADS_DEC = 12
HD = 64
IMG_DEV = 8
TOK = 96
K = 8
IMAGES = 512
PAIRS = 4096
CAP = 2


def projection_draw(key, model_width):
    key_query, key_other, key_value = jax.random.split(key, 3)
    factor = model_width ** (-0.5)
    queries = jax.random.truncated_normal(key_query, -4.0, 4.0, (model_width, model_width), jnp.float32) * factor
    key_part = jax.random.truncated_normal(key_other, -4.0, 4.0, (model_width, model_width), jnp.float32) * factor
    value_part = jax.random.truncated_normal(key_value, -4.0, 4.0, (model_width, model_width), jnp.float32) * factor
    return jnp.stack([queries, key_part, value_part], axis=1).astype(jnp.bfloat16)


def draw_encoder_proj(key, part):
    key = jax.random.fold_in(key, 3)
    return projection_draw(key, D)


def draw_decoder_proj(key, part):
    key = jax.random.fold_in(key, 5)
    return projection_draw(key, DD)


def draw_patches(key, part):
    key = jax.random.fold_in(key, 1)
    key_fresh = jax.random.fold_in(key, 1)
    fresh_part = jax.random.normal(key_fresh, (IMAGES, TOK, D), jnp.float32)
    values = fresh_part
    return jnp.clip(values, -5.0, 5.0).astype(jnp.bfloat16)


def draw_camera_poses(key, part):
    key = jax.random.fold_in(key, 7)
    key_spread, key_shift = jax.random.split(key, 2)
    spread = 0.3 * jax.random.truncated_normal(key_spread, -3.0, 3.0, (12, IMAGES), jnp.float32)
    shifts = jax.random.truncated_normal(key_shift, -3.0, 3.0, (12, IMAGES), jnp.float32)
    identity_rows = jnp.array([1, 0, 0, 0, 0, 1, 0, 0, 0, 0, 1, 0], jnp.float32)[:, None]
    shift_rows = jnp.array([0, 0, 0, 1, 0, 0, 0, 1, 0, 0, 0, 1], jnp.float32)[:, None]
    return identity_rows + jnp.where(shift_rows > 0.5, shifts, spread)


def draw_partners(key, part):
    key = jax.random.fold_in(key, 11)
    key_order, key_local = jax.random.split(key, 2)
    devices = IMAGES // IMG_DEV
    pair_count = IMG_DEV * K
    raw = jax.random.randint(key_order, (devices, devices), 0, 1 << 20)
    ranked = raw * devices + jnp.arange(devices, dtype=jnp.int32)[None, :]
    orders = jnp.argsort(ranked, axis=1, stable=True).astype(jnp.int32)
    slot_index = jnp.arange(pair_count, dtype=jnp.int32)
    owners = orders[:, slot_index // CAP]
    local_index = jax.random.randint(key_local, (devices, pair_count), 0, IMG_DEV)
    own_image = (slot_index // K)[None, :]
    device_ids = jnp.arange(devices, dtype=jnp.int32)[:, None]
    clash = (owners == device_ids) & (local_index == own_image)
    local_index = jnp.where(clash, (local_index + 1) % IMG_DEV, local_index)
    return (owners * IMG_DEV + local_index).reshape(IMAGES, K).astype(jnp.int32)


def touch_ends(result, own_key, smallest, largest):
    extent = result.shape
    spot = [jax.random.randint(jax.random.fold_in(own_key, axis), (), 0, extent[axis]) for axis in range(len(extent))]
    result = result.at[tuple(spot)].set(smallest)
    longest = extent.index(max(extent))
    spot[longest] = (spot[longest] + 1) % extent[longest]
    return result.at[tuple(spot)].set(largest)


def block_levels(own_key, shape, pieces, low, top_value):
    factor_of, own = 1.0, jax.random.fold_in(own_key, 6)
    for position, parts in pieces:
        steps = jnp.exp(jax.random.uniform(jax.random.fold_in(own, position), (parts,), jnp.float32, low / len(pieces), top_value / len(pieces)))
        factor_of = factor_of * jnp.repeat(steps, shape[position] // parts).reshape([-1 if axis == position else 1 for axis in range(len(shape))])
    return factor_of


def gaussian(key, shape, deviation, most, shards=(), kind=jnp.bfloat16):
    factor_of = block_levels(key, shape, shards, -0.22, 0.18) if shards else 1.0
    entries = jax.random.normal(key, shape, jnp.float32) * deviation * factor_of
    return jnp.minimum(jnp.maximum(entries, -most), most).astype(kind)


def setup_inputs(seed: int = 0) -> dict:
    keys = jax.random.split(jax.random.key(seed), 12)
    return {
        "patches": draw_patches(jax.random.fold_in(keys[11], 71), 0),
        "encoder_proj": draw_encoder_proj(jax.random.fold_in(keys[11], 71), 0),
        "encoder_out": gaussian(keys[2], (D, D), D ** -0.5, 0.1875, ((0, 4),)),
        "decoder_embed": gaussian(keys[3], (D, DD), D ** -0.5, 0.1875),
        "decoder_proj": draw_decoder_proj(jax.random.fold_in(keys[11], 71), 0),
        "decoder_out": gaussian(keys[5], (DD, DD), DD ** -0.5, 0.21875, ((0, 4),)),
        "head_weight": gaussian(keys[6], (DD, 4), DD ** -0.5, 0.21875),
        "partners": draw_partners(jax.random.fold_in(keys[11], 71), 0),
        "depths": jnp.clip(1.0 + 3.0 * jax.random.uniform(keys[8], (IMAGES, TOK), jnp.float32) ** block_levels(keys[8], (IMAGES, TOK), ((0, 64), (1, 4)), -0.2, 0.2), 1.0, 4.0),
        "camera_poses": draw_camera_poses(jax.random.fold_in(keys[11], 71), 0),
        "valid_mask": touch_ends((jax.random.randint(keys[10], (IMAGES, TOK), 0, 4) < 3).astype(jnp.int32), jax.random.fold_in(keys[10], 1), 0, 1),
    }


epsilon = 1e-06
depth_step = 0.1
pose_step = 0.005

def norm_rows(values):
    average = lax.optimization_barrier(jnp.mean(values, axis=-1, keepdims=True))
    centred = values - average
    variance = lax.optimization_barrier(jnp.mean(centred * centred, axis=-1, keepdims=True))
    return (centred * lax.rsqrt(variance + epsilon)).astype(jnp.bfloat16)

def attend_one(query_rows, key_rows, value_rows):
    scores = jnp.einsum('qhd,thd->hqt', query_rows.astype(jnp.float32), key_rows.astype(jnp.float32)) * HD ** (-0.5)
    top_score = lax.optimization_barrier(jnp.max(scores, axis=-1, keepdims=True))
    expos = jnp.exp(scores - top_score)
    attn_weights = (expos / lax.optimization_barrier(jnp.sum(expos, axis=-1, keepdims=True))).astype(jnp.bfloat16)
    return jnp.einsum('hqt,thd->qhd', attn_weights.astype(jnp.float32), value_rows.astype(jnp.float32)).astype(jnp.bfloat16)

def make_rays(token_index, rows_total):
    column = (token_index % 16).astype(jnp.float32)
    row_pos = (token_index // 16).astype(jnp.float32)
    return jnp.stack([(column - 7.5) * 0.125, (row_pos - (rows_total - 1) * 0.5) * 0.125, jnp.ones_like(column)])

def align_loss(depth_map, pose_own, pose_far, points, confidence, weight, ray_dirs, loss_scale):
    summed = 0.0
    for component in range(3):
        world_pts = pose_own[4 * component + 3][:, None] + depth_map * (pose_own[4 * component][:, None] * ray_dirs[0] + pose_own[4 * component + 1][:, None] * ray_dirs[1] + pose_own[4 * component + 2][:, None] * ray_dirs[2])
        predicted = pose_far[4 * component + 3][:, :, None] + (pose_far[4 * component][:, :, None] * points[0] + pose_far[4 * component + 1][:, :, None] * points[1] + pose_far[4 * component + 2][:, :, None] * points[2])
        residual = world_pts[:, None, :] - predicted
        summed = summed + jnp.sum(weight[:, None, :] * confidence * residual * residual)
    return summed * loss_scale

def reference(patches, encoder_proj, encoder_out, decoder_embed, decoder_proj, decoder_out, head_weight, partners, depths, camera_poses, valid_mask):

    def encode(image_rows):
        normed = norm_rows(image_rows.astype(jnp.float32))
        projected = jnp.dot(normed, encoder_proj.reshape(D, 3 * D), preferred_element_type=jnp.float32)
        projected = projected.astype(jnp.bfloat16).reshape(TOK, 3, HEADS_ENC, HD)
        mixed_rows = attend_one(projected[:, 0], projected[:, 1], projected[:, 2]).reshape(TOK, D)
        encoded = image_rows.astype(jnp.float32) + jnp.dot(mixed_rows, encoder_out, preferred_element_type=jnp.float32)
        embedded = jnp.dot(norm_rows(encoded), decoder_embed, preferred_element_type=jnp.float32).astype(jnp.bfloat16)
        dec_rows = jnp.dot(norm_rows(embedded.astype(jnp.float32)), decoder_proj.reshape(DD, 3 * DD), preferred_element_type=jnp.float32)
        return (embedded, dec_rows.astype(jnp.bfloat16).reshape(TOK, 3, HEADS_DEC, HD))
    embedded_all, decoder_all = lax.map(encode, patches)

    def decode(image_item):
        own_rows, own_queries, partner_ids = image_item
        far_rows = decoder_all[partner_ids]
        mixed_rows = jax.vmap(lambda key_rows, value_rows: attend_one(own_queries, key_rows, value_rows))(far_rows[:, :, 1], far_rows[:, :, 2])
        mixed_rows = mixed_rows.reshape(K * TOK, DD)
        settled = jnp.dot(mixed_rows, decoder_out, preferred_element_type=jnp.float32).reshape(K, TOK, DD) + own_rows.astype(jnp.float32)[None]
        return jnp.dot(norm_rows(settled), head_weight, preferred_element_type=jnp.float32)
    head_out = lax.map(decode, (embedded_all, decoder_all[:, :, 0], partners))
    moved = jnp.moveaxis(head_out, 3, 0)
    points = moved[:3]
    confidence = 1.0 + jnp.exp(moved[3])
    pointmap = jnp.concatenate([points, confidence[None]], axis=0).reshape(4, PAIRS, TOK)
    rounded = lax.optimization_barrier(camera_poses.astype(jnp.bfloat16))
    far_pose = rounded.astype(jnp.float32)[:, partners]
    ray_dirs = make_rays(jnp.arange(TOK, dtype=jnp.int32), TOK // 16)
    weight = valid_mask.astype(jnp.float32)

    def loss_fn(depth_map, pose_own, pose_far):
        return align_loss(depth_map, pose_own, pose_far, points, confidence, weight, ray_dirs, 1.0 / TOK)
    loss_value, pullback = jax.vjp(loss_fn, depths, camera_poses, far_pose)
    grad_depth, grad_own, grad_far = pullback(jnp.ones_like(loss_value))
    far_sum = jax.ops.segment_sum(grad_far.reshape(12, -1).T, partners.reshape(-1), num_segments=IMAGES).T
    new_depths = depths - depth_step * grad_depth
    new_poses = camera_poses - pose_step * (grad_own + far_sum)
    return (pointmap, new_depths, new_poses)
```

```python
import jax
import jax.numpy as jnp
from jax import lax
from jax.sharding import PartitionSpec as P

HD = 64
K = 8


epsilon = 1e-06
depth_step = 0.1
pose_step = 0.005


def norm_rows(values):
    average = jnp.mean(values, axis=-1, keepdims=True)
    centred = values - average
    variance = jnp.mean(centred * centred, axis=-1, keepdims=True)
    return (centred * lax.rsqrt(variance + epsilon)).astype(jnp.bfloat16)


def soft_weights(scores):
    top_score = jnp.max(scores, axis=-1, keepdims=True)
    expos = jnp.exp(scores - top_score)
    return (expos / jnp.sum(expos, axis=-1, keepdims=True)).astype(jnp.bfloat16)


def make_rays(token_index, rows_total):
    column = (token_index % 16).astype(jnp.float32)
    row_pos = (token_index // 16).astype(jnp.float32)
    return jnp.stack(
        [(column - 7.5) * 0.125, (row_pos - (rows_total - 1) * 0.5) * 0.125, jnp.ones_like(column)]
    )


def align_loss(depth_map, pose_own, pose_far, points, confidence, weight, ray_dirs, loss_scale):
    summed = 0.0
    for component in range(3):
        world_pts = pose_own[4 * component + 3][:, None] + depth_map * (
            pose_own[4 * component][:, None] * ray_dirs[0]
            + pose_own[4 * component + 1][:, None] * ray_dirs[1]
            + pose_own[4 * component + 2][:, None] * ray_dirs[2]
        )
        predicted = pose_far[4 * component + 3][:, :, None] + (
            pose_far[4 * component][:, :, None] * points[0]
            + pose_far[4 * component + 1][:, :, None] * points[1]
            + pose_far[4 * component + 2][:, :, None] * points[2]
        )
        residual = world_pts[:, None, :] - predicted
        summed = summed + jnp.sum(weight[:, None, :] * confidence * residual * residual)
    return summed * loss_scale


def shards(
    patches,
    encoder_proj,
    encoder_out,
    decoder_embed,
    decoder_proj,
    decoder_out,
    head_weight,
    partners,
    depths,
    camera_poses,
    valid_mask,
):
    images, tokens, model_width = patches.shape
    dec_width = decoder_embed.shape[1]
    enc_local = encoder_proj.shape[2]
    dec_local = decoder_proj.shape[2]
    head_scale = HD ** (-0.5)
    split = lax.axis_size("mp")
    place = lax.axis_index("mp")
    own_count = images // split
    flat_partner = partners.reshape(-1)
    pair_count = flat_partner.shape[0]
    out_full = lax.all_gather(encoder_out, "mp", axis=0, tiled=True)
    proj_full = lax.all_gather(jnp.transpose(decoder_proj, (1, 2, 0)), "mp", axis=1, tiled=True)
    dec_out_full = lax.all_gather(decoder_out, "mp", axis=0, tiled=True)
    all_poses = lax.all_gather(camera_poses.astype(jnp.bfloat16), "img", axis=1, tiled=True)

    normed = norm_rows(patches.astype(jnp.float32))
    projected = jnp.dot(
        normed, encoder_proj.reshape(model_width, 3 * enc_local), preferred_element_type=jnp.float32
    )
    projected = projected.astype(jnp.bfloat16).reshape(images, tokens, 3, enc_local // HD, HD)
    scores = (
        jnp.einsum(
            "aqhd,athd->ahqt",
            projected[:, :, 0],
            projected[:, :, 1],
            preferred_element_type=jnp.float32,
        )
        * head_scale
    )
    mixed_rows = jnp.einsum(
        "ahqt,athd->aqhd",
        soft_weights(scores),
        projected[:, :, 2],
        preferred_element_type=jnp.float32,
    )
    mixed_rows = mixed_rows.astype(jnp.bfloat16).reshape(images, tokens, enc_local)
    mixed_own = lax.all_to_all(mixed_rows, "mp", split_axis=0, concat_axis=2, tiled=True)
    patch_own = lax.dynamic_slice_in_dim(patches, place * own_count, own_count, 0)
    encoded = patch_own.astype(jnp.float32) + jnp.dot(
        mixed_own, out_full, preferred_element_type=jnp.float32
    )
    embedded = jnp.dot(
        norm_rows(encoded), decoder_embed, preferred_element_type=jnp.float32
    ).astype(jnp.bfloat16)
    rows = norm_rows(embedded.astype(jnp.float32))
    quarter = lax.all_to_all(rows, "mp", split_axis=1, concat_axis=0, tiled=True)
    everything = lax.all_gather(quarter, "img", axis=0, tiled=True)
    picked = everything[flat_partner]
    far_rows = lax.all_to_all(picked, "mp", split_axis=0, concat_axis=1, tiled=True)
    own_pairs = pair_count // split

    def project(values, which):
        return lax.dot_general(
            values,
            proj_full[which],
            (((2,), (1,)), ((), ())),
            preferred_element_type=jnp.float32,
        ).astype(jnp.bfloat16)

    heads = dec_width // HD
    queries = project(rows, 0).reshape(own_count, tokens, heads, HD)
    far_keys = project(far_rows, 1).reshape(own_count, K, tokens, heads, HD)
    far_values = project(far_rows, 2).reshape(own_count, K, tokens, heads, HD)
    cross_scores = (
        jnp.einsum("aqhd,akthd->akhqt", queries, far_keys, preferred_element_type=jnp.float32)
        * head_scale
    )
    cross_rows = jnp.einsum(
        "akhqt,akthd->akqhd",
        soft_weights(cross_scores),
        far_values,
        preferred_element_type=jnp.float32,
    )
    cross_rows = cross_rows.astype(jnp.bfloat16).reshape(own_count, K, tokens, dec_width)
    settled = (
        jnp.dot(cross_rows, dec_out_full, preferred_element_type=jnp.float32)
        + embedded.astype(jnp.float32)[:, None]
    )
    head_own = lax.dot_general(
        head_weight,
        norm_rows(settled).reshape(own_pairs, tokens, dec_width),
        (((0,), (2,)), ((), ())),
        preferred_element_type=jnp.float32,
    )
    moved = lax.all_to_all(head_own, "mp", split_axis=2, concat_axis=1, tiled=True)
    token_share = tokens // split
    first_token = place * token_share
    points = moved[:3]
    confidence = 1.0 + jnp.exp(moved[3])
    pointmap = jnp.concatenate([points, confidence[None]], axis=0)
    ray_dirs = make_rays(first_token + jnp.arange(token_share, dtype=jnp.int32), tokens // 16)
    weight = valid_mask.astype(jnp.float32)
    pose_far = all_poses[:, flat_partner].astype(jnp.float32).reshape(12, images, K)
    point_grid = points.reshape(3, images, K, token_share)
    conf_grid = confidence.reshape(images, K, token_share)

    def loss_fn(depth_map, pose_own, pose_other):
        return align_loss(
            depth_map, pose_own, pose_other, point_grid, conf_grid, weight, ray_dirs, 1.0 / tokens
        )

    loss_value, pullback = jax.vjp(loss_fn, depths, camera_poses, pose_far)
    grad_depth, grad_own, grad_far = pullback(jnp.ones_like(loss_value))
    grad_far_flat = grad_far.reshape(12, pair_count)
    groups = lax.axis_size("img")
    total_images = groups * images
    base_image = lax.axis_index("img") * images
    image_ids = jnp.arange(total_images, dtype=jnp.int32)
    partner_hits = (flat_partner[:, None] == image_ids[None, :]).astype(jnp.float32)
    own_hits = (
        (base_image + jnp.arange(images, dtype=jnp.int32))[:, None] == image_ids[None, :]
    ).astype(jnp.float32)
    dense_grad = jnp.dot(grad_far_flat, partner_hits, precision=lax.Precision.HIGHEST) + jnp.dot(
        grad_own, own_hits, precision=lax.Precision.HIGHEST
    )
    summed = lax.psum(dense_grad, ("img", "mp"))
    grad_pose = lax.dynamic_slice_in_dim(summed, base_image, images, 1)
    new_depths = depths - depth_step * grad_depth
    new_poses = camera_poses - pose_step * grad_pose
    return (pointmap, new_depths, new_poses)


def solution(mesh):
    placed = (
        P("img", None, None),
        P(None, None, "mp"),
        P("mp", None),
        P(),
        P(None, None, "mp"),
        P("mp", None),
        P(),
        P("img", None),
        P("img", "mp"),
        P(None, "img"),
        P("img", "mp"),
    )
    return jax.shard_map(
        shards,
        mesh=mesh,
        in_specs=placed,
        out_specs=(P(None, "img", "mp"), P("img", "mp"), P(None, "img")),
        check_vma=False,
    )
```

```python
import jax
import jax.numpy as jnp
from jax import lax
from jax.experimental import pallas as pl
from jax.experimental.pallas import tpu as pltpu
from jax.sharding import PartitionSpec as P

HD = 64
K = 8


epsilon = 1e-06
depth_step = 0.1
pose_step = 0.005


def norm_rows(values):
    average = jnp.mean(values, axis=-1, keepdims=True)
    centred = values - average
    variance = jnp.mean(centred * centred, axis=-1, keepdims=True)
    return (centred * lax.rsqrt(variance + epsilon)).astype(jnp.bfloat16)


def soft_weights(scores):
    top_score = jnp.max(scores, axis=-1, keepdims=True)
    expos = jnp.exp(scores - top_score)
    return (expos / jnp.sum(expos, axis=-1, keepdims=True)).astype(jnp.bfloat16)


def make_rays(token_index, rows_total):
    column = (token_index % 16).astype(jnp.float32)
    row_pos = (token_index // 16).astype(jnp.float32)
    return jnp.stack(
        [(column - 7.5) * 0.125, (row_pos - (rows_total - 1) * 0.5) * 0.125, jnp.ones_like(column)]
    )


def align_loss(depth_map, pose_own, pose_far, points, confidence, weight, ray_dirs, loss_scale):
    summed = 0.0
    for component in range(3):
        world_pts = pose_own[4 * component + 3][:, None] + depth_map * (
            pose_own[4 * component][:, None] * ray_dirs[0]
            + pose_own[4 * component + 1][:, None] * ray_dirs[1]
            + pose_own[4 * component + 2][:, None] * ray_dirs[2]
        )
        predicted = pose_far[4 * component + 3][:, :, None] + (
            pose_far[4 * component][:, :, None] * points[0]
            + pose_far[4 * component + 1][:, :, None] * points[1]
            + pose_far[4 * component + 2][:, :, None] * points[2]
        )
        residual = world_pts[:, None, :] - predicted
        summed = summed + jnp.sum(weight[:, None, :] * confidence * residual * residual)
    return summed * loss_scale


YS, ZS, CORES = 4, 8, 2
FIRST = 5
MESH = pl.DeviceIdType.MESH


def link_plan(images):
    latency = 1.0
    split = {"z": (0, FIRST), "y": (FIRST, images)}
    free = {"y+": 0.0, "y-": 0.0, "z+": 0.0, "z-": 0.0}
    arrivals = []

    def push(now, link, source, target, span):
        begin = max(now, free[link])
        free[link] = begin + (span[1] - span[0])
        arrivals.append((free[link] + latency, len(arrivals), link, source, target, span))

    def forward(now, dy, dz, span):
        if span[1] <= FIRST:
            low, high = split["z"]
            half = (low + high + 1) // 2
            if dy == 0:
                if dz in (0, 1, 2):
                    push(now, "z+", (dy, dz), (dy, dz + 1), span)
                if dz == 3:
                    push(now, "z+", (dy, dz), (dy, 4), (low, half))
                if dz in (0, 7, 6):
                    push(now, "z-", (dy, dz), (dy, (dz - 1) % ZS), span)
                if dz == 5:
                    push(now, "z-", (dy, dz), (dy, 4), (half, high))
                push(now, "y+", (dy, dz), (1, dz), span)
                push(now, "y-", (dy, dz), (3, dz), span)
            if dy == 1 and dz % 2 == 0:
                push(now, "y+", (dy, dz), (2, dz), span)
            if dy == 3 and dz % 2 == 1:
                push(now, "y-", (dy, dz), (2, dz), span)
        else:
            low, high = split["y"]
            half = (low + high + 1) // 2
            if dz == 0:
                if dy == 0:
                    push(now, "y+", (0, 0), (1, 0), span)
                    push(now, "y-", (0, 0), (3, 0), span)
                if dy == 1:
                    push(now, "y+", (1, 0), (2, 0), (low, half))
                if dy == 3:
                    push(now, "y-", (3, 0), (2, 0), (half, high))
            if dz in (0, 1, 2):
                push(now, "z+", (dy, dz), (dy, dz + 1), span)
            if dz == 3 and dy < 2:
                push(now, "z+", (dy, dz), (dy, 4), span)
            if dz in (0, 7, 6):
                push(now, "z-", (dy, dz), (dy, (dz - 1) % ZS), span)
            if dz == 5 and dy >= 2:
                push(now, "z-", (dy, dz), (dy, 4), span)

    forward(0.0, 0, 0, split["z"])
    forward(0.0, 0, 0, split["y"])
    sent = []
    steps = [("send", list(range(len(arrivals))))]
    waited = set()
    while len(waited) < len(arrivals):
        entry = min(e for e in arrivals if e[1] not in waited)
        waited.add(entry[1])
        before = len(arrivals)
        forward(entry[0], entry[4][0], entry[4][1], entry[5])
        steps.append(("wait", entry[1]))
        steps.append(("send", list(range(before, len(arrivals)))))
    by_number = sorted(arrivals, key=lambda e: e[1])
    return steps, [e[2:] for e in by_number]


def exchange_kernel(
    pick_ref,
    rows_ref,
    emb_ref,
    weights_ref,
    pose_ref,
    far_ref,
    own_ref,
    weights_all,
    pose_all,
    held,
    staged,
    ring_send,
    ring_recv,
    twin_send,
    twin_recv,
    line_send,
    line_recv,
    pose_send,
    pose_recv,
    local_sem,
):
    images = rows_ref.shape[0]
    here = lax.axis_index("img")
    me = lax.axis_index("mp")
    core = lax.rem(here, 2)
    z = lax.rem(here // 2, ZS)
    y = here // (2 * ZS)
    split = far_ref.shape[1]
    per_dev = far_ref.shape[0]

    def spot(yy, zz, cc):
        return ((yy * ZS + zz) * 2 + cc, me)

    def mate(step):
        return (here, lax.rem(me + step, split))

    twin = spot(y, z, 1 - core)
    links = {
        "y+": spot(lax.rem(y + 1, YS), z, core),
        "y-": spot(lax.rem(y + YS - 1, YS), z, core),
        "z+": spot(y, lax.rem(z + 1, ZS), core),
        "z-": spot(y, lax.rem(z + ZS - 1, ZS), core),
    }
    line = [(dz, dc) for dz in range(ZS) for dc in range(CORES) if dz or dc]

    def line_peer(dz, dc, sign):
        return spot(y, lax.rem(z + ZS + sign * dz, ZS), lax.rem(core + dc, 2))

    def y_peer(dy, sign):
        return spot(lax.rem(y + YS + sign * dy, YS), z, core)

    barrier = pltpu.get_barrier_semaphore()
    peers = [line_peer(dz, dc, 1) for dz, dc in line]
    peers += [y_peer(dy, 1) for dy in range(1, YS)]
    peers += [mate(step) for step in range(1, split)]
    for peer in peers:
        pl.semaphore_signal(barrier, inc=1, device_id=peer, device_id_type=MESH)
    held[pl.ds(0, images)] = rows_ref[...]
    pose_all[here] = pose_ref[...]
    pl.semaphore_wait(barrier, len(peers))

    def remote(source, target, send, recv, device):
        return pltpu.make_async_remote_copy(
            src_ref=source,
            dst_ref=target,
            send_sem=send,
            recv_sem=recv,
            device_id=device,
            device_id_type=MESH,
        )

    steps, plan = link_plan(images)

    def block(side, slot, span):
        first = ((side * YS + slot[0]) * ZS + slot[1]) * images
        return held.at[pl.ds(first + span[0], span[1] - span[0])]

    def ring(number):
        link, source, target, span = plan[number]
        return remote(
            block(0, source, span),
            block(0, target, span),
            ring_send.at[number],
            ring_recv.at[number],
            links[link],
        )

    twins = [((0, 0), (0, images))] + [(entry[2], entry[3]) for entry in plan]

    def twin_copy(number):
        slot, span = twins[number]
        return remote(
            block(0, slot, span),
            block(1, slot, span),
            twin_send.at[number],
            twin_recv.at[number],
            twin,
        )

    for number in steps[0][1]:
        ring(number).start()
    twin_copy(0).start()

    def pose_line(dz, dc, number, slot):
        return remote(
            pose_all.at[slot],
            pose_all.at[slot],
            pose_send.at[number],
            pose_recv.at[number],
            line_peer(dz, dc, 1),
        )

    for number, (dz, dc) in enumerate(line):
        pose_line(dz, dc, number, here).start()

    pair_images = images // split

    def own_copy(step, slot):
        return remote(
            emb_ref.at[pl.ds(pair_images * lax.rem(me + step, split), pair_images)],
            own_ref.at[:, slot],
            line_send.at[step],
            line_recv.at[step],
            mate(step),
        )

    def weight_copy(step, slot):
        return remote(
            weights_ref.at[pl.ds(2 * core, 2)],
            weights_all.at[pl.ds(2 * core, 2), slot],
            line_send.at[split + step],
            line_recv.at[split + step],
            mate(step),
        )

    def weight_twin(step, half, slot):
        return remote(
            weights_all.at[pl.ds(2 * half, 2), slot],
            weights_all.at[pl.ds(2 * half, 2), slot],
            line_send.at[2 * split + step],
            line_recv.at[2 * split + step],
            twin,
        )

    def far_copy(step, slot):
        return remote(
            staged.at[pl.ds(per_dev * lax.rem(me + step, split), per_dev)],
            far_ref.at[:, slot],
            line_send.at[3 * split + step],
            line_recv.at[3 * split + step],
            mate(step),
        )

    for step in range(1, split):
        own_copy(step, me).start()
        weight_copy(step, me).start()
    own_local = pltpu.make_async_copy(
        emb_ref.at[pl.ds(pair_images * me, pair_images)], own_ref.at[:, me], local_sem.at[0]
    )
    own_local.start()
    weight_local = pltpu.make_async_copy(weights_ref, weights_all.at[:, me], local_sem.at[1])
    weight_local.start()

    def run(part):
        for kind, what in part:
            if kind == "wait":
                ring(what).wait_recv()
                twin_copy(1 + what).start()
            else:
                for number in what:
                    ring(number).start()

    third = len(steps) // 3
    run(steps[1:third])
    for number, (dz, dc) in enumerate(line):
        source = line_peer(dz, dc, -1)[0]
        pose_line(dz, dc, number, source).wait_recv()

    def pose_cross(dy, row):
        return remote(
            pose_all.at[pl.ds(row * 2 * ZS, 2 * ZS)],
            pose_all.at[pl.ds(row * 2 * ZS, 2 * ZS)],
            pose_send.at[len(line) + dy - 1],
            pose_recv.at[len(line) + dy - 1],
            y_peer(dy, 1),
        )

    for dy in range(1, YS):
        pose_cross(dy, y).start()
    run(steps[third : 2 * third])
    for step in range(1, split):
        source = lax.rem(me + split - step, split)
        weight_copy(step, source).wait_recv()
        weight_twin(step, core, source).start()
    run(steps[2 * third :])
    for number in range(len(twins)):
        twin_copy(number).wait_recv()

    def pick(index, carry):
        staged[index] = held[pick_ref[index]]
        return carry

    lax.fori_loop(0, per_dev * split, pick, 0)
    for step in (2, 1, 3):
        far_copy(step, me).start()
    far_local = pltpu.make_async_copy(
        staged.at[pl.ds(per_dev * me, per_dev)], far_ref.at[:, me], local_sem.at[2]
    )
    far_local.start()
    for dy in range(1, YS):
        pose_cross(dy, lax.rem(y + YS - dy, YS)).wait_recv()
    for step in range(1, split):
        source = lax.rem(me + split - step, split)
        own_copy(step, source).wait_recv()
        weight_twin(step, 1 - core, source).wait_recv()
    own_local.wait()
    weight_local.wait()
    for number in range(len(plan)):
        ring(number).wait_send()
    for number in range(len(twins)):
        twin_copy(number).wait_send()
    for number, (dz, dc) in enumerate(line):
        pose_line(dz, dc, number, here).wait_send()
    for dy in range(1, YS):
        pose_cross(dy, y).wait_send()
    for step in range(1, split):
        own_copy(step, me).wait_send()
        weight_copy(step, me).wait_send()
        weight_twin(step, core, lax.rem(me + split - step, split)).wait_send()
    for step in (1, 3, 2):
        source = lax.rem(me + split - step, split)
        far_copy(step, source).wait_recv()
        far_copy(step, me).wait_send()
    far_local.wait()


def exchange(pick, rows, emb, weights, pose, pairs, groups, split):
    images, share, width = rows.shape
    count = len(link_plan(images)[1])
    vmem = pl.BlockSpec(memory_space=pltpu.VMEM)
    return pl.pallas_call(
        exchange_kernel,
        out_shape=(
            jax.ShapeDtypeStruct((pairs // split, split, share, width), jnp.bfloat16),
            jax.ShapeDtypeStruct((images // split, split, share, width), jnp.bfloat16),
            jax.ShapeDtypeStruct((4, split) + weights.shape[1:], jnp.bfloat16),
            jax.ShapeDtypeStruct((groups,) + pose.shape, jnp.bfloat16),
        ),
        in_specs=[pl.BlockSpec(memory_space=pltpu.SMEM)] + [vmem] * 4,
        out_specs=(vmem,) * 4,
        scratch_shapes=[
            pltpu.VMEM((groups * images, share, width), jnp.bfloat16),
            pltpu.VMEM((pairs, share, width), jnp.bfloat16),
            pltpu.SemaphoreType.DMA((count,)),
            pltpu.SemaphoreType.DMA((count,)),
            pltpu.SemaphoreType.DMA((count + 1,)),
            pltpu.SemaphoreType.DMA((count + 1,)),
            pltpu.SemaphoreType.DMA((4 * split,)),
            pltpu.SemaphoreType.DMA((4 * split,)),
            pltpu.SemaphoreType.DMA((2 * ZS + YS,)),
            pltpu.SemaphoreType.DMA((2 * ZS + YS,)),
            pltpu.SemaphoreType.DMA((3,)),
        ],
        compiler_params=pltpu.CompilerParams(
            collective_id=0, has_side_effects=True, vmem_limit_bytes=56 * 2**20
        ),
        name="exchange",
    )(pick, rows, emb, weights, pose)


def reduce_kernel(
    grad_ref, total_ref, across, summed, lined, part, crossed, x_send, x_recv, l_send, l_recv, c_send, c_recv
):
    here = lax.axis_index("img")
    me = lax.axis_index("mp")
    core = lax.rem(here, 2)
    z = lax.rem(here // 2, ZS)
    y = here // (2 * ZS)
    split = across.shape[0]
    row = z * 2 + core
    rows = 2 * ZS
    line = [(dz, dc) for dz in range(ZS) for dc in range(CORES) if dz or dc]

    def line_row(dz, dc, sign):
        return lax.rem(z + ZS + sign * dz, ZS) * 2 + lax.rem(core + dc, 2)

    def mate(step):
        return (here, lax.rem(me + step, split))

    barrier = pltpu.get_barrier_semaphore()
    for step in range(1, split):
        pl.semaphore_signal(barrier, inc=1, device_id=mate(step), device_id_type=MESH)
    for dz, dc in line:
        pl.semaphore_signal(
            barrier, inc=1, device_id=(y * rows + line_row(dz, dc, 1), me), device_id_type=MESH
        )
    for other in range(YS):
        pl.semaphore_signal(barrier, inc=1, device_id=(other * rows + row, y), device_id_type=MESH)

    pl.semaphore_wait(barrier, split - 1 + len(line) + YS)

    def remote(source, target, send, recv, device):
        return pltpu.make_async_remote_copy(
            src_ref=source,
            dst_ref=target,
            send_sem=send,
            recv_sem=recv,
            device_id=device,
            device_id_type=MESH,
        )

    def x_copy(step, slot):
        return remote(
            grad_ref.at[lax.rem(me + step, split)],
            across.at[slot],
            x_send.at[step],
            x_recv.at[step],
            mate(step),
        )

    for step in range(1, split):
        x_copy(step, me).start()
    across[me] = grad_ref[me]
    for step in range(1, split):
        x_copy(step, lax.rem(me + split - step, split)).wait_recv()
    summed[...] = jnp.sum(across[...], axis=0)

    def l_copy(number, dz, dc, slot):
        target = line_row(dz, dc, 1)
        return remote(
            summed.at[target],
            lined.at[slot],
            l_send.at[number],
            l_recv.at[number],
            (y * rows + target, me),
        )

    for number, (dz, dc) in enumerate(line):
        l_copy(number, dz, dc, row).start()
    lined[row] = summed[row]
    for number, (dz, dc) in enumerate(line):
        l_copy(number, dz, dc, line_row(dz, dc, -1)).wait_recv()
    part[...] = jnp.sum(lined[...], axis=0)

    def c_copy(other, slot):
        return remote(
            part, crossed.at[slot], c_send.at[other], c_recv.at[slot], (me * rows + row, other)
        )

    for other in range(split):

        @pl.when(jnp.logical_or(y != me, me != other))
        def _():
            c_copy(other, y).start()

    @pl.when(y == me)
    def _():
        crossed[y] = part[...]

    for other in range(YS):

        @pl.when(jnp.logical_or(y != me, y != other))
        def _():
            c_copy(0, other).wait_recv()

    total_ref[...] = jnp.sum(crossed[...], axis=0)
    for step in range(1, split):
        x_copy(step, me).wait_send()
    for number, (dz, dc) in enumerate(line):
        l_copy(number, dz, dc, row).wait_send()
    for other in range(split):

        @pl.when(jnp.logical_or(y != me, me != other))
        def _():
            c_copy(other, y).wait_send()


def reduce_poses(dense, split):
    groups = dense.shape[0] * dense.shape[1]
    tile = dense.shape[2:]
    vmem = pl.BlockSpec(memory_space=pltpu.VMEM)
    rows = 2 * ZS
    return pl.pallas_call(
        reduce_kernel,
        out_shape=jax.ShapeDtypeStruct(tile, jnp.float32),
        in_specs=[vmem],
        out_specs=vmem,
        scratch_shapes=[
            pltpu.VMEM((split, rows) + tile, jnp.float32),
            pltpu.VMEM((rows,) + tile, jnp.float32),
            pltpu.VMEM((rows,) + tile, jnp.float32),
            pltpu.VMEM(tile, jnp.float32),
            pltpu.VMEM((YS,) + tile, jnp.float32),
            pltpu.SemaphoreType.DMA((split,)),
            pltpu.SemaphoreType.DMA((split,)),
            pltpu.SemaphoreType.DMA((rows,)),
            pltpu.SemaphoreType.DMA((rows,)),
            pltpu.SemaphoreType.DMA((split,)),
            pltpu.SemaphoreType.DMA((YS,)),
        ],
        compiler_params=pltpu.CompilerParams(collective_id=1, has_side_effects=True),
        name="reduce_poses",
    )(dense)


def shards(
    patches,
    encoder_proj,
    encoder_out,
    decoder_embed,
    decoder_proj,
    decoder_out,
    head_weight,
    partners,
    depths,
    camera_poses,
    valid_mask,
):
    images, tokens, model_width = patches.shape
    dec_width = decoder_embed.shape[1]
    enc_local = encoder_proj.shape[2]
    dec_local = decoder_proj.shape[2]
    head_scale = HD ** (-0.5)
    split = lax.axis_size("mp")
    place = lax.axis_index("mp")
    own_count = images // split
    flat_partner = partners.reshape(-1)
    pair_count = flat_partner.shape[0]
    out_full = lax.all_gather(encoder_out, "mp", axis=0, tiled=True)
    groups = lax.axis_size("img")
    here = lax.axis_index("img")
    weights = jnp.concatenate([jnp.transpose(decoder_proj, (1, 2, 0)), decoder_out[None]], axis=0)
    pose_tile = jnp.pad(
        camera_poses.astype(jnp.bfloat16), ((0, 4), (0, 128 - camera_poses.shape[1]))
    )

    normed = norm_rows(patches.astype(jnp.float32))
    projected = jnp.dot(
        normed, encoder_proj.reshape(model_width, 3 * enc_local), preferred_element_type=jnp.float32
    )
    projected = projected.astype(jnp.bfloat16).reshape(images, tokens, 3, enc_local // HD, HD)
    scores = (
        jnp.einsum(
            "aqhd,athd->ahqt",
            projected[:, :, 0],
            projected[:, :, 1],
            preferred_element_type=jnp.float32,
        )
        * head_scale
    )
    mixed_rows = jnp.einsum(
        "ahqt,athd->aqhd",
        soft_weights(scores),
        projected[:, :, 2],
        preferred_element_type=jnp.float32,
    )
    mixed_rows = mixed_rows.astype(jnp.bfloat16).reshape(images, tokens, enc_local)
    token_share = tokens // split
    first_token = place * token_share
    mixed_own = lax.all_to_all(mixed_rows, "mp", split_axis=1, concat_axis=2, tiled=True)
    patch_own = lax.dynamic_slice_in_dim(patches, first_token, token_share, 1)
    encoded = patch_own.astype(jnp.float32) + jnp.dot(
        mixed_own, out_full, preferred_element_type=jnp.float32
    )
    emb_share = jnp.dot(
        norm_rows(encoded), decoder_embed, preferred_element_type=jnp.float32
    ).astype(jnp.bfloat16)
    rows_share = norm_rows(emb_share.astype(jnp.float32))
    owner = flat_partner // images
    shift_y = (here // (2 * ZS) - owner // (2 * ZS)) % YS
    shift_z = ((here // 2) % ZS - (owner // 2) % ZS) % ZS
    shift_core = (here - owner) % 2
    pick = ((shift_core * YS + shift_y) * ZS + shift_z) * images + flat_partner % images
    far_rows, own_rows, weights_full, pose_tiles = exchange(
        pick, rows_share, emb_share, weights, pose_tile, pair_count, groups, split
    )
    far_rows = far_rows.reshape(pair_count // split, tokens, dec_width)
    embedded = own_rows.reshape(own_count, tokens, dec_width)
    rows = norm_rows(embedded.astype(jnp.float32))
    proj_full = weights_full.reshape(4, dec_width, dec_width)
    dec_out_full = proj_full[3]
    own_pairs = pair_count // split

    def project(values, which):
        return lax.dot_general(
            values,
            proj_full[which],
            (((2,), (1,)), ((), ())),
            preferred_element_type=jnp.float32,
        ).astype(jnp.bfloat16)

    heads = dec_width // HD
    queries = project(rows, 0).reshape(own_count, tokens, heads, HD)
    far_keys = project(far_rows, 1).reshape(own_count, K, tokens, heads, HD)
    far_values = project(far_rows, 2).reshape(own_count, K, tokens, heads, HD)
    cross_scores = (
        jnp.einsum("aqhd,akthd->akhqt", queries, far_keys, preferred_element_type=jnp.float32)
        * head_scale
    )
    cross_rows = jnp.einsum(
        "akhqt,akthd->akqhd",
        soft_weights(cross_scores),
        far_values,
        preferred_element_type=jnp.float32,
    )
    cross_rows = cross_rows.astype(jnp.bfloat16).reshape(own_count, K, tokens, dec_width)
    settled = (
        jnp.dot(cross_rows, dec_out_full, preferred_element_type=jnp.float32)
        + embedded.astype(jnp.float32)[:, None]
    )
    head_own = lax.dot_general(
        head_weight,
        norm_rows(settled).reshape(own_pairs, tokens, dec_width),
        (((0,), (2,)), ((), ())),
        preferred_element_type=jnp.float32,
    )
    moved = lax.all_to_all(head_own, "mp", split_axis=2, concat_axis=1, tiled=True)
    points = moved[:3]
    confidence = 1.0 + jnp.exp(moved[3])
    pointmap = jnp.concatenate([points, confidence[None]], axis=0)
    ray_dirs = make_rays(first_token + jnp.arange(token_share, dtype=jnp.int32), tokens // 16)
    weight = valid_mask.astype(jnp.float32)
    pose_table = pose_tiles[:, :12, :images].transpose(1, 0, 2).reshape(12, groups * images)
    pose_far = pose_table[:, flat_partner].astype(jnp.float32).reshape(12, images, K)
    point_grid = points.reshape(3, images, K, token_share)
    conf_grid = confidence.reshape(images, K, token_share)

    def loss_fn(depth_map, pose_own, pose_other):
        return align_loss(
            depth_map, pose_own, pose_other, point_grid, conf_grid, weight, ray_dirs, 1.0 / tokens
        )

    loss_value, pullback = jax.vjp(loss_fn, depths, camera_poses, pose_far)
    grad_depth, grad_own, grad_far = pullback(jnp.ones_like(loss_value))
    grad_far_flat = grad_far.reshape(12, pair_count)
    total_images = groups * images
    base_image = lax.axis_index("img") * images
    image_ids = jnp.arange(total_images, dtype=jnp.int32)
    partner_hits = (flat_partner[:, None] == image_ids[None, :]).astype(jnp.float32)
    own_hits = (
        (base_image + jnp.arange(images, dtype=jnp.int32))[:, None] == image_ids[None, :]
    ).astype(jnp.float32)
    dense_grad = jnp.dot(grad_far_flat, partner_hits, precision=lax.Precision.HIGHEST) + jnp.dot(
        grad_own, own_hits, precision=lax.Precision.HIGHEST
    )
    dense_rows = dense_grad.reshape(12, groups, images).transpose(1, 0, 2).reshape(groups, 1, -1)
    dense_rows = jnp.pad(dense_rows, ((0, 0), (0, 7), (0, 128 - 12 * images)))
    total = reduce_poses(dense_rows.reshape(YS, 2 * ZS, 8, 128), split)
    grad_pose = total[0, : 12 * images].reshape(12, images)
    new_depths = depths - depth_step * grad_depth
    new_poses = camera_poses - pose_step * grad_pose
    return (pointmap, new_depths, new_poses)


def solution(mesh):
    placed = (
        P("img", None, None),
        P(None, None, "mp"),
        P("mp", None),
        P(),
        P(None, None, "mp"),
        P("mp", None),
        P(),
        P("img", None),
        P("img", "mp"),
        P(None, "img"),
        P("img", "mp"),
    )
    return jax.shard_map(
        shards,
        mesh=mesh,
        in_specs=placed,
        out_specs=(P(None, "img", "mp"), P("img", "mp"), P(None, "img")),
        check_vma=False,
    )
```

```python
import functools

import jax
import jax.numpy as jnp
from jax import lax
from jax.experimental import pallas as pl
from jax.experimental.pallas import tpu as pltpu
from jax.sharding import PartitionSpec as P

HD = 64
K = 8


epsilon = 1e-06
depth_step = 0.1
pose_step = 0.005


def norm_rows(values):
    average = jnp.mean(values, axis=-1, keepdims=True)
    centred = values - average
    variance = jnp.mean(centred * centred, axis=-1, keepdims=True)
    return (centred * lax.rsqrt(variance + epsilon)).astype(jnp.bfloat16)


def soft_weights(scores):
    top_score = jnp.max(scores, axis=-1, keepdims=True)
    expos = jnp.exp(scores - top_score)
    return (expos / jnp.sum(expos, axis=-1, keepdims=True)).astype(jnp.bfloat16)


def make_rays(token_index, rows_total):
    column = (token_index % 16).astype(jnp.float32)
    row_pos = (token_index // 16).astype(jnp.float32)
    return jnp.stack(
        [(column - 7.5) * 0.125, (row_pos - (rows_total - 1) * 0.5) * 0.125, jnp.ones_like(column)]
    )


def align_loss(depth_map, pose_own, pose_far, points, confidence, weight, ray_dirs, loss_scale):
    summed = 0.0
    for component in range(3):
        world_pts = pose_own[4 * component + 3][:, None] + depth_map * (
            pose_own[4 * component][:, None] * ray_dirs[0]
            + pose_own[4 * component + 1][:, None] * ray_dirs[1]
            + pose_own[4 * component + 2][:, None] * ray_dirs[2]
        )
        predicted = pose_far[4 * component + 3][:, :, None] + (
            pose_far[4 * component][:, :, None] * points[0]
            + pose_far[4 * component + 1][:, :, None] * points[1]
            + pose_far[4 * component + 2][:, :, None] * points[2]
        )
        residual = world_pts[:, None, :] - predicted
        summed = summed + jnp.sum(weight[:, None, :] * confidence * residual * residual)
    return summed * loss_scale


YS, ZS, CORES = 4, 8, 2
FIRST = 5
WIDTHS = (384, 384)
RELAY = 18
AHEAD, DELAY = 4.0, 4.0
MESH = pl.DeviceIdType.MESH


def link_plan(images, spans):
    split = {"z": (0, FIRST), "y": (FIRST, images)}
    full = sum(spans)
    waiting = {"y+": [], "y-": [], "z+": [], "z-": []}
    free = {link: 0.0 for link in waiting}
    plan, flight, steps = [], [], []

    def push(now, chunk, link, source, target, span):
        waiting[link].append((chunk, len(waiting[link]) + 1000 * now, source, target, span))

    def issue(now):
        for link, queue in waiting.items():
            while queue and free[link] <= now + AHEAD:
                entry = min(queue)
                queue.remove(entry)
                chunk, _, source, target, span = entry
                free[link] = max(now, free[link]) + (span[1] - span[0]) * spans[chunk] / full
                flight.append((free[link] + DELAY, len(plan)))
                steps.append(("send", len(plan)))
                plan.append((chunk, link, source, target, span))

    def forward(now, chunk, dy, dz, span):
        if span[1] <= FIRST:
            low, high = split["z"]
            half = (low + high + 1) // 2
            if dy == 0:
                if dz in (0, 1, 2):
                    push(now, chunk, "z+", (dy, dz), (dy, dz + 1), span)
                if dz == 3:
                    push(now, chunk, "z+", (dy, dz), (dy, 4), (low, half))
                if dz in (0, 7, 6):
                    push(now, chunk, "z-", (dy, dz), (dy, (dz - 1) % ZS), span)
                if dz == 5:
                    push(now, chunk, "z-", (dy, dz), (dy, 4), (half, high))
                push(now, chunk, "y+", (dy, dz), (1, dz), span)
                push(now, chunk, "y-", (dy, dz), (3, dz), span)
            if dy == 1 and dz % 2 == 0:
                push(now, chunk, "y+", (dy, dz), (2, dz), span)
            if dy == 3 and dz % 2 == 1:
                push(now, chunk, "y-", (dy, dz), (2, dz), span)
        else:
            low, high = split["y"]
            half = (low + high + 1) // 2
            if dz == 0:
                if dy == 0:
                    push(now, chunk, "y+", (0, 0), (1, 0), span)
                    push(now, chunk, "y-", (0, 0), (3, 0), span)
                if dy == 1:
                    push(now, chunk, "y+", (1, 0), (2, 0), (low, half))
                if dy == 3:
                    push(now, chunk, "y-", (3, 0), (2, 0), (half, high))
            if dz in (0, 1, 2):
                push(now, chunk, "z+", (dy, dz), (dy, dz + 1), span)
            if dz == 3 and dy < 2:
                push(now, chunk, "z+", (dy, dz), (dy, 4), span)
            if dz in (0, 7, 6):
                push(now, chunk, "z-", (dy, dz), (dy, (dz - 1) % ZS), span)
            if dz == 5 and dy >= 2:
                push(now, chunk, "z-", (dy, dz), (dy, 4), span)

    for chunk in range(len(spans)):
        forward(0.0, chunk, 0, 0, split["z"])
        forward(0.0, chunk, 0, 0, split["y"])
    issue(0.0)
    while flight:
        entry = min(flight)
        flight.remove(entry)
        now, number = entry
        chunk, _, _, target, span = plan[number]
        steps.append(("wait", number))
        forward(now, chunk, target[0], target[1], span)
        issue(now)
    return steps, plan


def exchange_kernel(
    pick_ref,
    patches_ref,
    patch_own_ref,
    enc_proj_ref,
    enc_out_ref,
    embed_ref,
    weights_ref,
    pose_ref,
    far_ref,
    own_ref,
    weights_all,
    pose_all,
    *scratch,
):
    chunks = len(WIDTHS)
    held, scratch = scratch[:chunks], scratch[chunks:]
    staged, scratch = scratch[:chunks], scratch[chunks:]
    relay, scratch = scratch[:chunks], scratch[chunks:]
    (
        mixed,
        mixed_all,
        enc_out_all,
        emb_ref,
        enc_send,
        enc_recv,
        ring_send,
        ring_recv,
        twin_send,
        twin_recv,
        line_send,
        line_recv,
        pose_send,
        pose_recv,
        far_send,
        far_recv,
        local_sem,
    ) = scratch
    columns = [slice(sum(WIDTHS[:c]), sum(WIDTHS[: c + 1])) for c in range(chunks)]
    images, share, width = emb_ref.shape
    here = lax.axis_index("img")
    me = lax.axis_index("mp")
    core = lax.rem(here, 2)
    z = lax.rem(here // 2, ZS)
    y = here // (2 * ZS)
    split = far_ref.shape[1]
    per_dev = far_ref.shape[0]
    half_dev = per_dev // 2

    def spot(yy, zz, cc):
        return ((yy * ZS + zz) * 2 + cc, me)

    def mate(step):
        return (here, lax.rem(me + step, split))

    def behind(step):
        return lax.rem(me + split - step, split)

    twin = spot(y, z, 1 - core)
    links = {
        "y+": spot(lax.rem(y + 1, YS), z, core),
        "y-": spot(lax.rem(y + YS - 1, YS), z, core),
        "z+": spot(y, lax.rem(z + 1, ZS), core),
        "z-": spot(y, lax.rem(z + ZS - 1, ZS), core),
    }
    line = [(dz, dc) for dz in range(ZS) for dc in range(CORES) if dz or dc]

    def line_peer(dz, dc, sign):
        return spot(y, lax.rem(z + ZS + sign * dz, ZS), lax.rem(core + dc, 2))

    def y_peer(dy, sign):
        return spot(lax.rem(y + YS + sign * dy, YS), z, core)

    barrier = pltpu.get_barrier_semaphore()
    peers = [line_peer(dz, dc, 1) for dz, dc in line]
    peers += [y_peer(dy, 1) for dy in range(1, YS)]
    peers += [mate(step) for step in range(1, split)]
    for peer in peers:
        pl.semaphore_signal(barrier, inc=1, device_id=peer, device_id_type=MESH)
    pose_all[here] = pose_ref[...]
    pl.semaphore_wait(barrier, len(peers))

    def remote(source, target, send, recv, device):
        return pltpu.make_async_remote_copy(
            src_ref=source,
            dst_ref=target,
            send_sem=send,
            recv_sem=recv,
            device_id=device,
            device_id_type=MESH,
        )

    steps, plan = link_plan(images, WIDTHS)

    def block(chunk, side, slot, span):
        first = ((side * YS + slot[0]) * ZS + slot[1]) * images
        return held[chunk].at[pl.ds(first + span[0], span[1] - span[0])]

    def ring(number):
        chunk, link, source, target, span = plan[number]
        return remote(
            block(chunk, 0, source, span),
            block(chunk, 0, target, span),
            ring_send.at[number],
            ring_recv.at[number],
            links[link],
        )

    twins = [(entry[0], entry[3], entry[4]) for entry in plan]
    twins += [(chunk, (0, 0), (0, images)) for chunk in range(chunks)]

    def twin_copy(number):
        chunk, slot, span = twins[number]
        return remote(
            block(chunk, 0, slot, span),
            block(chunk, 1, slot, span),
            twin_send.at[number],
            twin_recv.at[number],
            twin,
        )

    def pose_line(dz, dc, number, slot):
        return remote(
            pose_all.at[slot],
            pose_all.at[slot],
            pose_send.at[number],
            pose_recv.at[number],
            line_peer(dz, dc, 1),
        )

    for number, (dz, dc) in enumerate(line):
        pose_line(dz, dc, number, here).start()

    pair_images = images // split

    def own_copy(step, slot):
        return remote(
            emb_ref.at[pl.ds(pair_images * lax.rem(me + step, split), pair_images)],
            own_ref.at[:, slot],
            line_send.at[step],
            line_recv.at[step],
            mate(step),
        )

    def weight_copy(step, slot):
        return remote(
            weights_ref.at[pl.ds(2 * core, 2)],
            weights_all.at[pl.ds(2 * core, 2), slot],
            line_send.at[split + step],
            line_recv.at[split + step],
            mate(step),
        )

    def weight_relay(step, slot):
        kind = 2 * core + (0 if step == 1 else 1)
        return remote(
            weights_all.at[pl.ds(kind, 1), slot],
            weights_all.at[pl.ds(kind, 1), slot],
            line_send.at[3 * split + step],
            line_recv.at[3 * split + step],
            mate(step),
        )

    def weight_twin(step, half, slot):
        return remote(
            weights_all.at[pl.ds(2 * half, 2), slot],
            weights_all.at[pl.ds(2 * half, 2), slot],
            line_send.at[2 * split + step],
            line_recv.at[2 * split + step],
            twin,
        )

    def far_direct(chunk, step, slot):
        return remote(
            staged[chunk].at[pl.ds(per_dev * lax.rem(me + step, split), per_dev)],
            far_ref.at[:, slot, :, columns[chunk]],
            far_send.at[chunk, step],
            far_recv.at[chunk, step],
            mate(step),
        )

    def far_relay(chunk, step):
        side = 0 if step == 1 else 1
        return remote(
            staged[chunk].at[pl.ds(per_dev * lax.rem(me + 2, split) + side * half_dev, half_dev)],
            relay[chunk].at[side],
            far_send.at[chunk, split + step],
            far_recv.at[chunk, split + step],
            mate(step),
        )

    def far_onward(chunk, step, slot):
        side = 0 if step == 1 else 1
        return remote(
            relay[chunk].at[side],
            far_ref.at[pl.ds(side * half_dev, half_dev), slot, :, columns[chunk]],
            far_send.at[chunk, 2 * split + step],
            far_recv.at[chunk, 2 * split + step],
            mate(step),
        )

    def out_copy(step, slot):
        return remote(
            enc_out_ref,
            enc_out_all.at[slot],
            enc_send.at[step],
            enc_recv.at[step],
            mate(step),
        )

    def mixed_copy(part, step, slot):
        span = pl.ds(part * (images // 2), images // 2)
        return remote(
            mixed.at[lax.rem(me + step, split), span],
            mixed_all.at[slot, span],
            enc_send.at[split * (1 + part) + step],
            enc_recv.at[split * (1 + part) + step],
            mate(step),
        )

    for step in range(1, split):
        out_copy(step, me).start()
    enc_out_all[me] = enc_out_ref[...]
    tokens = share * split
    local = enc_out_ref.shape[0]
    last = (((1,), (1,)), ((), ()))
    first_half = lax.broadcasted_iota(jnp.int32, (1, 128), 1) < HD
    zero = jnp.zeros((), jnp.bfloat16)
    ones = jnp.ones((tokens, 128), jnp.bfloat16)

    def encode(pair, carry):
        span = pl.ds(pl.multiple_of(pair * 2 * tokens, 2 * tokens), 2 * tokens)
        normed = norm_rows(patches_ref[span, :].astype(jnp.float32))
        projected = jnp.dot(normed, enc_proj_ref[...], preferred_element_type=jnp.float32)
        projected = projected.astype(jnp.bfloat16)
        for image in range(2):
            lines = slice(image * tokens, (image + 1) * tokens)
            for first in range(0, local, 128):
                query = projected[lines, first : first + 128] * jnp.bfloat16(HD ** (-0.5))
                key = projected[lines, local + first : local + first + 128]
                value = projected[lines, 2 * local + first : 2 * local + first + 128]
                both = jnp.concatenate(
                    [jnp.where(first_half, query, zero), jnp.where(first_half, zero, query)], axis=0
                )
                scores = lax.dot_general(both, key, last, preferred_element_type=jnp.float32)
                expos = jnp.exp(scores - jnp.max(scores, axis=1, keepdims=True))
                got = jnp.dot(
                    expos.astype(jnp.bfloat16),
                    jnp.concatenate([value, ones], axis=1),
                    preferred_element_type=jnp.float32,
                )
                got = got[:, :128] / got[:, 128:]
                got = jnp.where(first_half, got[:tokens], got[tokens:])
                for place in range(split):
                    mixed[place, pair * 2 + image, :, first : first + 128] = got[
                        place * share : (place + 1) * share
                    ].astype(jnp.bfloat16)
        return carry

    lax.fori_loop(0, images // 4, encode, 0)
    for step in range(1, split):
        mixed_copy(0, step, me).start()
    lax.fori_loop(images // 4, images // 2, encode, 0)
    for step in range(1, split):
        mixed_copy(1, step, me).start()
    for step in (1, 3):
        weight_copy(step, me).start()
    mixed_all[me] = mixed[me]
    encoded = patch_own_ref[...].astype(jnp.float32).reshape(images * share, -1)
    for step in range(split):
        source = behind(step)
        if step:
            out_copy(step, source).wait_recv()
            mixed_copy(0, step, source).wait_recv()
            mixed_copy(1, step, source).wait_recv()
        part = mixed_all[source].astype(jnp.float32).reshape(images * share, local)
        encoded = encoded + jnp.dot(
            part.astype(jnp.bfloat16), enc_out_all[source], preferred_element_type=jnp.float32
        )
    embedded = jnp.dot(norm_rows(encoded), embed_ref[...], preferred_element_type=jnp.float32)
    embedded = embedded.astype(jnp.bfloat16).astype(jnp.float32)
    emb_ref[...] = embedded.reshape(images, share, width).astype(jnp.bfloat16)
    normed_rows = norm_rows(embedded).astype(jnp.float32).reshape(images, share, width)
    for chunk in range(chunks):
        held[chunk][pl.ds(0, images)] = normed_rows[:, :, columns[chunk]].astype(jnp.bfloat16)
    opening = [kind for kind, _ in steps].index("wait")
    for _, number in steps[:opening]:
        ring(number).start()
    for chunk in range(chunks):
        twin_copy(len(plan) + chunk).start()

    for step in range(1, split):
        own_copy(step, me).start()
    own_local = pltpu.make_async_copy(
        emb_ref.at[pl.ds(pair_images * me, pair_images)], own_ref.at[:, me], local_sem.at[0]
    )
    own_local.start()
    weight_local = pltpu.make_async_copy(weights_ref, weights_all.at[:, me], local_sem.at[1])
    weight_local.start()

    def far_local(chunk):
        return pltpu.make_async_copy(
            staged[chunk].at[pl.ds(per_dev * me, per_dev)],
            far_ref.at[:, me, :, columns[chunk]],
            local_sem.at[2 + chunk],
        )

    def choose(chunk):
        for number, entry in enumerate(twins):
            if entry[0] == chunk:
                twin_copy(number).wait_recv()

        def pick(index, carry):
            staged[chunk][index] = held[chunk][pick_ref[index]]
            return carry

        lax.fori_loop(0, per_dev * split, pick, 0, unroll=4)
        for step in (1, 3):
            far_relay(chunk, step).start()
        for step in (1, 3):
            far_direct(chunk, step, me).start()
        far_local(chunk).start()

    def pass_on(chunk):
        for step in (1, 3):
            far_relay(chunk, step).wait_recv()
            far_onward(chunk, step, behind(step)).start()

    def pose_cross(dy, row):
        return remote(
            pose_all.at[pl.ds(row * 2 * ZS, 2 * ZS)],
            pose_all.at[pl.ds(row * 2 * ZS, 2 * ZS)],
            pose_send.at[len(line) + dy - 1],
            pose_recv.at[len(line) + dy - 1],
            y_peer(dy, 1),
        )

    def pose_second():
        for number, (dz, dc) in enumerate(line):
            pose_line(dz, dc, number, line_peer(dz, dc, -1)[0]).wait_recv()
        for dy in range(1, YS):
            pose_cross(dy, y).start()

    def weights_second():
        for step in (1, 3):
            weight_copy(step, behind(step)).wait_recv()
            weight_relay(step, behind(step)).start()
            weight_twin(step, core, behind(step)).start()

    def weights_third():
        for step in (1, 3):
            weight_relay(step, behind(2)).wait_recv()
        weight_twin(2, core, behind(2)).start()

    waits = [number for kind, number in steps if kind == "wait"]
    final = {c: max(i for i, n in enumerate(waits) if plan[n][0] == c) for c in range(chunks)}
    events = {8: pose_second, len(waits) // 4: weights_second, len(waits) // 2: weights_third}
    later, pending, count = {}, [], 0
    for kind, number in steps[opening:]:
        if kind == "send":
            ring(number).start()
            continue
        for action in pending:
            action()
        pending = []
        ring(number).wait_recv()
        twin_copy(number).start()
        count += 1
        if count in events:
            pending.append(events[count])
        for chunk in range(chunks):
            if final[chunk] == count - 1:
                pending.append(functools.partial(choose, chunk))
                later[count + RELAY] = chunk
        if count in later:
            pending.append(functools.partial(pass_on, later.pop(count)))
    for action in pending:
        action()
    for chunk in later.values():
        pass_on(chunk)
    for dy in range(1, YS):
        pose_cross(dy, lax.rem(y + YS - dy, YS)).wait_recv()
    for step in range(1, split):
        own_copy(step, behind(step)).wait_recv()
        weight_twin(step, 1 - core, behind(step)).wait_recv()
    own_local.wait()
    weight_local.wait()
    for number in range(len(plan)):
        ring(number).wait_send()
    for number in range(len(twins)):
        twin_copy(number).wait_send()
    for number, (dz, dc) in enumerate(line):
        pose_line(dz, dc, number, here).wait_send()
    for dy in range(1, YS):
        pose_cross(dy, y).wait_send()
    for step in range(1, split):
        out_copy(step, me).wait_send()
        mixed_copy(0, step, me).wait_send()
        mixed_copy(1, step, me).wait_send()
        own_copy(step, me).wait_send()
        weight_twin(step, core, behind(step)).wait_send()
    for step in (1, 3):
        weight_copy(step, me).wait_send()
        weight_relay(step, behind(step)).wait_send()
    for chunk in range(chunks):
        far_local(chunk).wait()
        for step in (1, 3):
            far_relay(chunk, step).wait_send()
            far_direct(chunk, step, behind(step)).wait_recv()
            far_direct(chunk, step, me).wait_send()
            far_onward(chunk, step, behind(2)).wait_recv()
            far_onward(chunk, step, behind(step)).wait_send()


def exchange(pick, patches, patch_own, enc_proj, enc_out, embed, weights, pose, pairs, groups, split):
    images, share, _ = patch_own.shape
    width = embed.shape[1]
    chunks = len(WIDTHS)
    count = len(link_plan(images, WIDTHS)[1])
    vmem = pl.BlockSpec(memory_space=pltpu.VMEM)
    per_dev = pairs // split
    return pl.pallas_call(
        exchange_kernel,
        out_shape=(
            jax.ShapeDtypeStruct((per_dev, split, share, width), jnp.bfloat16),
            jax.ShapeDtypeStruct((images // split, split, share, width), jnp.bfloat16),
            jax.ShapeDtypeStruct((4, split) + weights.shape[1:], jnp.bfloat16),
            jax.ShapeDtypeStruct((groups,) + pose.shape, jnp.bfloat16),
        ),
        in_specs=[pl.BlockSpec(memory_space=pltpu.SMEM)] + [vmem] * 7,
        out_specs=(vmem,) * 4,
        scratch_shapes=[pltpu.VMEM((groups * images, share, w), jnp.bfloat16) for w in WIDTHS]
        + [pltpu.VMEM((pairs, share, w), jnp.bfloat16) for w in WIDTHS]
        + [pltpu.VMEM((2, per_dev // 2, share, w), jnp.bfloat16) for w in WIDTHS]
        + [
            pltpu.VMEM((split, images, share, enc_out.shape[0]), jnp.bfloat16),
            pltpu.VMEM((split, images, share, enc_out.shape[0]), jnp.bfloat16),
            pltpu.VMEM((split,) + enc_out.shape, jnp.bfloat16),
            pltpu.VMEM((images, share, width), jnp.bfloat16),
            pltpu.SemaphoreType.DMA((3 * split,)),
            pltpu.SemaphoreType.DMA((3 * split,)),
            pltpu.SemaphoreType.DMA((count,)),
            pltpu.SemaphoreType.DMA((count,)),
            pltpu.SemaphoreType.DMA((count + chunks,)),
            pltpu.SemaphoreType.DMA((count + chunks,)),
            pltpu.SemaphoreType.DMA((4 * split,)),
            pltpu.SemaphoreType.DMA((4 * split,)),
            pltpu.SemaphoreType.DMA((2 * ZS + YS,)),
            pltpu.SemaphoreType.DMA((2 * ZS + YS,)),
            pltpu.SemaphoreType.DMA((chunks, 3 * split)),
            pltpu.SemaphoreType.DMA((chunks, 3 * split)),
            pltpu.SemaphoreType.DMA((2 + chunks,)),
        ],
        compiler_params=pltpu.CompilerParams(
            collective_id=0, has_side_effects=True, vmem_limit_bytes=56 * 2**20
        ),
        name="exchange",
    )(pick, patches, patch_own, enc_proj, enc_out, embed, weights, pose)


def reduce_kernel(
    grad_ref, total_ref, across, summed, lined, part, crossed, x_send, x_recv, l_send, l_recv, c_send, c_recv
):
    here = lax.axis_index("img")
    me = lax.axis_index("mp")
    core = lax.rem(here, 2)
    z = lax.rem(here // 2, ZS)
    y = here // (2 * ZS)
    split = across.shape[0]
    row = z * 2 + core
    rows = 2 * ZS
    line = [(dz, dc) for dz in range(ZS) for dc in range(CORES) if dz or dc]

    def line_row(dz, dc, sign):
        return lax.rem(z + ZS + sign * dz, ZS) * 2 + lax.rem(core + dc, 2)

    def mate(step):
        return (here, lax.rem(me + step, split))

    barrier = pltpu.get_barrier_semaphore()
    for step in range(1, split):
        pl.semaphore_signal(barrier, inc=1, device_id=mate(step), device_id_type=MESH)
    for dz, dc in line:
        pl.semaphore_signal(
            barrier, inc=1, device_id=(y * rows + line_row(dz, dc, 1), me), device_id_type=MESH
        )
    for other in range(YS):
        pl.semaphore_signal(barrier, inc=1, device_id=(other * rows + row, y), device_id_type=MESH)

    pl.semaphore_wait(barrier, split - 1 + len(line) + YS)

    def remote(source, target, send, recv, device):
        return pltpu.make_async_remote_copy(
            src_ref=source,
            dst_ref=target,
            send_sem=send,
            recv_sem=recv,
            device_id=device,
            device_id_type=MESH,
        )

    def x_copy(step, slot):
        return remote(
            grad_ref.at[lax.rem(me + step, split)],
            across.at[slot],
            x_send.at[step],
            x_recv.at[step],
            mate(step),
        )

    for step in range(1, split):
        x_copy(step, me).start()
    across[me] = grad_ref[me]
    for step in range(1, split):
        x_copy(step, lax.rem(me + split - step, split)).wait_recv()
    summed[...] = jnp.sum(across[...], axis=0)

    def l_copy(number, dz, dc, slot):
        target = line_row(dz, dc, 1)
        return remote(
            summed.at[target],
            lined.at[slot],
            l_send.at[number],
            l_recv.at[number],
            (y * rows + target, me),
        )

    for number, (dz, dc) in enumerate(line):
        l_copy(number, dz, dc, row).start()
    lined[row] = summed[row]
    for number, (dz, dc) in enumerate(line):
        l_copy(number, dz, dc, line_row(dz, dc, -1)).wait_recv()
    part[...] = jnp.sum(lined[...], axis=0)

    def c_copy(other, slot):
        return remote(
            part, crossed.at[slot], c_send.at[other], c_recv.at[slot], (me * rows + row, other)
        )

    for other in range(split):

        @pl.when(jnp.logical_or(y != me, me != other))
        def _():
            c_copy(other, y).start()

    @pl.when(y == me)
    def _():
        crossed[y] = part[...]

    for other in range(YS):

        @pl.when(jnp.logical_or(y != me, y != other))
        def _():
            c_copy(0, other).wait_recv()

    total_ref[...] = jnp.sum(crossed[...], axis=0)
    for step in range(1, split):
        x_copy(step, me).wait_send()
    for number, (dz, dc) in enumerate(line):
        l_copy(number, dz, dc, row).wait_send()
    for other in range(split):

        @pl.when(jnp.logical_or(y != me, me != other))
        def _():
            c_copy(other, y).wait_send()


def reduce_poses(dense, split):
    groups = dense.shape[0] * dense.shape[1]
    tile = dense.shape[2:]
    vmem = pl.BlockSpec(memory_space=pltpu.VMEM)
    rows = 2 * ZS
    return pl.pallas_call(
        reduce_kernel,
        out_shape=jax.ShapeDtypeStruct(tile, jnp.float32),
        in_specs=[vmem],
        out_specs=vmem,
        scratch_shapes=[
            pltpu.VMEM((split, rows) + tile, jnp.float32),
            pltpu.VMEM((rows,) + tile, jnp.float32),
            pltpu.VMEM((rows,) + tile, jnp.float32),
            pltpu.VMEM(tile, jnp.float32),
            pltpu.VMEM((YS,) + tile, jnp.float32),
            pltpu.SemaphoreType.DMA((split,)),
            pltpu.SemaphoreType.DMA((split,)),
            pltpu.SemaphoreType.DMA((rows,)),
            pltpu.SemaphoreType.DMA((rows,)),
            pltpu.SemaphoreType.DMA((split,)),
            pltpu.SemaphoreType.DMA((YS,)),
        ],
        compiler_params=pltpu.CompilerParams(collective_id=1, has_side_effects=True),
        name="reduce_poses",
    )(dense)


def decode_kernel(far_ref, own_ref, weights_ref, head_ref, out_ref, queries, keys, values, mixed):
    width = own_ref.shape[1]
    tokens = out_ref.shape[2]
    pairs = out_ref.shape[0]
    blocks = width // 128
    own_count = own_ref.shape[0] // tokens
    per_image = pairs // own_count
    last = (((1,), (1,)), ((), ()))
    lane = lax.broadcasted_iota(jnp.int32, (1, 128), 1)
    first_half = lane < HD

    rows = norm_rows(own_ref[...].astype(jnp.float32))
    projected = lax.dot_general(rows, weights_ref[0], last, preferred_element_type=jnp.float32)
    projected = projected.astype(jnp.bfloat16) * jnp.bfloat16(HD ** (-0.5))
    zero = jnp.zeros((), jnp.bfloat16)
    for image in range(own_count):
        for block in range(blocks):
            part = projected[image * tokens : (image + 1) * tokens, block * 128 : (block + 1) * 128]
            queries[image, block, :tokens] = jnp.where(first_half, part, zero)
            queries[image, block, tokens:] = jnp.where(first_half, zero, part)

    chunk = 4 * tokens

    def project(step, carry):
        span = pl.ds(pl.multiple_of(step * chunk, chunk), chunk)
        part = far_ref[span, :]
        keys[span, :] = lax.dot_general(
            part, weights_ref[1], last, preferred_element_type=jnp.float32
        ).astype(jnp.bfloat16)
        values[span, :] = lax.dot_general(
            part, weights_ref[2], last, preferred_element_type=jnp.float32
        ).astype(jnp.bfloat16)
        return carry

    lax.fori_loop(0, pairs // 4, project, 0)
    ones = jnp.ones((tokens, 128), jnp.bfloat16)

    def attend(pair, carry):
        span = pl.ds(pl.multiple_of(pair * tokens, tokens), tokens)
        image = pair // per_image
        for block in range(blocks):
            columns = slice(block * 128, (block + 1) * 128)
            scores = lax.dot_general(
                queries[image, block], keys[span, columns], last, preferred_element_type=jnp.float32
            )
            expos = jnp.exp(scores - jnp.max(scores, axis=1, keepdims=True)).astype(jnp.bfloat16)
            both = jnp.concatenate([values[span, columns], ones], axis=1)
            got = jnp.dot(expos, both, preferred_element_type=jnp.float32)
            got = got[:, :128] / got[:, 128:]
            mixed[span, columns] = jnp.where(first_half, got[:tokens], got[tokens:]).astype(
                jnp.bfloat16
            )
        return carry

    lax.fori_loop(0, pairs, attend, 0)

    def finish(step, carry):
        span = pl.ds(pl.multiple_of(step * chunk, chunk), chunk)
        image = step * 4 // per_image
        own = own_ref[pl.ds(pl.multiple_of(image * tokens, tokens), tokens), :].astype(jnp.float32)
        settled = jnp.dot(mixed[span, :], weights_ref[3], preferred_element_type=jnp.float32)
        settled = settled + jnp.concatenate([own] * 4, axis=0)
        heads = lax.dot_general(
            head_ref[...], norm_rows(settled), last, preferred_element_type=jnp.float32
        )
        for part in range(4):
            out_ref[step * 4 + part] = heads[:, part * tokens : (part + 1) * tokens]
        return carry

    lax.fori_loop(0, pairs // 4, finish, 0)


def decode(far, own, weights, head_rows, pairs):
    width = own.shape[1]
    tokens = far.shape[0] // pairs
    own_count = own.shape[0] // tokens
    vmem = pl.BlockSpec(memory_space=pltpu.VMEM)
    return pl.pallas_call(
        decode_kernel,
        out_shape=jax.ShapeDtypeStruct((pairs, head_rows.shape[0], tokens), jnp.float32),
        in_specs=[vmem] * 4,
        out_specs=vmem,
        scratch_shapes=[
            pltpu.VMEM((own_count, width // 128, 2 * tokens, 128), jnp.bfloat16),
            pltpu.VMEM(far.shape, jnp.bfloat16),
            pltpu.VMEM(far.shape, jnp.bfloat16),
            pltpu.VMEM(far.shape, jnp.bfloat16),
        ],
        compiler_params=pltpu.CompilerParams(vmem_limit_bytes=48 * 2**20),
        name="decode",
    )(far, own, weights, head_rows)


def shards(
    patches,
    encoder_proj,
    encoder_out,
    decoder_embed,
    decoder_proj,
    decoder_out,
    head_weight,
    partners,
    depths,
    camera_poses,
    valid_mask,
):
    images, tokens, model_width = patches.shape
    dec_width = decoder_embed.shape[1]
    enc_local = encoder_proj.shape[2]
    split = lax.axis_size("mp")
    place = lax.axis_index("mp")
    own_count = images // split
    flat_partner = partners.reshape(-1)
    pair_count = flat_partner.shape[0]
    groups = lax.axis_size("img")
    here = lax.axis_index("img")
    weights = jnp.concatenate([jnp.transpose(decoder_proj, (1, 2, 0)), decoder_out[None]], axis=0)
    pose_tile = jnp.pad(
        camera_poses.astype(jnp.bfloat16), ((0, 4), (0, 128 - camera_poses.shape[1]))
    )

    token_share = tokens // split
    first_token = place * token_share
    patch_own = lax.dynamic_slice_in_dim(patches, first_token, token_share, 1)
    owner = flat_partner // images
    shift_y = (here // (2 * ZS) - owner // (2 * ZS)) % YS
    shift_z = ((here // 2) % ZS - (owner // 2) % ZS) % ZS
    shift_core = (here - owner) % 2
    pick = ((shift_core * YS + shift_y) * ZS + shift_z) * images + flat_partner % images
    far_rows, own_rows, weights_full, pose_tiles = exchange(
        pick,
        patches.reshape(images * tokens, model_width),
        patch_own,
        encoder_proj.reshape(model_width, 3 * enc_local),
        encoder_out,
        decoder_embed,
        weights,
        pose_tile,
        pair_count,
        groups,
        split,
    )
    head_rows = jnp.pad(head_weight.T, ((0, 12), (0, 0)))
    head_own = decode(
        far_rows.reshape(pair_count // split * tokens, dec_width),
        own_rows.reshape(own_count * tokens, dec_width),
        weights_full.reshape(4, dec_width, dec_width),
        head_rows,
        pair_count // split,
    )
    head_own = head_own[:, :4].transpose(1, 0, 2)
    moved = lax.all_to_all(head_own, "mp", split_axis=2, concat_axis=1, tiled=True)
    points = moved[:3]
    confidence = 1.0 + jnp.exp(moved[3])
    pointmap = jnp.concatenate([points, confidence[None]], axis=0)
    ray_dirs = make_rays(first_token + jnp.arange(token_share, dtype=jnp.int32), tokens // 16)
    weight = valid_mask.astype(jnp.float32)
    pose_table = pose_tiles[:, :12, :images].transpose(1, 0, 2).reshape(12, groups * images)
    pose_far = pose_table[:, flat_partner].astype(jnp.float32).reshape(12, images, K)
    point_grid = points.reshape(3, images, K, token_share)
    conf_grid = confidence.reshape(images, K, token_share)

    def loss_fn(depth_map, pose_own, pose_other):
        return align_loss(
            depth_map, pose_own, pose_other, point_grid, conf_grid, weight, ray_dirs, 1.0 / tokens
        )

    loss_value, pullback = jax.vjp(loss_fn, depths, camera_poses, pose_far)
    grad_depth, grad_own, grad_far = pullback(jnp.ones_like(loss_value))
    grad_far_flat = grad_far.reshape(12, pair_count)
    total_images = groups * images
    base_image = lax.axis_index("img") * images
    image_ids = jnp.arange(total_images, dtype=jnp.int32)
    partner_hits = (flat_partner[:, None] == image_ids[None, :]).astype(jnp.float32)
    own_hits = (
        (base_image + jnp.arange(images, dtype=jnp.int32))[:, None] == image_ids[None, :]
    ).astype(jnp.float32)
    dense_grad = jnp.dot(grad_far_flat, partner_hits, precision=lax.Precision.HIGHEST) + jnp.dot(
        grad_own, own_hits, precision=lax.Precision.HIGHEST
    )
    dense_rows = dense_grad.reshape(12, groups, images).transpose(1, 0, 2).reshape(groups, 1, -1)
    dense_rows = jnp.pad(dense_rows, ((0, 0), (0, 7), (0, 128 - 12 * images)))
    total = reduce_poses(dense_rows.reshape(YS, 2 * ZS, 8, 128), split)
    grad_pose = total[0, : 12 * images].reshape(12, images)
    new_depths = depths - depth_step * grad_depth
    new_poses = camera_poses - pose_step * grad_pose
    return (pointmap, new_depths, new_poses)


def solution(mesh):
    placed = (
        P("img", None, None),
        P(None, None, "mp"),
        P("mp", None),
        P(),
        P(None, None, "mp"),
        P("mp", None),
        P(),
        P("img", None),
        P("img", "mp"),
        P(None, "img"),
        P("img", "mp"),
    )
    return jax.shard_map(
        shards,
        mesh=mesh,
        in_specs=placed,
        out_specs=(P(None, "img", "mp"), P("img", "mp"), P(None, "img")),
        check_vma=False,
    )
```

```python
import functools

import jax
import jax.numpy as jnp
from jax import lax
from jax.experimental import pallas as pl
from jax.experimental.pallas import tpu as pltpu
from jax.sharding import PartitionSpec as P

HD = 64
K = 8


epsilon = 1e-06
depth_step = 0.1
pose_step = 0.005


def norm_rows(values):
    average = jnp.mean(values, axis=-1, keepdims=True)
    centred = values - average
    variance = jnp.mean(centred * centred, axis=-1, keepdims=True)
    return (centred * lax.rsqrt(variance + epsilon)).astype(jnp.bfloat16)


YS, ZS, CORES = 4, 8, 2
FIRST = 5
WIDTHS = (384, 384)
RELAY = 18
AHEAD, DELAY = 4.0, 4.0
MESH = pl.DeviceIdType.MESH


def link_plan(images, spans):
    split = {"z": (0, FIRST), "y": (FIRST, images)}
    full = sum(spans)
    waiting = {"y+": [], "y-": [], "z+": [], "z-": []}
    free = {link: 0.0 for link in waiting}
    plan, flight, steps = [], [], []

    def push(now, chunk, link, source, target, span):
        waiting[link].append((chunk, len(waiting[link]) + 1000 * now, source, target, span))

    def issue(now):
        for link, queue in waiting.items():
            while queue and free[link] <= now + AHEAD:
                entry = min(queue)
                queue.remove(entry)
                chunk, _, source, target, span = entry
                free[link] = max(now, free[link]) + (span[1] - span[0]) * spans[chunk] / full
                flight.append((free[link] + DELAY, len(plan)))
                steps.append(("send", len(plan)))
                plan.append((chunk, link, source, target, span))

    def forward(now, chunk, dy, dz, span):
        if span[1] <= FIRST:
            low, high = split["z"]
            half = (low + high + 1) // 2
            if dy == 0:
                if dz in (0, 1, 2):
                    push(now, chunk, "z+", (dy, dz), (dy, dz + 1), span)
                if dz == 3:
                    push(now, chunk, "z+", (dy, dz), (dy, 4), (low, half))
                if dz in (0, 7, 6):
                    push(now, chunk, "z-", (dy, dz), (dy, (dz - 1) % ZS), span)
                if dz == 5:
                    push(now, chunk, "z-", (dy, dz), (dy, 4), (half, high))
                push(now, chunk, "y+", (dy, dz), (1, dz), span)
                push(now, chunk, "y-", (dy, dz), (3, dz), span)
            if dy == 1 and dz % 2 == 0:
                push(now, chunk, "y+", (dy, dz), (2, dz), span)
            if dy == 3 and dz % 2 == 1:
                push(now, chunk, "y-", (dy, dz), (2, dz), span)
        else:
            low, high = split["y"]
            half = (low + high + 1) // 2
            if dz == 0:
                if dy == 0:
                    push(now, chunk, "y+", (0, 0), (1, 0), span)
                    push(now, chunk, "y-", (0, 0), (3, 0), span)
                if dy == 1:
                    push(now, chunk, "y+", (1, 0), (2, 0), (low, half))
                if dy == 3:
                    push(now, chunk, "y-", (3, 0), (2, 0), (half, high))
            if dz in (0, 1, 2):
                push(now, chunk, "z+", (dy, dz), (dy, dz + 1), span)
            if dz == 3 and dy < 2:
                push(now, chunk, "z+", (dy, dz), (dy, 4), span)
            if dz in (0, 7, 6):
                push(now, chunk, "z-", (dy, dz), (dy, (dz - 1) % ZS), span)
            if dz == 5 and dy >= 2:
                push(now, chunk, "z-", (dy, dz), (dy, 4), span)

    for chunk in range(len(spans)):
        forward(0.0, chunk, 0, 0, split["z"])
        forward(0.0, chunk, 0, 0, split["y"])
    issue(0.0)
    while flight:
        entry = min(flight)
        flight.remove(entry)
        now, number = entry
        chunk, _, _, target, span = plan[number]
        steps.append(("wait", number))
        forward(now, chunk, target[0], target[1], span)
        issue(now)
    return steps, plan


def exchange_kernel(
    pick_ref,
    patches_ref,
    patch_own_ref,
    enc_proj_ref,
    enc_out_ref,
    embed_ref,
    weights_ref,
    pose_ref,
    far_ref,
    own_ref,
    weights_all,
    pose_all,
    *scratch,
):
    chunks = len(WIDTHS)
    held, scratch = scratch[:chunks], scratch[chunks:]
    staged, scratch = scratch[:chunks], scratch[chunks:]
    relay, scratch = scratch[:chunks], scratch[chunks:]
    (
        mixed,
        mixed_all,
        enc_out_all,
        emb_ref,
        enc_send,
        enc_recv,
        ring_send,
        ring_recv,
        twin_send,
        twin_recv,
        line_send,
        line_recv,
        pose_send,
        pose_recv,
        far_send,
        far_recv,
        local_sem,
    ) = scratch
    columns = [slice(sum(WIDTHS[:c]), sum(WIDTHS[: c + 1])) for c in range(chunks)]
    images, share, width = emb_ref.shape
    here = lax.axis_index("img")
    me = lax.axis_index("mp")
    core = lax.rem(here, 2)
    z = lax.rem(here // 2, ZS)
    y = here // (2 * ZS)
    split = far_ref.shape[1]
    per_dev = far_ref.shape[0]
    half_dev = per_dev // 2

    def spot(yy, zz, cc):
        return ((yy * ZS + zz) * 2 + cc, me)

    def mate(step):
        return (here, lax.rem(me + step, split))

    def behind(step):
        return lax.rem(me + split - step, split)

    twin = spot(y, z, 1 - core)
    links = {
        "y+": spot(lax.rem(y + 1, YS), z, core),
        "y-": spot(lax.rem(y + YS - 1, YS), z, core),
        "z+": spot(y, lax.rem(z + 1, ZS), core),
        "z-": spot(y, lax.rem(z + ZS - 1, ZS), core),
    }
    line = [(dz, dc) for dz in range(ZS) for dc in range(CORES) if dz or dc]

    def line_peer(dz, dc, sign):
        return spot(y, lax.rem(z + ZS + sign * dz, ZS), lax.rem(core + dc, 2))

    def y_peer(dy, sign):
        return spot(lax.rem(y + YS + sign * dy, YS), z, core)

    barrier = pltpu.get_barrier_semaphore()
    peers = [line_peer(dz, dc, 1) for dz, dc in line]
    peers += [y_peer(dy, 1) for dy in range(1, YS)]
    peers += [mate(step) for step in range(1, split)]
    for peer in peers:
        pl.semaphore_signal(barrier, inc=1, device_id=peer, device_id_type=MESH)
    pose_all[here] = pose_ref[...]
    pl.semaphore_wait(barrier, len(peers))

    def remote(source, target, send, recv, device):
        return pltpu.make_async_remote_copy(
            src_ref=source,
            dst_ref=target,
            send_sem=send,
            recv_sem=recv,
            device_id=device,
            device_id_type=MESH,
        )

    steps, plan = link_plan(images, WIDTHS)

    def block(chunk, side, slot, span):
        first = ((side * YS + slot[0]) * ZS + slot[1]) * images
        return held[chunk].at[pl.ds(first + span[0], span[1] - span[0])]

    def ring(number):
        chunk, link, source, target, span = plan[number]
        return remote(
            block(chunk, 0, source, span),
            block(chunk, 0, target, span),
            ring_send.at[number],
            ring_recv.at[number],
            links[link],
        )

    twins = [(entry[0], entry[3], entry[4]) for entry in plan]
    twins += [(chunk, (0, 0), (0, images)) for chunk in range(chunks)]

    def twin_copy(number):
        chunk, slot, span = twins[number]
        return remote(
            block(chunk, 0, slot, span),
            block(chunk, 1, slot, span),
            twin_send.at[number],
            twin_recv.at[number],
            twin,
        )

    def pose_line(dz, dc, number, slot):
        return remote(
            pose_all.at[slot],
            pose_all.at[slot],
            pose_send.at[number],
            pose_recv.at[number],
            line_peer(dz, dc, 1),
        )

    for number, (dz, dc) in enumerate(line):
        pose_line(dz, dc, number, here).start()

    pair_images = images // split

    def own_copy(step, slot):
        return remote(
            emb_ref.at[pl.ds(pair_images * lax.rem(me + step, split), pair_images)],
            own_ref.at[:, slot],
            line_send.at[step],
            line_recv.at[step],
            mate(step),
        )

    def weight_copy(step, slot):
        return remote(
            weights_ref.at[pl.ds(2 * core, 2)],
            weights_all.at[pl.ds(2 * core, 2), slot],
            line_send.at[split + step],
            line_recv.at[split + step],
            mate(step),
        )

    def weight_relay(step, slot):
        kind = 2 * core + (0 if step == 1 else 1)
        return remote(
            weights_all.at[pl.ds(kind, 1), slot],
            weights_all.at[pl.ds(kind, 1), slot],
            line_send.at[3 * split + step],
            line_recv.at[3 * split + step],
            mate(step),
        )

    def weight_twin(step, half, slot):
        return remote(
            weights_all.at[pl.ds(2 * half, 2), slot],
            weights_all.at[pl.ds(2 * half, 2), slot],
            line_send.at[2 * split + step],
            line_recv.at[2 * split + step],
            twin,
        )

    def far_direct(chunk, step, slot):
        return remote(
            staged[chunk].at[pl.ds(per_dev * lax.rem(me + step, split), per_dev)],
            far_ref.at[:, slot, :, columns[chunk]],
            far_send.at[chunk, step],
            far_recv.at[chunk, step],
            mate(step),
        )

    def far_relay(chunk, step):
        side = 0 if step == 1 else 1
        return remote(
            staged[chunk].at[pl.ds(per_dev * lax.rem(me + 2, split) + side * half_dev, half_dev)],
            relay[chunk].at[side],
            far_send.at[chunk, split + step],
            far_recv.at[chunk, split + step],
            mate(step),
        )

    def far_onward(chunk, step, slot):
        side = 0 if step == 1 else 1
        return remote(
            relay[chunk].at[side],
            far_ref.at[pl.ds(side * half_dev, half_dev), slot, :, columns[chunk]],
            far_send.at[chunk, 2 * split + step],
            far_recv.at[chunk, 2 * split + step],
            mate(step),
        )

    def out_copy(step, slot):
        return remote(
            enc_out_ref,
            enc_out_all.at[slot],
            enc_send.at[step],
            enc_recv.at[step],
            mate(step),
        )

    def mixed_copy(part, step, slot):
        span = pl.ds(part * (images // 2), images // 2)
        return remote(
            mixed.at[lax.rem(me + step, split), span],
            mixed_all.at[slot, span],
            enc_send.at[split * (1 + part) + step],
            enc_recv.at[split * (1 + part) + step],
            mate(step),
        )

    for step in range(1, split):
        out_copy(step, me).start()
    enc_out_all[me] = enc_out_ref[...]
    tokens = share * split
    local = enc_out_ref.shape[0]
    last = (((1,), (1,)), ((), ()))
    first_half = lax.broadcasted_iota(jnp.int32, (1, 128), 1) < HD
    zero = jnp.zeros((), jnp.bfloat16)
    ones = jnp.ones((tokens, 128), jnp.bfloat16)

    def encode(pair, carry):
        span = pl.ds(pl.multiple_of(pair * 2 * tokens, 2 * tokens), 2 * tokens)
        normed = norm_rows(patches_ref[span, :].astype(jnp.float32))
        projected = jnp.dot(normed, enc_proj_ref[...], preferred_element_type=jnp.float32)
        projected = projected.astype(jnp.bfloat16)
        for image in range(2):
            lines = slice(image * tokens, (image + 1) * tokens)
            for first in range(0, local, 128):
                query = projected[lines, first : first + 128] * jnp.bfloat16(HD ** (-0.5))
                key = projected[lines, local + first : local + first + 128]
                value = projected[lines, 2 * local + first : 2 * local + first + 128]
                both = jnp.concatenate(
                    [jnp.where(first_half, query, zero), jnp.where(first_half, zero, query)], axis=0
                )
                scores = lax.dot_general(both, key, last, preferred_element_type=jnp.float32)
                expos = jnp.exp(scores - jnp.max(scores, axis=1, keepdims=True))
                got = jnp.dot(
                    expos.astype(jnp.bfloat16),
                    jnp.concatenate([value, ones], axis=1),
                    preferred_element_type=jnp.float32,
                )
                got = got[:, :128] / got[:, 128:]
                got = jnp.where(first_half, got[:tokens], got[tokens:])
                for place in range(split):
                    mixed[place, pair * 2 + image, :, first : first + 128] = got[
                        place * share : (place + 1) * share
                    ].astype(jnp.bfloat16)
        return carry

    lax.fori_loop(0, images // 4, encode, 0)
    for step in range(1, split):
        mixed_copy(0, step, me).start()
    lax.fori_loop(images // 4, images // 2, encode, 0)
    for step in range(1, split):
        mixed_copy(1, step, me).start()
    for step in (1, 3):
        weight_copy(step, me).start()
    mixed_all[me] = mixed[me]
    encoded = patch_own_ref[...].astype(jnp.float32).reshape(images * share, -1)
    for step in range(split):
        source = behind(step)
        if step:
            out_copy(step, source).wait_recv()
            mixed_copy(0, step, source).wait_recv()
            mixed_copy(1, step, source).wait_recv()
        part = mixed_all[source].astype(jnp.float32).reshape(images * share, local)
        encoded = encoded + jnp.dot(
            part.astype(jnp.bfloat16), enc_out_all[source], preferred_element_type=jnp.float32
        )
    embedded = jnp.dot(norm_rows(encoded), embed_ref[...], preferred_element_type=jnp.float32)
    embedded = embedded.astype(jnp.bfloat16).astype(jnp.float32)
    emb_ref[...] = embedded.reshape(images, share, width).astype(jnp.bfloat16)
    normed_rows = norm_rows(embedded).astype(jnp.float32).reshape(images, share, width)
    for chunk in range(chunks):
        held[chunk][pl.ds(0, images)] = normed_rows[:, :, columns[chunk]].astype(jnp.bfloat16)
    opening = [kind for kind, _ in steps].index("wait")
    for _, number in steps[:opening]:
        ring(number).start()
    for chunk in range(chunks):
        twin_copy(len(plan) + chunk).start()

    for step in range(1, split):
        own_copy(step, me).start()
    own_local = pltpu.make_async_copy(
        emb_ref.at[pl.ds(pair_images * me, pair_images)], own_ref.at[:, me], local_sem.at[0]
    )
    own_local.start()
    weight_local = pltpu.make_async_copy(weights_ref, weights_all.at[:, me], local_sem.at[1])
    weight_local.start()

    def far_local(chunk):
        return pltpu.make_async_copy(
            staged[chunk].at[pl.ds(per_dev * me, per_dev)],
            far_ref.at[:, me, :, columns[chunk]],
            local_sem.at[2 + chunk],
        )

    def choose(chunk):
        for number, entry in enumerate(twins):
            if entry[0] == chunk:
                twin_copy(number).wait_recv()

        def pick(index, carry):
            staged[chunk][index] = held[chunk][pick_ref[index]]
            return carry

        lax.fori_loop(0, per_dev * split, pick, 0, unroll=4)
        for step in (1, 3):
            far_relay(chunk, step).start()
        for step in (1, 3):
            far_direct(chunk, step, me).start()
        far_local(chunk).start()

    def pass_on(chunk):
        for step in (1, 3):
            far_relay(chunk, step).wait_recv()
            far_onward(chunk, step, behind(step)).start()

    def pose_cross(dy, row):
        return remote(
            pose_all.at[pl.ds(row * 2 * ZS, 2 * ZS)],
            pose_all.at[pl.ds(row * 2 * ZS, 2 * ZS)],
            pose_send.at[len(line) + dy - 1],
            pose_recv.at[len(line) + dy - 1],
            y_peer(dy, 1),
        )

    def pose_second():
        for number, (dz, dc) in enumerate(line):
            pose_line(dz, dc, number, line_peer(dz, dc, -1)[0]).wait_recv()
        for dy in range(1, YS):
            pose_cross(dy, y).start()

    def weights_second():
        for step in (1, 3):
            weight_copy(step, behind(step)).wait_recv()
            weight_relay(step, behind(step)).start()
            weight_twin(step, core, behind(step)).start()

    def weights_third():
        for step in (1, 3):
            weight_relay(step, behind(2)).wait_recv()
        weight_twin(2, core, behind(2)).start()

    waits = [number for kind, number in steps if kind == "wait"]
    final = {c: max(i for i, n in enumerate(waits) if plan[n][0] == c) for c in range(chunks)}
    events = {8: pose_second, len(waits) // 4: weights_second, len(waits) // 2: weights_third}
    later, pending, count = {}, [], 0
    for kind, number in steps[opening:]:
        if kind == "send":
            ring(number).start()
            continue
        for action in pending:
            action()
        pending = []
        ring(number).wait_recv()
        twin_copy(number).start()
        count += 1
        if count in events:
            pending.append(events[count])
        for chunk in range(chunks):
            if final[chunk] == count - 1:
                pending.append(functools.partial(choose, chunk))
                later[count + RELAY] = chunk
        if count in later:
            pending.append(functools.partial(pass_on, later.pop(count)))
    for action in pending:
        action()
    for chunk in later.values():
        pass_on(chunk)
    for dy in range(1, YS):
        pose_cross(dy, lax.rem(y + YS - dy, YS)).wait_recv()
    for step in range(1, split):
        own_copy(step, behind(step)).wait_recv()
        weight_twin(step, 1 - core, behind(step)).wait_recv()
    own_local.wait()
    weight_local.wait()
    for number in range(len(plan)):
        ring(number).wait_send()
    for number in range(len(twins)):
        twin_copy(number).wait_send()
    for number, (dz, dc) in enumerate(line):
        pose_line(dz, dc, number, here).wait_send()
    for dy in range(1, YS):
        pose_cross(dy, y).wait_send()
    for step in range(1, split):
        out_copy(step, me).wait_send()
        mixed_copy(0, step, me).wait_send()
        mixed_copy(1, step, me).wait_send()
        own_copy(step, me).wait_send()
        weight_twin(step, core, behind(step)).wait_send()
    for step in (1, 3):
        weight_copy(step, me).wait_send()
        weight_relay(step, behind(step)).wait_send()
    for chunk in range(chunks):
        far_local(chunk).wait()
        for step in (1, 3):
            far_relay(chunk, step).wait_send()
            far_direct(chunk, step, behind(step)).wait_recv()
            far_direct(chunk, step, me).wait_send()
            far_onward(chunk, step, behind(2)).wait_recv()
            far_onward(chunk, step, behind(step)).wait_send()


def exchange(pick, patches, patch_own, enc_proj, enc_out, embed, weights, pose, pairs, groups, split):
    images, share, _ = patch_own.shape
    width = embed.shape[1]
    chunks = len(WIDTHS)
    count = len(link_plan(images, WIDTHS)[1])
    vmem = pl.BlockSpec(memory_space=pltpu.VMEM)
    per_dev = pairs // split
    return pl.pallas_call(
        exchange_kernel,
        out_shape=(
            jax.ShapeDtypeStruct((per_dev, split, share, width), jnp.bfloat16),
            jax.ShapeDtypeStruct((images // split, split, share, width), jnp.bfloat16),
            jax.ShapeDtypeStruct((4, split) + weights.shape[1:], jnp.bfloat16),
            jax.ShapeDtypeStruct((groups,) + pose.shape, jnp.bfloat16),
        ),
        in_specs=[pl.BlockSpec(memory_space=pltpu.SMEM)] + [vmem] * 7,
        out_specs=(vmem,) * 4,
        scratch_shapes=[pltpu.VMEM((groups * images, share, w), jnp.bfloat16) for w in WIDTHS]
        + [pltpu.VMEM((pairs, share, w), jnp.bfloat16) for w in WIDTHS]
        + [pltpu.VMEM((2, per_dev // 2, share, w), jnp.bfloat16) for w in WIDTHS]
        + [
            pltpu.VMEM((split, images, share, enc_out.shape[0]), jnp.bfloat16),
            pltpu.VMEM((split, images, share, enc_out.shape[0]), jnp.bfloat16),
            pltpu.VMEM((split,) + enc_out.shape, jnp.bfloat16),
            pltpu.VMEM((images, share, width), jnp.bfloat16),
            pltpu.SemaphoreType.DMA((3 * split,)),
            pltpu.SemaphoreType.DMA((3 * split,)),
            pltpu.SemaphoreType.DMA((count,)),
            pltpu.SemaphoreType.DMA((count,)),
            pltpu.SemaphoreType.DMA((count + chunks,)),
            pltpu.SemaphoreType.DMA((count + chunks,)),
            pltpu.SemaphoreType.DMA((4 * split,)),
            pltpu.SemaphoreType.DMA((4 * split,)),
            pltpu.SemaphoreType.DMA((2 * ZS + YS,)),
            pltpu.SemaphoreType.DMA((2 * ZS + YS,)),
            pltpu.SemaphoreType.DMA((chunks, 3 * split)),
            pltpu.SemaphoreType.DMA((chunks, 3 * split)),
            pltpu.SemaphoreType.DMA((2 + chunks,)),
        ],
        compiler_params=pltpu.CompilerParams(
            collective_id=0, has_side_effects=True, vmem_limit_bytes=56 * 2**20
        ),
        name="exchange",
    )(pick, patches, patch_own, enc_proj, enc_out, embed, weights, pose)


def decode_kernel(
    far_ref,
    own_ref,
    weights_ref,
    head_ref,
    depth_ref,
    pose_own_ref,
    pose_far_ref,
    partner_ref,
    result_ref,
    total_ref,
    queries,
    keys,
    values,
    mixed,
    heads_all,
    depth_all,
    staging,
    dense,
    plane_in,
    part_sum,
    line_in,
    x_send,
    x_recv,
    plane_send,
    plane_recv,
    line_send,
    line_recv,
):
    width = own_ref.shape[1]
    pairs, _, tokens = heads_all.shape
    split = depth_all.shape[0]
    share = tokens // split
    here = lax.axis_index("img")
    me = lax.axis_index("mp")
    rows_count = 2 * ZS
    row = lax.rem(here, rows_count)
    y = here // rows_count
    plane = [(dx, dy) for dx in range(split) for dy in range(YS) if dx or dy]
    line = [(dz, dc) for dz in range(ZS) for dc in range(CORES) if dz or dc]

    def plane_peer(dx, dy, sign):
        return (
            lax.rem(y + YS + sign * dy, YS) * rows_count + row,
            lax.rem(me + split + sign * dx, split),
        )

    def line_row(dz, dc, sign):
        z = lax.rem(row // 2 + ZS + sign * dz, ZS)
        return z * 2 + lax.rem(lax.rem(row, 2) + dc, 2)

    def mate(step):
        return (here, lax.rem(me + step, split))

    def behind(step):
        return lax.rem(me + split - step, split)

    def remote(source, target, send, recv, device):
        return pltpu.make_async_remote_copy(
            src_ref=source,
            dst_ref=target,
            send_sem=send,
            recv_sem=recv,
            device_id=device,
            device_id_type=MESH,
        )

    barrier = pltpu.get_barrier_semaphore()
    for dx, dy in plane:
        pl.semaphore_signal(
            barrier, inc=1, device_id=plane_peer(dx, dy, 1), device_id_type=MESH
        )
    for dz, dc in line:
        pl.semaphore_signal(
            barrier, inc=1, device_id=(y * rows_count + line_row(dz, dc, 1), me), device_id_type=MESH
        )
    blocks = width // 128
    own_count = own_ref.shape[0] // tokens
    per_image = pairs // own_count
    last = (((1,), (1,)), ((), ()))
    lane = lax.broadcasted_iota(jnp.int32, (1, 128), 1)
    first_half = lane < HD

    rows = norm_rows(own_ref[...].astype(jnp.float32))
    projected = lax.dot_general(rows, weights_ref[0], last, preferred_element_type=jnp.float32)
    projected = projected.astype(jnp.bfloat16) * jnp.bfloat16(HD ** (-0.5))
    zero = jnp.zeros((), jnp.bfloat16)
    for image in range(own_count):
        for block in range(blocks):
            part = projected[image * tokens : (image + 1) * tokens, block * 128 : (block + 1) * 128]
            queries[image, block, :tokens] = jnp.where(first_half, part, zero)
            queries[image, block, tokens:] = jnp.where(first_half, zero, part)

    chunk = 4 * tokens

    def project(step, carry):
        span = pl.ds(pl.multiple_of(step * chunk, chunk), chunk)
        part = far_ref[span, :]
        keys[span, :] = lax.dot_general(
            part, weights_ref[1], last, preferred_element_type=jnp.float32
        ).astype(jnp.bfloat16)
        values[span, :] = lax.dot_general(
            part, weights_ref[2], last, preferred_element_type=jnp.float32
        ).astype(jnp.bfloat16)
        return carry

    lax.fori_loop(0, pairs // 4, project, 0)
    pl.semaphore_wait(barrier, len(plane) + len(line))

    def depth_copy(step, slot):
        return remote(
            depth_ref.at[lax.rem(me + step, split)],
            depth_all.at[slot],
            x_send.at[step],
            x_recv.at[step],
            mate(step),
        )

    for step in range(1, split):
        depth_copy(step, me).start()
    depth_all[me] = depth_ref[me]
    staging[...] = jnp.zeros_like(staging)
    ones = jnp.ones((tokens, 128), jnp.bfloat16)

    def attend(pair, carry):
        span = pl.ds(pl.multiple_of(pair * tokens, tokens), tokens)
        image = pair // per_image
        for block in range(blocks):
            columns = slice(block * 128, (block + 1) * 128)
            scores = lax.dot_general(
                queries[image, block], keys[span, columns], last, preferred_element_type=jnp.float32
            )
            expos = jnp.exp(scores - jnp.max(scores, axis=1, keepdims=True)).astype(jnp.bfloat16)
            both = jnp.concatenate([values[span, columns], ones], axis=1)
            got = jnp.dot(expos, both, preferred_element_type=jnp.float32)
            got = got[:, :128] / got[:, 128:]
            mixed[span, columns] = jnp.where(first_half, got[:tokens], got[tokens:]).astype(
                jnp.bfloat16
            )
        return carry

    lax.fori_loop(0, pairs, attend, 0)

    def finish(step, carry):
        span = pl.ds(pl.multiple_of(step * chunk, chunk), chunk)
        image = step * 4 // per_image
        own = own_ref[pl.ds(pl.multiple_of(image * tokens, tokens), tokens), :].astype(jnp.float32)
        settled = jnp.dot(mixed[span, :], weights_ref[3], preferred_element_type=jnp.float32)
        settled = settled + jnp.concatenate([own] * 4, axis=0)
        heads = lax.dot_general(
            head_ref[...], norm_rows(settled), last, preferred_element_type=jnp.float32
        )
        for part in range(4):
            heads_all[step * 4 + part] = heads[:, part * tokens : (part + 1) * tokens]
        return carry

    lax.fori_loop(0, pairs // 4, finish, 0)
    for step in range(1, split):
        depth_copy(step, behind(step)).wait_recv()

    def widen(offset):
        both = jnp.concatenate(
            [depth_all[q, offset : offset + own_count, :share] for q in range(split)], axis=1
        )
        return jnp.concatenate(
            [
                jnp.broadcast_to(both[image : image + 1], (per_image, tokens))
                for image in range(own_count)
            ],
            axis=0,
        )

    depth = widen(0)
    valid = widen(own_count)
    token = lax.broadcasted_iota(jnp.int32, (1, tokens), 1)
    ray_x = (lax.rem(token, 16).astype(jnp.float32) - 7.5) * 0.125
    ray_y = (lax.div(token, 16).astype(jnp.float32) - (tokens // 16 - 1) * 0.5) * 0.125
    rays = [ray_x, ray_y, jnp.ones_like(ray_x)]
    points = [heads_all[:, component, :] for component in range(3)]
    confidence = 1.0 + jnp.exp(heads_all[:, 3, :])
    weight = valid * confidence * (2.0 / tokens)
    own_pose, far_pose = pose_own_ref[...], pose_far_ref[...]
    lane128 = lax.broadcasted_iota(jnp.int32, (pairs, 128), 1)
    own_grad = jnp.zeros((pairs, 128), jnp.float32)
    far_grad = jnp.zeros((pairs, 128), jnp.float32)
    depth_grad = jnp.zeros((pairs, tokens), jnp.float32)
    for component in range(3):
        base = 4 * component
        direction = sum(own_pose[:, base + k : base + k + 1] * rays[k] for k in range(3))
        world = own_pose[:, base + 3 : base + 4] + depth * direction
        predicted = far_pose[:, base + 3 : base + 4] + sum(
            far_pose[:, base + k : base + k + 1] * points[k] for k in range(3)
        )
        slope = weight * (world - predicted)
        depth_grad = depth_grad + slope * direction
        scaled = slope * depth
        for k in range(4):
            mine = scaled * rays[k] if k < 3 else slope
            other = slope * points[k] if k < 3 else slope
            mine = jnp.sum(mine, axis=1, keepdims=True)
            other = jnp.sum(other, axis=1, keepdims=True)
            own_grad = jnp.where(lane128 == base + k, mine, own_grad)
            far_grad = jnp.where(lane128 == base + k, -other, far_grad)
    total_images = YS * 128
    ids = lax.broadcasted_iota(jnp.int32, (pairs, total_images), 1)
    pair_ids = lax.broadcasted_iota(jnp.int32, (pairs, total_images), 0)
    own_ids = (here * split + me) * own_count + lax.div(pair_ids, per_image)
    hits = jnp.concatenate([ids == own_ids, ids == partner_ref[:, :1]], axis=0)
    table = lax.dot_general(
        jnp.concatenate([own_grad, far_grad], axis=0),
        hits.astype(jnp.float32),
        (((0,), (0,)), ((), ())),
        precision=lax.Precision.HIGHEST,
        preferred_element_type=jnp.float32,
    )
    for part in range(YS):
        dense[part] = table[:16, part * 128 : (part + 1) * 128]

    def plane_copy(number, dx, dy, slot):
        return remote(
            dense.at[lax.rem(y + dy, YS)],
            plane_in.at[slot],
            plane_send.at[number],
            plane_recv.at[number],
            plane_peer(dx, dy, 1),
        )

    for number, (dx, dy) in enumerate(plane):
        plane_copy(number, dx, dy, me * YS + y).start()
    plane_in[me * YS + y] = dense[y]

    old = jnp.concatenate(
        [depth[image * per_image : image * per_image + 1] for image in range(own_count)], axis=0
    )
    change = jnp.concatenate(
        [
            jnp.sum(
                depth_grad[image * per_image : (image + 1) * per_image], axis=0, keepdims=True
            )
            for image in range(own_count)
        ],
        axis=0,
    )
    moved = old - depth_step * change
    for place in range(split):
        span = slice(place * share, (place + 1) * share)
        for component, values_now in enumerate(points + [confidence]):
            staging[place, component * pairs : (component + 1) * pairs, :share] = values_now[:, span]
        staging[place, 4 * pairs : 4 * pairs + own_count, :share] = moved[:, span]

    def result_copy(step, slot):
        return remote(
            staging.at[lax.rem(me + step, split)],
            result_ref.at[slot],
            x_send.at[split + step],
            x_recv.at[split + step],
            mate(step),
        )

    for step in range(1, split):
        result_copy(step, me).start()
    result_ref[me] = staging[me]
    for number, (dx, dy) in enumerate(plane):
        source = lax.rem(me + split - dx, split) * YS + lax.rem(y + YS - dy, YS)
        plane_copy(number, dx, dy, source).wait_recv()
    gathered = jnp.sum(plane_in[...], axis=0)
    part_sum[...] = gathered
    line_in[row] = gathered

    def line_copy(number, dz, dc, slot):
        return remote(
            part_sum,
            line_in.at[slot],
            line_send.at[number],
            line_recv.at[number],
            (y * rows_count + line_row(dz, dc, 1), me),
        )

    for number, (dz, dc) in enumerate(line):
        line_copy(number, dz, dc, row).start()
    for number, (dz, dc) in enumerate(line):
        line_copy(number, dz, dc, line_row(dz, dc, -1)).wait_recv()
    total_ref[...] = jnp.sum(line_in[...], axis=0)
    for step in range(1, split):
        depth_copy(step, me).wait_send()
        result_copy(step, behind(step)).wait_recv()
        result_copy(step, me).wait_send()
    for number, (dx, dy) in enumerate(plane):
        plane_copy(number, dx, dy, me * YS + y).wait_send()
    for number, (dz, dc) in enumerate(line):
        line_copy(number, dz, dc, row).wait_send()


def decode(far, own, weights, head_rows, depth_tiles, pose_own, pose_far, partner_tile, pairs):
    width = own.shape[1]
    tokens = far.shape[0] // pairs
    own_count = own.shape[0] // tokens
    split = depth_tiles.shape[0]
    vmem = pl.BlockSpec(memory_space=pltpu.VMEM)
    result_rows = 4 * pairs + 8
    return pl.pallas_call(
        decode_kernel,
        out_shape=(
            jax.ShapeDtypeStruct((split, result_rows, 128), jnp.float32),
            jax.ShapeDtypeStruct((16, 128), jnp.float32),
        ),
        in_specs=[vmem] * 8,
        out_specs=(vmem, vmem),
        scratch_shapes=[
            pltpu.VMEM((own_count, width // 128, 2 * tokens, 128), jnp.bfloat16),
            pltpu.VMEM(far.shape, jnp.bfloat16),
            pltpu.VMEM(far.shape, jnp.bfloat16),
            pltpu.VMEM(far.shape, jnp.bfloat16),
            pltpu.VMEM((pairs, head_rows.shape[0], tokens), jnp.float32),
            pltpu.VMEM(depth_tiles.shape, jnp.float32),
            pltpu.VMEM((split, result_rows, 128), jnp.float32),
            pltpu.VMEM((YS, 16, 128), jnp.float32),
            pltpu.VMEM((split * YS, 16, 128), jnp.float32),
            pltpu.VMEM((16, 128), jnp.float32),
            pltpu.VMEM((2 * ZS, 16, 128), jnp.float32),
            pltpu.SemaphoreType.DMA((2 * split,)),
            pltpu.SemaphoreType.DMA((2 * split,)),
            pltpu.SemaphoreType.DMA((split * YS,)),
            pltpu.SemaphoreType.DMA((split * YS,)),
            pltpu.SemaphoreType.DMA((2 * ZS,)),
            pltpu.SemaphoreType.DMA((2 * ZS,)),
        ],
        compiler_params=pltpu.CompilerParams(
            collective_id=1, has_side_effects=True, vmem_limit_bytes=48 * 2**20
        ),
        name="decode",
    )(far, own, weights, head_rows, depth_tiles, pose_own, pose_far, partner_tile)


def shards(
    patches,
    encoder_proj,
    encoder_out,
    decoder_embed,
    decoder_proj,
    decoder_out,
    head_weight,
    partners,
    depths,
    camera_poses,
    valid_mask,
):
    images, tokens, model_width = patches.shape
    dec_width = decoder_embed.shape[1]
    enc_local = encoder_proj.shape[2]
    split = lax.axis_size("mp")
    place = lax.axis_index("mp")
    own_count = images // split
    flat_partner = partners.reshape(-1)
    pair_count = flat_partner.shape[0]
    groups = lax.axis_size("img")
    here = lax.axis_index("img")
    weights = jnp.concatenate([jnp.transpose(decoder_proj, (1, 2, 0)), decoder_out[None]], axis=0)
    pose_tile = jnp.pad(
        camera_poses.astype(jnp.bfloat16), ((0, 4), (0, 128 - camera_poses.shape[1]))
    )

    token_share = tokens // split
    first_token = place * token_share
    patch_own = lax.dynamic_slice_in_dim(patches, first_token, token_share, 1)
    owner = flat_partner // images
    shift_y = (here // (2 * ZS) - owner // (2 * ZS)) % YS
    shift_z = ((here // 2) % ZS - (owner // 2) % ZS) % ZS
    shift_core = (here - owner) % 2
    pick = ((shift_core * YS + shift_y) * ZS + shift_z) * images + flat_partner % images
    far_rows, own_rows, weights_full, pose_tiles = exchange(
        pick,
        patches.reshape(images * tokens, model_width),
        patch_own,
        encoder_proj.reshape(model_width, 3 * enc_local),
        encoder_out,
        decoder_embed,
        weights,
        pose_tile,
        pair_count,
        groups,
        split,
    )
    head_rows = jnp.pad(head_weight.T, ((0, 12), (0, 0)))
    own_pairs = pair_count // split
    depth_mask = jnp.stack([depths, valid_mask.astype(jnp.float32)], axis=0)
    depth_tiles = depth_mask.reshape(2, split, own_count, token_share).transpose(1, 0, 2, 3)
    depth_tiles = jnp.pad(
        depth_tiles.reshape(split, 2 * own_count, token_share),
        ((0, 0), (0, 8 - 2 * own_count), (0, 128 - token_share)),
    )
    pose_own = lax.dynamic_slice_in_dim(camera_poses, place * own_count, own_count, 1)
    pose_own = jnp.pad(jnp.repeat(pose_own.T, K, axis=0), ((0, 0), (0, 116)))
    own_partner = lax.dynamic_slice_in_dim(flat_partner, place * own_pairs, own_pairs, 0)
    partner_tile = jnp.broadcast_to(own_partner[:, None], (own_pairs, 128))
    picked_pose = pose_tiles[own_partner // images, :12, :images].astype(jnp.float32)
    local = (own_partner % images)[:, None, None] == jnp.arange(images, dtype=jnp.int32)
    pose_far = jnp.pad(jnp.sum(jnp.where(local, picked_pose, 0.0), axis=2), ((0, 0), (0, 116)))
    results, total = decode(
        far_rows.reshape(own_pairs * tokens, dec_width),
        own_rows.reshape(own_count * tokens, dec_width),
        weights_full.reshape(4, dec_width, dec_width),
        head_rows,
        depth_tiles,
        pose_own,
        pose_far,
        partner_tile,
        own_pairs,
    )
    pointmap = results[:, : 4 * own_pairs, :token_share].reshape(split, 4, own_pairs, token_share)
    pointmap = pointmap.transpose(1, 0, 2, 3).reshape(4, pair_count, token_share)
    new_depths = results[:, 4 * own_pairs : 4 * own_pairs + own_count, :token_share]
    new_depths = new_depths.reshape(images, token_share)
    grad_pose = lax.dynamic_slice(total, (0, here % (2 * ZS) * images), (12, images))
    new_poses = camera_poses - pose_step * grad_pose
    return (pointmap, new_depths, new_poses)


def solution(mesh):
    placed = (
        P("img", None, None),
        P(None, None, "mp"),
        P("mp", None),
        P(),
        P(None, None, "mp"),
        P("mp", None),
        P(),
        P("img", None),
        P("img", "mp"),
        P(None, "img"),
        P("img", "mp"),
    )
    return jax.shard_map(
        shards,
        mesh=mesh,
        in_specs=placed,
        out_specs=(P(None, "img", "mp"), P("img", "mp"), P(None, "img")),
        check_vma=False,
    )
```

```python
import functools

import jax
import jax.numpy as jnp
from jax import lax
from jax.experimental import pallas as pl
from jax.experimental.pallas import tpu as pltpu
from jax.sharding import PartitionSpec as P

HD = 64
K = 8


epsilon = 1e-06
depth_step = 0.1
pose_step = 0.005


def norm_rows(values):
    average = jnp.mean(values, axis=-1, keepdims=True)
    centred = values - average
    variance = jnp.mean(centred * centred, axis=-1, keepdims=True)
    return (centred * lax.rsqrt(variance + epsilon)).astype(jnp.bfloat16)


YS, ZS, CORES = 4, 8, 2
FIRST = 5
WIDTHS = (384, 384)
RELAY = 18
AHEAD, DELAY = 4.0, 4.0
MESH = pl.DeviceIdType.MESH


def link_plan(images, spans):
    split = {"z": (0, FIRST), "y": (FIRST, images)}
    full = sum(spans)
    waiting = {"y+": [], "y-": [], "z+": [], "z-": []}
    free = {link: 0.0 for link in waiting}
    plan, flight, steps = [], [], []

    def push(now, chunk, link, source, target, span):
        waiting[link].append((chunk, len(waiting[link]) + 1000 * now, source, target, span))

    def issue(now):
        for link, queue in waiting.items():
            while queue and free[link] <= now + AHEAD:
                entry = min(queue)
                queue.remove(entry)
                chunk, _, source, target, span = entry
                free[link] = max(now, free[link]) + (span[1] - span[0]) * spans[chunk] / full
                flight.append((free[link] + DELAY, len(plan)))
                steps.append(("send", len(plan)))
                plan.append((chunk, link, source, target, span))

    def forward(now, chunk, dy, dz, span):
        if span[1] <= FIRST:
            low, high = split["z"]
            half = (low + high + 1) // 2
            if dy == 0:
                if dz in (0, 1, 2):
                    push(now, chunk, "z+", (dy, dz), (dy, dz + 1), span)
                if dz == 3:
                    push(now, chunk, "z+", (dy, dz), (dy, 4), (low, half))
                if dz in (0, 7, 6):
                    push(now, chunk, "z-", (dy, dz), (dy, (dz - 1) % ZS), span)
                if dz == 5:
                    push(now, chunk, "z-", (dy, dz), (dy, 4), (half, high))
                push(now, chunk, "y+", (dy, dz), (1, dz), span)
                push(now, chunk, "y-", (dy, dz), (3, dz), span)
            if dy == 1 and dz % 2 == 0:
                push(now, chunk, "y+", (dy, dz), (2, dz), span)
            if dy == 3 and dz % 2 == 1:
                push(now, chunk, "y-", (dy, dz), (2, dz), span)
        else:
            low, high = split["y"]
            half = (low + high + 1) // 2
            if dz == 0:
                if dy == 0:
                    push(now, chunk, "y+", (0, 0), (1, 0), span)
                    push(now, chunk, "y-", (0, 0), (3, 0), span)
                if dy == 1:
                    push(now, chunk, "y+", (1, 0), (2, 0), (low, half))
                if dy == 3:
                    push(now, chunk, "y-", (3, 0), (2, 0), (half, high))
            if dz in (0, 1, 2):
                push(now, chunk, "z+", (dy, dz), (dy, dz + 1), span)
            if dz == 3 and dy < 2:
                push(now, chunk, "z+", (dy, dz), (dy, 4), span)
            if dz in (0, 7, 6):
                push(now, chunk, "z-", (dy, dz), (dy, (dz - 1) % ZS), span)
            if dz == 5 and dy >= 2:
                push(now, chunk, "z-", (dy, dz), (dy, 4), span)

    for chunk in range(len(spans)):
        forward(0.0, chunk, 0, 0, split["z"])
        forward(0.0, chunk, 0, 0, split["y"])
    issue(0.0)
    while flight:
        entry = min(flight)
        flight.remove(entry)
        now, number = entry
        chunk, _, _, target, span = plan[number]
        steps.append(("wait", number))
        forward(now, chunk, target[0], target[1], span)
        issue(now)
    return steps, plan


def exchange_kernel(
    pick_ref,
    patches_ref,
    patch_own_ref,
    enc_proj_ref,
    enc_out_ref,
    embed_ref,
    weights_ref,
    pose_ref,
    far_ref,
    own_ref,
    weights_all,
    pose_all,
    *scratch,
):
    chunks = len(WIDTHS)
    held, scratch = scratch[:chunks], scratch[chunks:]
    staged, scratch = scratch[:chunks], scratch[chunks:]
    relay, scratch = scratch[:chunks], scratch[chunks:]
    (
        mixed,
        mixed_all,
        enc_out_all,
        emb_ref,
        enc_send,
        enc_recv,
        ring_send,
        ring_recv,
        twin_send,
        twin_recv,
        line_send,
        line_recv,
        pose_send,
        pose_recv,
        far_send,
        far_recv,
        local_sem,
    ) = scratch
    columns = [slice(sum(WIDTHS[:c]), sum(WIDTHS[: c + 1])) for c in range(chunks)]
    images, share, width = emb_ref.shape
    here = lax.axis_index("img")
    me = lax.axis_index("mp")
    core = lax.rem(here, 2)
    z = lax.rem(here // 2, ZS)
    y = here // (2 * ZS)
    split = far_ref.shape[1]
    per_dev = far_ref.shape[0]
    half_dev = per_dev // 2

    def spot(yy, zz, cc):
        return ((yy * ZS + zz) * 2 + cc, me)

    def mate(step):
        return (here, lax.rem(me + step, split))

    def behind(step):
        return lax.rem(me + split - step, split)

    twin = spot(y, z, 1 - core)
    links = {
        "y+": spot(lax.rem(y + 1, YS), z, core),
        "y-": spot(lax.rem(y + YS - 1, YS), z, core),
        "z+": spot(y, lax.rem(z + 1, ZS), core),
        "z-": spot(y, lax.rem(z + ZS - 1, ZS), core),
    }
    line = [(dz, dc) for dz in range(ZS) for dc in range(CORES) if dz or dc]

    def line_peer(dz, dc, sign):
        return spot(y, lax.rem(z + ZS + sign * dz, ZS), lax.rem(core + dc, 2))

    def y_peer(dy, sign):
        return spot(lax.rem(y + YS + sign * dy, YS), z, core)

    barrier = pltpu.get_barrier_semaphore()
    peers = [line_peer(dz, dc, 1) for dz, dc in line]
    peers += [y_peer(dy, 1) for dy in range(1, YS)]
    peers += [mate(step) for step in range(1, split)]
    for peer in peers:
        pl.semaphore_signal(barrier, inc=1, device_id=peer, device_id_type=MESH)
    pose_all[here] = pose_ref[...]
    pl.semaphore_wait(barrier, len(peers))

    def remote(source, target, send, recv, device):
        return pltpu.make_async_remote_copy(
            src_ref=source,
            dst_ref=target,
            send_sem=send,
            recv_sem=recv,
            device_id=device,
            device_id_type=MESH,
        )

    steps, plan = link_plan(images, WIDTHS)

    def block(chunk, side, slot, span):
        first = ((side * YS + slot[0]) * ZS + slot[1]) * images
        return held[chunk].at[pl.ds(first + span[0], span[1] - span[0])]

    def ring(number):
        chunk, link, source, target, span = plan[number]
        return remote(
            block(chunk, 0, source, span),
            block(chunk, 0, target, span),
            ring_send.at[number],
            ring_recv.at[number],
            links[link],
        )

    twins = [(entry[0], entry[3], entry[4]) for entry in plan]
    twins += [(chunk, (0, 0), (0, images)) for chunk in range(chunks)]

    def twin_copy(number):
        chunk, slot, span = twins[number]
        return remote(
            block(chunk, 0, slot, span),
            block(chunk, 1, slot, span),
            twin_send.at[number],
            twin_recv.at[number],
            twin,
        )

    def pose_line(dz, dc, number, slot):
        return remote(
            pose_all.at[slot],
            pose_all.at[slot],
            pose_send.at[number],
            pose_recv.at[number],
            line_peer(dz, dc, 1),
        )

    for number, (dz, dc) in enumerate(line):
        pose_line(dz, dc, number, here).start()

    pair_images = images // split

    def own_copy(step, slot):
        return remote(
            emb_ref.at[pl.ds(pair_images * lax.rem(me + step, split), pair_images)],
            own_ref.at[:, slot],
            line_send.at[step],
            line_recv.at[step],
            mate(step),
        )

    def weight_copy(step, slot):
        return remote(
            weights_ref.at[pl.ds(2 * core, 2)],
            weights_all.at[pl.ds(2 * core, 2), slot],
            line_send.at[split + step],
            line_recv.at[split + step],
            mate(step),
        )

    def weight_relay(step, slot):
        kind = 2 * core + (0 if step == 1 else 1)
        return remote(
            weights_all.at[pl.ds(kind, 1), slot],
            weights_all.at[pl.ds(kind, 1), slot],
            line_send.at[3 * split + step],
            line_recv.at[3 * split + step],
            mate(step),
        )

    def weight_twin(step, half, slot):
        return remote(
            weights_all.at[pl.ds(2 * half, 2), slot],
            weights_all.at[pl.ds(2 * half, 2), slot],
            line_send.at[2 * split + step],
            line_recv.at[2 * split + step],
            twin,
        )

    def far_direct(chunk, step, slot):
        return remote(
            staged[chunk].at[pl.ds(per_dev * lax.rem(me + step, split), per_dev)],
            far_ref.at[:, slot, :, columns[chunk]],
            far_send.at[chunk, step],
            far_recv.at[chunk, step],
            mate(step),
        )

    def far_relay(chunk, step):
        side = 0 if step == 1 else 1
        return remote(
            staged[chunk].at[pl.ds(per_dev * lax.rem(me + 2, split) + side * half_dev, half_dev)],
            relay[chunk].at[side],
            far_send.at[chunk, split + step],
            far_recv.at[chunk, split + step],
            mate(step),
        )

    def far_onward(chunk, step, slot):
        side = 0 if step == 1 else 1
        return remote(
            relay[chunk].at[side],
            far_ref.at[pl.ds(side * half_dev, half_dev), slot, :, columns[chunk]],
            far_send.at[chunk, 2 * split + step],
            far_recv.at[chunk, 2 * split + step],
            mate(step),
        )

    def out_copy(step, slot):
        return remote(
            enc_out_ref,
            enc_out_all.at[slot],
            enc_send.at[step],
            enc_recv.at[step],
            mate(step),
        )

    def mixed_copy(part, step, slot):
        span = pl.ds(part * (images // 2), images // 2)
        return remote(
            mixed.at[lax.rem(me + step, split), span],
            mixed_all.at[slot, span],
            enc_send.at[split * (1 + part) + step],
            enc_recv.at[split * (1 + part) + step],
            mate(step),
        )

    for step in range(1, split):
        out_copy(step, me).start()
    enc_out_all[me] = enc_out_ref[...]
    tokens = share * split
    local = enc_out_ref.shape[0]
    last = (((1,), (1,)), ((), ()))
    first_half = lax.broadcasted_iota(jnp.int32, (1, 128), 1) < HD
    zero = jnp.zeros((), jnp.bfloat16)
    ones = jnp.ones((tokens, 128), jnp.bfloat16)

    def encode(pair, carry):
        span = pl.ds(pl.multiple_of(pair * 2 * tokens, 2 * tokens), 2 * tokens)
        normed = norm_rows(patches_ref[span, :].astype(jnp.float32))
        projected = jnp.dot(normed, enc_proj_ref[...], preferred_element_type=jnp.float32)
        projected = projected.astype(jnp.bfloat16)
        places = [(image, first) for image in range(2) for first in range(0, local, 128)]

        def take(kind, image, first):
            lines = slice(image * tokens, (image + 1) * tokens)
            return projected[lines, kind * local + first : kind * local + first + 128]

        scores = []
        for image, first in places:
            query = take(0, image, first) * jnp.bfloat16(HD ** (-0.5))
            both = jnp.concatenate(
                [jnp.where(first_half, query, zero), jnp.where(first_half, zero, query)], axis=0
            )
            scores.append(
                lax.dot_general(
                    both, take(1, image, first), last, preferred_element_type=jnp.float32
                )
            )
        expos = [
            jnp.exp(each - jnp.max(each, axis=1, keepdims=True)).astype(jnp.bfloat16)
            for each in scores
        ]
        sums = [
            jnp.dot(
                each,
                jnp.concatenate([take(2, image, first), ones], axis=1),
                preferred_element_type=jnp.float32,
            )
            for each, (image, first) in zip(expos, places)
        ]
        for each, (image, first) in zip(sums, places):
            got = each[:, :128] / each[:, 128:]
            got = jnp.where(first_half, got[:tokens], got[tokens:])
            for place in range(split):
                mixed[place, pair * 2 + image, :, first : first + 128] = got[
                    place * share : (place + 1) * share
                ].astype(jnp.bfloat16)
        return carry

    lax.fori_loop(0, images // 4, encode, 0)
    for step in range(1, split):
        mixed_copy(0, step, me).start()
    lax.fori_loop(images // 4, images // 2, encode, 0)
    for step in range(1, split):
        mixed_copy(1, step, me).start()
    for step in (1, 3):
        weight_copy(step, me).start()
    mixed_all[me] = mixed[me]
    encoded = patch_own_ref[...].astype(jnp.float32).reshape(images * share, -1)
    for step in range(split):
        source = behind(step)
        if step:
            out_copy(step, source).wait_recv()
            mixed_copy(0, step, source).wait_recv()
            mixed_copy(1, step, source).wait_recv()
        part = mixed_all[source].astype(jnp.float32).reshape(images * share, local)
        encoded = encoded + jnp.dot(
            part.astype(jnp.bfloat16), enc_out_all[source], preferred_element_type=jnp.float32
        )
    embedded = jnp.dot(norm_rows(encoded), embed_ref[...], preferred_element_type=jnp.float32)
    embedded = embedded.astype(jnp.bfloat16).astype(jnp.float32)
    emb_ref[...] = embedded.reshape(images, share, width).astype(jnp.bfloat16)
    normed_rows = norm_rows(embedded).astype(jnp.float32).reshape(images, share, width)
    for chunk in range(chunks):
        held[chunk][pl.ds(0, images)] = normed_rows[:, :, columns[chunk]].astype(jnp.bfloat16)
    opening = [kind for kind, _ in steps].index("wait")
    for _, number in steps[:opening]:
        ring(number).start()
    for chunk in range(chunks):
        twin_copy(len(plan) + chunk).start()

    for step in range(1, split):
        own_copy(step, me).start()
    own_local = pltpu.make_async_copy(
        emb_ref.at[pl.ds(pair_images * me, pair_images)], own_ref.at[:, me], local_sem.at[0]
    )
    own_local.start()
    weight_local = pltpu.make_async_copy(weights_ref, weights_all.at[:, me], local_sem.at[1])
    weight_local.start()

    def far_local(chunk):
        return pltpu.make_async_copy(
            staged[chunk].at[pl.ds(per_dev * me, per_dev)],
            far_ref.at[:, me, :, columns[chunk]],
            local_sem.at[2 + chunk],
        )

    def choose(chunk):
        for number, entry in enumerate(twins):
            if entry[0] == chunk:
                twin_copy(number).wait_recv()

        def pick(index, carry):
            staged[chunk][index] = held[chunk][pick_ref[index]]
            return carry

        lax.fori_loop(0, per_dev * split, pick, 0, unroll=4)
        for step in (1, 3):
            far_relay(chunk, step).start()
        for step in (1, 3):
            far_direct(chunk, step, me).start()
        far_local(chunk).start()

    def pass_on(chunk):
        for step in (1, 3):
            far_relay(chunk, step).wait_recv()
            far_onward(chunk, step, behind(step)).start()

    def pose_cross(dy, row):
        return remote(
            pose_all.at[pl.ds(row * 2 * ZS, 2 * ZS)],
            pose_all.at[pl.ds(row * 2 * ZS, 2 * ZS)],
            pose_send.at[len(line) + dy - 1],
            pose_recv.at[len(line) + dy - 1],
            y_peer(dy, 1),
        )

    def pose_second():
        for number, (dz, dc) in enumerate(line):
            pose_line(dz, dc, number, line_peer(dz, dc, -1)[0]).wait_recv()
        for dy in range(1, YS):
            pose_cross(dy, y).start()

    def weights_second():
        for step in (1, 3):
            weight_copy(step, behind(step)).wait_recv()
            weight_relay(step, behind(step)).start()
            weight_twin(step, core, behind(step)).start()

    def weights_third():
        for step in (1, 3):
            weight_relay(step, behind(2)).wait_recv()
        weight_twin(2, core, behind(2)).start()

    waits = [number for kind, number in steps if kind == "wait"]
    final = {c: max(i for i, n in enumerate(waits) if plan[n][0] == c) for c in range(chunks)}
    events = {8: pose_second, len(waits) // 4: weights_second, len(waits) // 2: weights_third}
    later, pending, count = {}, [], 0
    for kind, number in steps[opening:]:
        if kind == "send":
            ring(number).start()
            continue
        for action in pending:
            action()
        pending = []
        ring(number).wait_recv()
        twin_copy(number).start()
        count += 1
        if count in events:
            pending.append(events[count])
        for chunk in range(chunks):
            if final[chunk] == count - 1:
                pending.append(functools.partial(choose, chunk))
                later[count + RELAY] = chunk
        if count in later:
            pending.append(functools.partial(pass_on, later.pop(count)))
    for action in pending:
        action()
    for chunk in later.values():
        pass_on(chunk)
    for dy in range(1, YS):
        pose_cross(dy, lax.rem(y + YS - dy, YS)).wait_recv()
    for step in range(1, split):
        own_copy(step, behind(step)).wait_recv()
        weight_twin(step, 1 - core, behind(step)).wait_recv()
    own_local.wait()
    weight_local.wait()
    for number in range(len(plan)):
        ring(number).wait_send()
    for number in range(len(twins)):
        twin_copy(number).wait_send()
    for number, (dz, dc) in enumerate(line):
        pose_line(dz, dc, number, here).wait_send()
    for dy in range(1, YS):
        pose_cross(dy, y).wait_send()
    for step in range(1, split):
        out_copy(step, me).wait_send()
        mixed_copy(0, step, me).wait_send()
        mixed_copy(1, step, me).wait_send()
        own_copy(step, me).wait_send()
        weight_twin(step, core, behind(step)).wait_send()
    for step in (1, 3):
        weight_copy(step, me).wait_send()
        weight_relay(step, behind(step)).wait_send()
    for chunk in range(chunks):
        far_local(chunk).wait()
        for step in (1, 3):
            far_relay(chunk, step).wait_send()
            far_direct(chunk, step, behind(step)).wait_recv()
            far_direct(chunk, step, me).wait_send()
            far_onward(chunk, step, behind(2)).wait_recv()
            far_onward(chunk, step, behind(step)).wait_send()


def exchange(pick, patches, patch_own, enc_proj, enc_out, embed, weights, pose, pairs, groups, split):
    images, share, _ = patch_own.shape
    width = embed.shape[1]
    chunks = len(WIDTHS)
    count = len(link_plan(images, WIDTHS)[1])
    vmem = pl.BlockSpec(memory_space=pltpu.VMEM)
    per_dev = pairs // split
    return pl.pallas_call(
        exchange_kernel,
        out_shape=(
            jax.ShapeDtypeStruct((per_dev, split, share, width), jnp.bfloat16),
            jax.ShapeDtypeStruct((images // split, split, share, width), jnp.bfloat16),
            jax.ShapeDtypeStruct((4, split) + weights.shape[1:], jnp.bfloat16),
            jax.ShapeDtypeStruct((groups,) + pose.shape, jnp.bfloat16),
        ),
        in_specs=[pl.BlockSpec(memory_space=pltpu.SMEM)] + [vmem] * 7,
        out_specs=(vmem,) * 4,
        scratch_shapes=[pltpu.VMEM((groups * images, share, w), jnp.bfloat16) for w in WIDTHS]
        + [pltpu.VMEM((pairs, share, w), jnp.bfloat16) for w in WIDTHS]
        + [pltpu.VMEM((2, per_dev // 2, share, w), jnp.bfloat16) for w in WIDTHS]
        + [
            pltpu.VMEM((split, images, share, enc_out.shape[0]), jnp.bfloat16),
            pltpu.VMEM((split, images, share, enc_out.shape[0]), jnp.bfloat16),
            pltpu.VMEM((split,) + enc_out.shape, jnp.bfloat16),
            pltpu.VMEM((images, share, width), jnp.bfloat16),
            pltpu.SemaphoreType.DMA((3 * split,)),
            pltpu.SemaphoreType.DMA((3 * split,)),
            pltpu.SemaphoreType.DMA((count,)),
            pltpu.SemaphoreType.DMA((count,)),
            pltpu.SemaphoreType.DMA((count + chunks,)),
            pltpu.SemaphoreType.DMA((count + chunks,)),
            pltpu.SemaphoreType.DMA((4 * split,)),
            pltpu.SemaphoreType.DMA((4 * split,)),
            pltpu.SemaphoreType.DMA((2 * ZS + YS,)),
            pltpu.SemaphoreType.DMA((2 * ZS + YS,)),
            pltpu.SemaphoreType.DMA((chunks, 3 * split)),
            pltpu.SemaphoreType.DMA((chunks, 3 * split)),
            pltpu.SemaphoreType.DMA((2 + chunks,)),
        ],
        compiler_params=pltpu.CompilerParams(
            collective_id=0, has_side_effects=True, vmem_limit_bytes=56 * 2**20
        ),
        name="exchange",
    )(pick, patches, patch_own, enc_proj, enc_out, embed, weights, pose)


def decode_kernel(
    far_ref,
    own_ref,
    weights_ref,
    head_ref,
    depth_ref,
    pose_own_ref,
    pose_all_ref,
    partner_ref,
    partner_row_ref,
    result_ref,
    total_ref,
    queries,
    keys,
    values,
    mixed,
    heads_all,
    depth_all,
    staging,
    dense,
    plane_in,
    part_sum,
    line_in,
    x_send,
    x_recv,
    plane_send,
    plane_recv,
    line_send,
    line_recv,
):
    width = own_ref.shape[1]
    pairs, _, tokens = heads_all.shape
    split = depth_all.shape[0]
    share = tokens // split
    here = lax.axis_index("img")
    me = lax.axis_index("mp")
    rows_count = 2 * ZS
    row = lax.rem(here, rows_count)
    y = here // rows_count
    plane = [(dx, dy) for dx in range(split) for dy in range(YS) if dx or dy]
    line = [(dz, dc) for dz in range(ZS) for dc in range(CORES) if dz or dc]

    def plane_peer(dx, dy, sign):
        return (
            lax.rem(y + YS + sign * dy, YS) * rows_count + row,
            lax.rem(me + split + sign * dx, split),
        )

    def line_row(dz, dc, sign):
        z = lax.rem(row // 2 + ZS + sign * dz, ZS)
        return z * 2 + lax.rem(lax.rem(row, 2) + dc, 2)

    def mate(step):
        return (here, lax.rem(me + step, split))

    def behind(step):
        return lax.rem(me + split - step, split)

    def remote(source, target, send, recv, device):
        return pltpu.make_async_remote_copy(
            src_ref=source,
            dst_ref=target,
            send_sem=send,
            recv_sem=recv,
            device_id=device,
            device_id_type=MESH,
        )

    barrier = pltpu.get_barrier_semaphore()
    for dx, dy in plane:
        pl.semaphore_signal(
            barrier, inc=1, device_id=plane_peer(dx, dy, 1), device_id_type=MESH
        )
    for dz, dc in line:
        pl.semaphore_signal(
            barrier, inc=1, device_id=(y * rows_count + line_row(dz, dc, 1), me), device_id_type=MESH
        )
    blocks = width // 128
    own_count = own_ref.shape[0] // tokens
    per_image = pairs // own_count
    last = (((1,), (1,)), ((), ()))
    lane = lax.broadcasted_iota(jnp.int32, (1, 128), 1)
    first_half = lane < HD

    rows = norm_rows(own_ref[...].astype(jnp.float32))
    projected = lax.dot_general(rows, weights_ref[0], last, preferred_element_type=jnp.float32)
    projected = projected.astype(jnp.bfloat16) * jnp.bfloat16(HD ** (-0.5))
    zero = jnp.zeros((), jnp.bfloat16)
    for image in range(own_count):
        for block in range(blocks):
            part = projected[image * tokens : (image + 1) * tokens, block * 128 : (block + 1) * 128]
            queries[image, block, :tokens] = jnp.where(first_half, part, zero)
            queries[image, block, tokens:] = jnp.where(first_half, zero, part)

    chunk = 4 * tokens

    def project(step, carry):
        span = pl.ds(pl.multiple_of(step * chunk, chunk), chunk)
        part = far_ref[span, :]
        keys[span, :] = lax.dot_general(
            part, weights_ref[1], last, preferred_element_type=jnp.float32
        ).astype(jnp.bfloat16)
        values[span, :] = lax.dot_general(
            part, weights_ref[2], last, preferred_element_type=jnp.float32
        ).astype(jnp.bfloat16)
        return carry

    lax.fori_loop(0, pairs // 4, project, 0, unroll=2)
    pl.semaphore_wait(barrier, len(plane) + len(line))

    def depth_copy(step, slot):
        return remote(
            depth_ref.at[lax.rem(me + step, split)],
            depth_all.at[slot],
            x_send.at[step],
            x_recv.at[step],
            mate(step),
        )

    for step in range(1, split):
        depth_copy(step, me).start()
    depth_all[me] = depth_ref[me]
    staging[...] = jnp.zeros_like(staging)
    members = own_count * split
    group_count, pose_rows, _ = pose_all_ref.shape
    lane_ids = lax.broadcasted_iota(jnp.int32, (pairs, 128), 1)
    chosen = (lane_ids == lax.rem(partner_ref[...], members)).astype(jnp.bfloat16)
    candidates = lax.dot_general(
        pose_all_ref[...].reshape(group_count * pose_rows, 128),
        chosen,
        last,
        preferred_element_type=jnp.float32,
    ).reshape(group_count, pose_rows, pairs)
    owners = lax.broadcasted_iota(jnp.int32, (group_count, pose_rows, pairs), 0)
    held_by = lax.div(partner_row_ref[:1, :pairs], members)
    turned = jnp.sum(jnp.where(owners == held_by[None], candidates, 0.0), axis=0)
    same = lax.broadcasted_iota(jnp.int32, (pose_rows, pose_rows), 0) == lax.broadcasted_iota(
        jnp.int32, (pose_rows, pose_rows), 1
    )
    far_pose = lax.dot_general(
        turned.astype(jnp.bfloat16),
        same.astype(jnp.bfloat16),
        (((0,), (0,)), ((), ())),
        preferred_element_type=jnp.float32,
    )
    ones = jnp.ones((tokens, 128), jnp.bfloat16)

    def attend(pair, carry):
        span = pl.ds(pl.multiple_of(pair * tokens, tokens), tokens)
        image = pair // per_image
        columns = [slice(block * 128, (block + 1) * 128) for block in range(blocks)]
        scores = [
            lax.dot_general(
                queries[image, block], keys[span, part], last, preferred_element_type=jnp.float32
            )
            for block, part in enumerate(columns)
        ]
        expos = [
            jnp.exp(each - jnp.max(each, axis=1, keepdims=True)).astype(jnp.bfloat16)
            for each in scores
        ]
        sums = [
            jnp.dot(
                each,
                jnp.concatenate([values[span, part], ones], axis=1),
                preferred_element_type=jnp.float32,
            )
            for each, part in zip(expos, columns)
        ]
        for each, part in zip(sums, columns):
            got = each[:, :128] / each[:, 128:]
            mixed[span, part] = jnp.where(first_half, got[:tokens], got[tokens:]).astype(
                jnp.bfloat16
            )
        return carry

    lax.fori_loop(0, pairs, attend, 0, unroll=2)

    def finish(step, carry):
        span = pl.ds(pl.multiple_of(step * chunk, chunk), chunk)
        image = step * 4 // per_image
        own = own_ref[pl.ds(pl.multiple_of(image * tokens, tokens), tokens), :].astype(jnp.float32)
        settled = jnp.dot(mixed[span, :], weights_ref[3], preferred_element_type=jnp.float32)
        settled = settled + jnp.concatenate([own] * 4, axis=0)
        heads = lax.dot_general(
            head_ref[...], norm_rows(settled), last, preferred_element_type=jnp.float32
        )
        for part in range(4):
            heads_all[step * 4 + part] = heads[:, part * tokens : (part + 1) * tokens]
        return carry

    lax.fori_loop(0, pairs // 4, finish, 0, unroll=2)
    for step in range(1, split):
        depth_copy(step, behind(step)).wait_recv()

    def widen(offset):
        both = jnp.concatenate(
            [depth_all[q, offset : offset + own_count, :share] for q in range(split)], axis=1
        )
        return jnp.concatenate(
            [
                jnp.broadcast_to(both[image : image + 1], (per_image, tokens))
                for image in range(own_count)
            ],
            axis=0,
        )

    depth = widen(0)
    valid = widen(own_count)
    token = lax.broadcasted_iota(jnp.int32, (1, tokens), 1)
    ray_x = (lax.rem(token, 16).astype(jnp.float32) - 7.5) * 0.125
    ray_y = (lax.div(token, 16).astype(jnp.float32) - (tokens // 16 - 1) * 0.5) * 0.125
    rays = [ray_x, ray_y, jnp.ones_like(ray_x)]
    points = [heads_all[:, component, :] for component in range(3)]
    confidence = 1.0 + jnp.exp(heads_all[:, 3, :])
    weight = valid * confidence * (2.0 / tokens)
    own_pose = pose_own_ref[...]
    lane128 = lax.broadcasted_iota(jnp.int32, (pairs, 128), 1)
    own_grad = jnp.zeros((pairs, 128), jnp.float32)
    far_grad = jnp.zeros((pairs, 128), jnp.float32)
    depth_grad = jnp.zeros((pairs, tokens), jnp.float32)
    for component in range(3):
        base = 4 * component
        direction = sum(own_pose[:, base + k : base + k + 1] * rays[k] for k in range(3))
        world = own_pose[:, base + 3 : base + 4] + depth * direction
        predicted = far_pose[:, base + 3 : base + 4] + sum(
            far_pose[:, base + k : base + k + 1] * points[k] for k in range(3)
        )
        slope = weight * (world - predicted)
        depth_grad = depth_grad + slope * direction
        scaled = slope * depth
        for k in range(4):
            mine = scaled * rays[k] if k < 3 else slope
            other = slope * points[k] if k < 3 else slope
            mine = jnp.sum(mine, axis=1, keepdims=True)
            other = jnp.sum(other, axis=1, keepdims=True)
            own_grad = jnp.where(lane128 == base + k, mine, own_grad)
            far_grad = jnp.where(lane128 == base + k, -other, far_grad)
    total_images = YS * 128
    ids = lax.broadcasted_iota(jnp.int32, (pairs, total_images), 1)
    pair_ids = lax.broadcasted_iota(jnp.int32, (pairs, total_images), 0)
    own_ids = (here * split + me) * own_count + lax.div(pair_ids, per_image)
    hits = jnp.concatenate([ids == own_ids, ids == partner_ref[:, :1]], axis=0)
    table = lax.dot_general(
        jnp.concatenate([own_grad, far_grad], axis=0),
        hits.astype(jnp.float32),
        (((0,), (0,)), ((), ())),
        precision=lax.Precision.HIGHEST,
        preferred_element_type=jnp.float32,
    )
    for part in range(YS):
        dense[part] = table[:16, part * 128 : (part + 1) * 128]

    def plane_copy(number, dx, dy, slot):
        return remote(
            dense.at[lax.rem(y + dy, YS)],
            plane_in.at[slot],
            plane_send.at[number],
            plane_recv.at[number],
            plane_peer(dx, dy, 1),
        )

    for number, (dx, dy) in enumerate(plane):
        plane_copy(number, dx, dy, me * YS + y).start()
    plane_in[me * YS + y] = dense[y]

    old = jnp.concatenate(
        [depth[image * per_image : image * per_image + 1] for image in range(own_count)], axis=0
    )
    change = jnp.concatenate(
        [
            jnp.sum(
                depth_grad[image * per_image : (image + 1) * per_image], axis=0, keepdims=True
            )
            for image in range(own_count)
        ],
        axis=0,
    )
    moved = old - depth_step * change
    for place in range(split):
        span = slice(place * share, (place + 1) * share)
        for component, values_now in enumerate(points + [confidence]):
            staging[place, component * pairs : (component + 1) * pairs, :share] = values_now[:, span]
        staging[place, 4 * pairs : 4 * pairs + own_count, :share] = moved[:, span]

    def result_copy(step, slot):
        return remote(
            staging.at[lax.rem(me + step, split)],
            result_ref.at[slot],
            x_send.at[split + step],
            x_recv.at[split + step],
            mate(step),
        )

    for step in range(1, split):
        result_copy(step, me).start()
    result_ref[me] = staging[me]
    for number, (dx, dy) in enumerate(plane):
        source = lax.rem(me + split - dx, split) * YS + lax.rem(y + YS - dy, YS)
        plane_copy(number, dx, dy, source).wait_recv()
    gathered = jnp.sum(plane_in[...], axis=0)
    part_sum[...] = gathered
    line_in[row] = gathered

    def line_copy(number, dz, dc, slot):
        return remote(
            part_sum,
            line_in.at[slot],
            line_send.at[number],
            line_recv.at[number],
            (y * rows_count + line_row(dz, dc, 1), me),
        )

    for number, (dz, dc) in enumerate(line):
        line_copy(number, dz, dc, row).start()
    for number, (dz, dc) in enumerate(line):
        line_copy(number, dz, dc, line_row(dz, dc, -1)).wait_recv()
    total_ref[...] = jnp.sum(line_in[...], axis=0)
    for step in range(1, split):
        depth_copy(step, me).wait_send()
        result_copy(step, behind(step)).wait_recv()
        result_copy(step, me).wait_send()
    for number, (dx, dy) in enumerate(plane):
        plane_copy(number, dx, dy, me * YS + y).wait_send()
    for number, (dz, dc) in enumerate(line):
        line_copy(number, dz, dc, row).wait_send()


def decode(
    far, own, weights, head_rows, depth_tiles, pose_own, poses, partner_tile, partner_row, pairs
):
    width = own.shape[1]
    tokens = far.shape[0] // pairs
    own_count = own.shape[0] // tokens
    split = depth_tiles.shape[0]
    vmem = pl.BlockSpec(memory_space=pltpu.VMEM)
    result_rows = 4 * pairs + 8
    return pl.pallas_call(
        decode_kernel,
        out_shape=(
            jax.ShapeDtypeStruct((split, result_rows, 128), jnp.float32),
            jax.ShapeDtypeStruct((16, 128), jnp.float32),
        ),
        in_specs=[vmem] * 9,
        out_specs=(vmem, vmem),
        scratch_shapes=[
            pltpu.VMEM((own_count, width // 128, 2 * tokens, 128), jnp.bfloat16),
            pltpu.VMEM(far.shape, jnp.bfloat16),
            pltpu.VMEM(far.shape, jnp.bfloat16),
            pltpu.VMEM(far.shape, jnp.bfloat16),
            pltpu.VMEM((pairs, head_rows.shape[0], tokens), jnp.float32),
            pltpu.VMEM(depth_tiles.shape, jnp.float32),
            pltpu.VMEM((split, result_rows, 128), jnp.float32),
            pltpu.VMEM((YS, 16, 128), jnp.float32),
            pltpu.VMEM((split * YS, 16, 128), jnp.float32),
            pltpu.VMEM((16, 128), jnp.float32),
            pltpu.VMEM((2 * ZS, 16, 128), jnp.float32),
            pltpu.SemaphoreType.DMA((2 * split,)),
            pltpu.SemaphoreType.DMA((2 * split,)),
            pltpu.SemaphoreType.DMA((split * YS,)),
            pltpu.SemaphoreType.DMA((split * YS,)),
            pltpu.SemaphoreType.DMA((2 * ZS,)),
            pltpu.SemaphoreType.DMA((2 * ZS,)),
        ],
        compiler_params=pltpu.CompilerParams(
            collective_id=1, has_side_effects=True, vmem_limit_bytes=48 * 2**20
        ),
        name="decode",
    )(far, own, weights, head_rows, depth_tiles, pose_own, poses, partner_tile, partner_row)


def shards(
    patches,
    encoder_proj,
    encoder_out,
    decoder_embed,
    decoder_proj,
    decoder_out,
    head_weight,
    partners,
    depths,
    camera_poses,
    valid_mask,
):
    images, tokens, model_width = patches.shape
    dec_width = decoder_embed.shape[1]
    enc_local = encoder_proj.shape[2]
    split = lax.axis_size("mp")
    place = lax.axis_index("mp")
    own_count = images // split
    flat_partner = partners.reshape(-1)
    pair_count = flat_partner.shape[0]
    groups = lax.axis_size("img")
    here = lax.axis_index("img")
    weights = jnp.concatenate([jnp.transpose(decoder_proj, (1, 2, 0)), decoder_out[None]], axis=0)
    pose_tile = jnp.pad(
        camera_poses.astype(jnp.bfloat16), ((0, 4), (0, 128 - camera_poses.shape[1]))
    )

    token_share = tokens // split
    first_token = place * token_share
    patch_own = lax.dynamic_slice_in_dim(patches, first_token, token_share, 1)
    owner = flat_partner // images
    shift_y = (here // (2 * ZS) - owner // (2 * ZS)) % YS
    shift_z = ((here // 2) % ZS - (owner // 2) % ZS) % ZS
    shift_core = (here - owner) % 2
    pick = ((shift_core * YS + shift_y) * ZS + shift_z) * images + flat_partner % images
    far_rows, own_rows, weights_full, pose_tiles = exchange(
        pick,
        patches.reshape(images * tokens, model_width),
        patch_own,
        encoder_proj.reshape(model_width, 3 * enc_local),
        encoder_out,
        decoder_embed,
        weights,
        pose_tile,
        pair_count,
        groups,
        split,
    )
    head_rows = jnp.pad(head_weight.T, ((0, 12), (0, 0)))
    own_pairs = pair_count // split
    depth_mask = jnp.stack([depths, valid_mask.astype(jnp.float32)], axis=0)
    depth_tiles = depth_mask.reshape(2, split, own_count, token_share).transpose(1, 0, 2, 3)
    depth_tiles = jnp.pad(
        depth_tiles.reshape(split, 2 * own_count, token_share),
        ((0, 0), (0, 8 - 2 * own_count), (0, 128 - token_share)),
    )
    pose_own = lax.dynamic_slice_in_dim(camera_poses, place * own_count, own_count, 1)
    pose_own = jnp.pad(jnp.repeat(pose_own.T, K, axis=0), ((0, 0), (0, 116)))
    own_partner = lax.dynamic_slice_in_dim(flat_partner, place * own_pairs, own_pairs, 0)
    partner_tile = jnp.broadcast_to(own_partner[:, None], (own_pairs, 128))
    partner_row = jnp.broadcast_to(jnp.pad(own_partner, (0, 128 - own_pairs))[None], (8, 128))
    results, total = decode(
        far_rows.reshape(own_pairs * tokens, dec_width),
        own_rows.reshape(own_count * tokens, dec_width),
        weights_full.reshape(4, dec_width, dec_width),
        head_rows,
        depth_tiles,
        pose_own,
        pose_tiles,
        partner_tile,
        partner_row,
        own_pairs,
    )
    pointmap = results[:, : 4 * own_pairs, :token_share].reshape(split, 4, own_pairs, token_share)
    pointmap = pointmap.transpose(1, 0, 2, 3).reshape(4, pair_count, token_share)
    new_depths = results[:, 4 * own_pairs : 4 * own_pairs + own_count, :token_share]
    new_depths = new_depths.reshape(images, token_share)
    grad_pose = lax.dynamic_slice(total, (0, here % (2 * ZS) * images), (12, images))
    new_poses = camera_poses - pose_step * grad_pose
    return (pointmap, new_depths, new_poses)


def solution(mesh):
    placed = (
        P("img", None, None),
        P(None, None, "mp"),
        P("mp", None),
        P(),
        P(None, None, "mp"),
        P("mp", None),
        P(),
        P("img", None),
        P("img", "mp"),
        P(None, "img"),
        P("img", "mp"),
    )
    return jax.shard_map(
        shards,
        mesh=mesh,
        in_specs=placed,
        out_specs=(P(None, "img", "mp"), P("img", "mp"), P(None, "img")),
        check_vma=False,
    )
```

```python
import functools

import jax
import jax.numpy as jnp
from jax import lax
from jax.experimental import pallas as pl
from jax.experimental.pallas import tpu as pltpu
from jax.sharding import PartitionSpec as P

HD = 64
K = 8


epsilon = 1e-06
depth_step = 0.1
pose_step = 0.005


def norm_rows(values):
    average = jnp.mean(values, axis=-1, keepdims=True)
    centred = values - average
    variance = jnp.mean(centred * centred, axis=-1, keepdims=True)
    return (centred * lax.rsqrt(variance + epsilon)).astype(jnp.bfloat16)


YS, ZS, CORES = 4, 8, 2
FIRST = 5
WIDTHS = (384, 384)
RELAY = 18
AHEAD, DELAY = 4.0, 4.0
MESH = pl.DeviceIdType.MESH


def link_plan(images, spans):
    split = {"z": (0, FIRST), "y": (FIRST, images)}
    full = sum(spans)
    waiting = {"y+": [], "y-": [], "z+": [], "z-": []}
    free = {link: 0.0 for link in waiting}
    plan, flight, steps = [], [], []

    def push(now, chunk, link, source, target, span):
        waiting[link].append((chunk, len(waiting[link]) + 1000 * now, source, target, span))

    def issue(now):
        for link, queue in waiting.items():
            while queue and free[link] <= now + AHEAD:
                entry = min(queue)
                queue.remove(entry)
                chunk, _, source, target, span = entry
                free[link] = max(now, free[link]) + (span[1] - span[0]) * spans[chunk] / full
                flight.append((free[link] + DELAY, len(plan)))
                steps.append(("send", len(plan)))
                plan.append((chunk, link, source, target, span))

    def forward(now, chunk, dy, dz, span):
        if span[1] <= FIRST:
            low, high = split["z"]
            half = (low + high + 1) // 2
            if dy == 0:
                if dz in (0, 1, 2):
                    push(now, chunk, "z+", (dy, dz), (dy, dz + 1), span)
                if dz == 3:
                    push(now, chunk, "z+", (dy, dz), (dy, 4), (low, half))
                if dz in (0, 7, 6):
                    push(now, chunk, "z-", (dy, dz), (dy, (dz - 1) % ZS), span)
                if dz == 5:
                    push(now, chunk, "z-", (dy, dz), (dy, 4), (half, high))
                push(now, chunk, "y+", (dy, dz), (1, dz), span)
                push(now, chunk, "y-", (dy, dz), (3, dz), span)
            if dy == 1 and dz % 2 == 0:
                push(now, chunk, "y+", (dy, dz), (2, dz), span)
            if dy == 3 and dz % 2 == 1:
                push(now, chunk, "y-", (dy, dz), (2, dz), span)
        else:
            low, high = split["y"]
            half = (low + high + 1) // 2
            if dz == 0:
                if dy == 0:
                    push(now, chunk, "y+", (0, 0), (1, 0), span)
                    push(now, chunk, "y-", (0, 0), (3, 0), span)
                if dy == 1:
                    push(now, chunk, "y+", (1, 0), (2, 0), (low, half))
                if dy == 3:
                    push(now, chunk, "y-", (3, 0), (2, 0), (half, high))
            if dz in (0, 1, 2):
                push(now, chunk, "z+", (dy, dz), (dy, dz + 1), span)
            if dz == 3 and dy < 2:
                push(now, chunk, "z+", (dy, dz), (dy, 4), span)
            if dz in (0, 7, 6):
                push(now, chunk, "z-", (dy, dz), (dy, (dz - 1) % ZS), span)
            if dz == 5 and dy >= 2:
                push(now, chunk, "z-", (dy, dz), (dy, 4), span)

    for chunk in range(len(spans)):
        forward(0.0, chunk, 0, 0, split["z"])
        forward(0.0, chunk, 0, 0, split["y"])
    issue(0.0)
    while flight:
        entry = min(flight)
        flight.remove(entry)
        now, number = entry
        chunk, _, _, target, span = plan[number]
        steps.append(("wait", number))
        forward(now, chunk, target[0], target[1], span)
        issue(now)
    return steps, plan


def exchange_kernel(
    pick_ref,
    patches_ref,
    enc_proj_ref,
    enc_out_ref,
    embed_ref,
    weights_ref,
    pose_ref,
    far_ref,
    own_ref,
    weights_all,
    pose_all,
    *scratch,
):
    chunks = len(WIDTHS)
    held, scratch = scratch[:chunks], scratch[chunks:]
    staged, scratch = scratch[:chunks], scratch[chunks:]
    relay, scratch = scratch[:chunks], scratch[chunks:]
    (
        mixed,
        mixed_all,
        enc_out_all,
        emb_ref,
        enc_send,
        enc_recv,
        ring_send,
        ring_recv,
        twin_send,
        twin_recv,
        line_send,
        line_recv,
        pose_send,
        pose_recv,
        far_send,
        far_recv,
        local_sem,
    ) = scratch
    columns = [slice(sum(WIDTHS[:c]), sum(WIDTHS[: c + 1])) for c in range(chunks)]
    images, share, width = emb_ref.shape
    here = lax.axis_index("img")
    me = lax.axis_index("mp")
    core = lax.rem(here, 2)
    z = lax.rem(here // 2, ZS)
    y = here // (2 * ZS)
    split = far_ref.shape[1]
    per_dev = far_ref.shape[0]
    half_dev = per_dev // 2

    def spot(yy, zz, cc):
        return ((yy * ZS + zz) * 2 + cc, me)

    def mate(step):
        return (here, lax.rem(me + step, split))

    def behind(step):
        return lax.rem(me + split - step, split)

    twin = spot(y, z, 1 - core)
    links = {
        "y+": spot(lax.rem(y + 1, YS), z, core),
        "y-": spot(lax.rem(y + YS - 1, YS), z, core),
        "z+": spot(y, lax.rem(z + 1, ZS), core),
        "z-": spot(y, lax.rem(z + ZS - 1, ZS), core),
    }
    line = [(dz, dc) for dz in range(ZS) for dc in range(CORES) if dz or dc]

    def line_peer(dz, dc, sign):
        return spot(y, lax.rem(z + ZS + sign * dz, ZS), lax.rem(core + dc, 2))

    def y_peer(dy, sign):
        return spot(lax.rem(y + YS + sign * dy, YS), z, core)

    barrier = pltpu.get_barrier_semaphore()
    peers = [line_peer(dz, dc, 1) for dz, dc in line]
    peers += [y_peer(dy, 1) for dy in range(1, YS)]
    peers += [mate(step) for step in range(1, split)]
    for peer in peers:
        pl.semaphore_signal(barrier, inc=1, device_id=peer, device_id_type=MESH)
    pose_all[here] = pose_ref[...]
    pl.semaphore_wait(barrier, len(peers))

    def remote(source, target, send, recv, device):
        return pltpu.make_async_remote_copy(
            src_ref=source,
            dst_ref=target,
            send_sem=send,
            recv_sem=recv,
            device_id=device,
            device_id_type=MESH,
        )

    steps, plan = link_plan(images, WIDTHS)

    def block(chunk, side, slot, span):
        first = ((side * YS + slot[0]) * ZS + slot[1]) * images
        return held[chunk].at[pl.ds(first + span[0], span[1] - span[0])]

    def ring(number):
        chunk, link, source, target, span = plan[number]
        return remote(
            block(chunk, 0, source, span),
            block(chunk, 0, target, span),
            ring_send.at[number],
            ring_recv.at[number],
            links[link],
        )

    twins = [(entry[0], entry[3], entry[4]) for entry in plan]
    twins += [(chunk, (0, 0), (0, images)) for chunk in range(chunks)]

    def twin_copy(number):
        chunk, slot, span = twins[number]
        return remote(
            block(chunk, 0, slot, span),
            block(chunk, 1, slot, span),
            twin_send.at[number],
            twin_recv.at[number],
            twin,
        )

    def pose_line(dz, dc, number, slot):
        return remote(
            pose_all.at[slot],
            pose_all.at[slot],
            pose_send.at[number],
            pose_recv.at[number],
            line_peer(dz, dc, 1),
        )

    for number, (dz, dc) in enumerate(line):
        pose_line(dz, dc, number, here).start()

    pair_images = images // split

    def own_copy(step, slot):
        return remote(
            emb_ref.at[pl.ds(pair_images * lax.rem(me + step, split), pair_images)],
            own_ref.at[:, slot],
            line_send.at[step],
            line_recv.at[step],
            mate(step),
        )

    def weight_copy(step, slot):
        return remote(
            weights_ref.at[pl.ds(2 * core, 2)],
            weights_all.at[pl.ds(2 * core, 2), slot],
            line_send.at[split + step],
            line_recv.at[split + step],
            mate(step),
        )

    def weight_relay(step, slot):
        kind = 2 * core + (0 if step == 1 else 1)
        return remote(
            weights_all.at[pl.ds(kind, 1), slot],
            weights_all.at[pl.ds(kind, 1), slot],
            line_send.at[3 * split + step],
            line_recv.at[3 * split + step],
            mate(step),
        )

    def weight_twin(step, half, slot):
        return remote(
            weights_all.at[pl.ds(2 * half, 2), slot],
            weights_all.at[pl.ds(2 * half, 2), slot],
            line_send.at[2 * split + step],
            line_recv.at[2 * split + step],
            twin,
        )

    def far_direct(chunk, step, slot):
        return remote(
            staged[chunk].at[pl.ds(per_dev * lax.rem(me + step, split), per_dev)],
            far_ref.at[:, slot, :, columns[chunk]],
            far_send.at[chunk, step],
            far_recv.at[chunk, step],
            mate(step),
        )

    def far_relay(chunk, step):
        side = 0 if step == 1 else 1
        return remote(
            staged[chunk].at[pl.ds(per_dev * lax.rem(me + 2, split) + side * half_dev, half_dev)],
            relay[chunk].at[side],
            far_send.at[chunk, split + step],
            far_recv.at[chunk, split + step],
            mate(step),
        )

    def far_onward(chunk, step, slot):
        side = 0 if step == 1 else 1
        return remote(
            relay[chunk].at[side],
            far_ref.at[pl.ds(side * half_dev, half_dev), slot, :, columns[chunk]],
            far_send.at[chunk, 2 * split + step],
            far_recv.at[chunk, 2 * split + step],
            mate(step),
        )

    def out_copy(step, slot):
        return remote(
            enc_out_ref.at[pl.ds(2 * core, 2)],
            enc_out_all.at[slot, pl.ds(2 * core, 2)],
            enc_send.at[step],
            enc_recv.at[step],
            mate(step),
        )

    def out_relay(step, slot):
        part = pl.ds(2 * core + (0 if step == 1 else 1), 1)
        return remote(
            enc_out_all.at[slot, part],
            enc_out_all.at[slot, part],
            enc_send.at[3 * split + step],
            enc_recv.at[3 * split + step],
            mate(step),
        )

    def out_twin(step, half, slot):
        return remote(
            enc_out_all.at[slot, pl.ds(2 * half, 2)],
            enc_out_all.at[slot, pl.ds(2 * half, 2)],
            enc_send.at[4 * split + step],
            enc_recv.at[4 * split + step],
            twin,
        )

    def mixed_copy(part, step, slot):
        span = pl.ds(part * (images // 2), images // 2)
        return remote(
            mixed.at[lax.rem(me + step, split), span],
            mixed_all.at[slot, span],
            enc_send.at[split * (1 + part) + step],
            enc_recv.at[split * (1 + part) + step],
            mate(step),
        )

    for step in (1, 3):
        out_copy(step, me).start()
    enc_out_all[me] = enc_out_ref[...]
    tokens = share * split
    local = enc_out_ref.shape[0] * enc_out_ref.shape[1]
    last = (((1,), (1,)), ((), ()))
    first_half = lax.broadcasted_iota(jnp.int32, (1, 128), 1) < HD
    zero = jnp.zeros((), jnp.bfloat16)
    ones = jnp.ones((tokens, 128), jnp.bfloat16)

    def encode(pair, carry):
        picture = patches_ref[pl.ds(2 * pair, 2)].astype(jnp.float32)
        normed = norm_rows(picture.reshape(2 * tokens, -1))
        projected = [
            jnp.dot(normed, enc_proj_ref[kind], preferred_element_type=jnp.float32).astype(
                jnp.bfloat16
            )
            for kind in range(3)
        ]
        places = [(image, first) for image in range(2) for first in range(0, local, 128)]

        def take(kind, image, first):
            lines = slice(image * tokens, (image + 1) * tokens)
            return projected[kind][lines, first : first + 128]

        scores = []
        for image, first in places:
            query = take(0, image, first) * jnp.bfloat16(HD ** (-0.5))
            both = jnp.concatenate(
                [jnp.where(first_half, query, zero), jnp.where(first_half, zero, query)], axis=0
            )
            scores.append(
                lax.dot_general(
                    both, take(1, image, first), last, preferred_element_type=jnp.float32
                )
            )
        expos = [
            jnp.exp(each - jnp.max(each, axis=1, keepdims=True)).astype(jnp.bfloat16)
            for each in scores
        ]
        sums = [
            jnp.dot(
                each,
                jnp.concatenate([take(2, image, first), ones], axis=1),
                preferred_element_type=jnp.float32,
            )
            for each, (image, first) in zip(expos, places)
        ]
        for each, (image, first) in zip(sums, places):
            got = each[:, :128] / each[:, 128:]
            got = jnp.where(first_half, got[:tokens], got[tokens:])
            for place in range(split):
                mixed[place, pair * 2 + image, :, first : first + 128] = got[
                    place * share : (place + 1) * share
                ].astype(jnp.bfloat16)
        return carry

    lax.fori_loop(0, images // 4, encode, 0)
    for step in range(1, split):
        mixed_copy(0, step, me).start()
    for step in (1, 3):
        out_copy(step, behind(step)).wait_recv()
        out_relay(step, behind(step)).start()
        out_twin(step, core, behind(step)).start()
    lax.fori_loop(images // 4, images // 2, encode, 0)
    for step in range(1, split):
        mixed_copy(1, step, me).start()
    for step in (1, 3):
        out_relay(step, behind(2)).wait_recv()
    out_twin(2, core, behind(2)).start()
    for step in (1, 3):
        weight_copy(step, me).start()
    mixed_all[me] = mixed[me]
    encoded = patches_ref[:, me].astype(jnp.float32).reshape(images * share, -1)
    for step in range(split):
        source = behind(step)
        if step:
            out_twin(step, 1 - core, source).wait_recv()
            mixed_copy(0, step, source).wait_recv()
            mixed_copy(1, step, source).wait_recv()
        part = mixed_all[source].astype(jnp.float32).reshape(images * share, local)
        encoded = encoded + jnp.dot(
            part.astype(jnp.bfloat16), enc_out_all[source].reshape(local, -1), preferred_element_type=jnp.float32
        )
    embedded = jnp.dot(norm_rows(encoded), embed_ref[...], preferred_element_type=jnp.float32)
    embedded = embedded.astype(jnp.bfloat16).astype(jnp.float32)
    emb_ref[...] = embedded.reshape(images, share, width).astype(jnp.bfloat16)
    normed_rows = norm_rows(embedded).astype(jnp.float32).reshape(images, share, width)
    for chunk in range(chunks):
        held[chunk][pl.ds(0, images)] = normed_rows[:, :, columns[chunk]].astype(jnp.bfloat16)
    opening = [kind for kind, _ in steps].index("wait")
    for _, number in steps[:opening]:
        ring(number).start()
    for chunk in range(chunks):
        twin_copy(len(plan) + chunk).start()

    for step in range(1, split):
        own_copy(step, me).start()
    own_local = pltpu.make_async_copy(
        emb_ref.at[pl.ds(pair_images * me, pair_images)], own_ref.at[:, me], local_sem.at[0]
    )
    own_local.start()
    weight_local = pltpu.make_async_copy(weights_ref, weights_all.at[:, me], local_sem.at[1])
    weight_local.start()

    def far_local(chunk):
        return pltpu.make_async_copy(
            staged[chunk].at[pl.ds(per_dev * me, per_dev)],
            far_ref.at[:, me, :, columns[chunk]],
            local_sem.at[2 + chunk],
        )

    def choose(chunk):
        for number, entry in enumerate(twins):
            if entry[0] == chunk:
                twin_copy(number).wait_recv()

        def pick(index, carry):
            staged[chunk][index] = held[chunk][pick_ref[index]]
            return carry

        lax.fori_loop(0, per_dev * split, pick, 0, unroll=4)
        for step in (1, 3):
            far_relay(chunk, step).start()
        for step in (1, 3):
            far_direct(chunk, step, me).start()
        far_local(chunk).start()

    def pass_on(chunk):
        for step in (1, 3):
            far_relay(chunk, step).wait_recv()
            far_onward(chunk, step, behind(step)).start()

    def pose_cross(dy, row):
        return remote(
            pose_all.at[pl.ds(row * 2 * ZS, 2 * ZS)],
            pose_all.at[pl.ds(row * 2 * ZS, 2 * ZS)],
            pose_send.at[len(line) + dy - 1],
            pose_recv.at[len(line) + dy - 1],
            y_peer(dy, 1),
        )

    def pose_second():
        for number, (dz, dc) in enumerate(line):
            pose_line(dz, dc, number, line_peer(dz, dc, -1)[0]).wait_recv()
        for dy in range(1, YS):
            pose_cross(dy, y).start()

    def weights_second():
        for step in (1, 3):
            weight_copy(step, behind(step)).wait_recv()
            weight_relay(step, behind(step)).start()
            weight_twin(step, core, behind(step)).start()

    def weights_third():
        for step in (1, 3):
            weight_relay(step, behind(2)).wait_recv()
        weight_twin(2, core, behind(2)).start()

    waits = [number for kind, number in steps if kind == "wait"]
    final = {c: max(i for i, n in enumerate(waits) if plan[n][0] == c) for c in range(chunks)}
    events = {8: pose_second, len(waits) // 4: weights_second, len(waits) // 2: weights_third}
    later, pending, count = {}, [], 0
    for kind, number in steps[opening:]:
        if kind == "send":
            ring(number).start()
            continue
        for action in pending:
            action()
        pending = []
        ring(number).wait_recv()
        twin_copy(number).start()
        count += 1
        if count in events:
            pending.append(events[count])
        for chunk in range(chunks):
            if final[chunk] == count - 1:
                pending.append(functools.partial(choose, chunk))
                later[count + RELAY] = chunk
        if count in later:
            pending.append(functools.partial(pass_on, later.pop(count)))
    for action in pending:
        action()
    for chunk in later.values():
        pass_on(chunk)
    for dy in range(1, YS):
        pose_cross(dy, lax.rem(y + YS - dy, YS)).wait_recv()
    for step in range(1, split):
        own_copy(step, behind(step)).wait_recv()
        weight_twin(step, 1 - core, behind(step)).wait_recv()
    own_local.wait()
    weight_local.wait()
    for number in range(len(plan)):
        ring(number).wait_send()
    for number in range(len(twins)):
        twin_copy(number).wait_send()
    for number, (dz, dc) in enumerate(line):
        pose_line(dz, dc, number, here).wait_send()
    for dy in range(1, YS):
        pose_cross(dy, y).wait_send()
    for step in range(1, split):
        out_twin(step, core, behind(step)).wait_send()
        mixed_copy(0, step, me).wait_send()
        mixed_copy(1, step, me).wait_send()
        own_copy(step, me).wait_send()
        weight_twin(step, core, behind(step)).wait_send()
    for step in (1, 3):
        out_copy(step, me).wait_send()
        out_relay(step, behind(step)).wait_send()
        weight_copy(step, me).wait_send()
        weight_relay(step, behind(step)).wait_send()
    for chunk in range(chunks):
        far_local(chunk).wait()
        for step in (1, 3):
            far_relay(chunk, step).wait_send()
            far_direct(chunk, step, behind(step)).wait_recv()
            far_direct(chunk, step, me).wait_send()
            far_onward(chunk, step, behind(2)).wait_recv()
            far_onward(chunk, step, behind(step)).wait_send()


def exchange(pick, patches, enc_proj, enc_out, embed, weights, pose, pairs, groups, split):
    images, _, share, _ = patches.shape
    local = enc_out.shape[0] * enc_out.shape[1]
    width = embed.shape[1]
    chunks = len(WIDTHS)
    count = len(link_plan(images, WIDTHS)[1])
    vmem = pl.BlockSpec(memory_space=pltpu.VMEM)
    per_dev = pairs // split
    return pl.pallas_call(
        exchange_kernel,
        out_shape=(
            jax.ShapeDtypeStruct((per_dev, split, share, width), jnp.bfloat16),
            jax.ShapeDtypeStruct((images // split, split, share, width), jnp.bfloat16),
            jax.ShapeDtypeStruct((4, split) + weights.shape[1:], jnp.bfloat16),
            jax.ShapeDtypeStruct((groups,) + pose.shape, jnp.bfloat16),
        ),
        in_specs=[pl.BlockSpec(memory_space=pltpu.SMEM)] + [vmem] * 6,
        out_specs=(vmem,) * 4,
        scratch_shapes=[pltpu.VMEM((groups * images, share, w), jnp.bfloat16) for w in WIDTHS]
        + [pltpu.VMEM((pairs, share, w), jnp.bfloat16) for w in WIDTHS]
        + [pltpu.VMEM((2, per_dev // 2, share, w), jnp.bfloat16) for w in WIDTHS]
        + [
            pltpu.VMEM((split, images, share, local), jnp.bfloat16),
            pltpu.VMEM((split, images, share, local), jnp.bfloat16),
            pltpu.VMEM((split,) + enc_out.shape, jnp.bfloat16),
            pltpu.VMEM((images, share, width), jnp.bfloat16),
            pltpu.SemaphoreType.DMA((5 * split,)),
            pltpu.SemaphoreType.DMA((5 * split,)),
            pltpu.SemaphoreType.DMA((count,)),
            pltpu.SemaphoreType.DMA((count,)),
            pltpu.SemaphoreType.DMA((count + chunks,)),
            pltpu.SemaphoreType.DMA((count + chunks,)),
            pltpu.SemaphoreType.DMA((4 * split,)),
            pltpu.SemaphoreType.DMA((4 * split,)),
            pltpu.SemaphoreType.DMA((2 * ZS + YS,)),
            pltpu.SemaphoreType.DMA((2 * ZS + YS,)),
            pltpu.SemaphoreType.DMA((chunks, 3 * split)),
            pltpu.SemaphoreType.DMA((chunks, 3 * split)),
            pltpu.SemaphoreType.DMA((2 + chunks,)),
        ],
        compiler_params=pltpu.CompilerParams(
            collective_id=0, has_side_effects=True, vmem_limit_bytes=56 * 2**20
        ),
        name="exchange",
    )(pick, patches, enc_proj, enc_out, embed, weights, pose)


def decode_kernel(
    far_ref,
    own_ref,
    weights_ref,
    head_ref,
    depth_ref,
    pose_own_ref,
    pose_all_ref,
    partner_ref,
    partner_row_ref,
    result_ref,
    total_ref,
    queries,
    keys,
    values,
    mixed,
    heads_all,
    depth_all,
    staging,
    dense,
    plane_in,
    part_sum,
    line_in,
    x_send,
    x_recv,
    plane_send,
    plane_recv,
    line_send,
    line_recv,
):
    width = own_ref.shape[1]
    pairs, _, tokens = heads_all.shape
    split = depth_all.shape[0]
    share = tokens // split
    here = lax.axis_index("img")
    me = lax.axis_index("mp")
    rows_count = 2 * ZS
    row = lax.rem(here, rows_count)
    y = here // rows_count
    plane = [(dx, dy) for dx in range(split) for dy in range(YS) if dx or dy]
    line = [(dz, dc) for dz in range(ZS) for dc in range(CORES) if dz or dc]

    def plane_peer(dx, dy, sign):
        return (
            lax.rem(y + YS + sign * dy, YS) * rows_count + row,
            lax.rem(me + split + sign * dx, split),
        )

    def line_row(dz, dc, sign):
        z = lax.rem(row // 2 + ZS + sign * dz, ZS)
        return z * 2 + lax.rem(lax.rem(row, 2) + dc, 2)

    def mate(step):
        return (here, lax.rem(me + step, split))

    def behind(step):
        return lax.rem(me + split - step, split)

    def remote(source, target, send, recv, device):
        return pltpu.make_async_remote_copy(
            src_ref=source,
            dst_ref=target,
            send_sem=send,
            recv_sem=recv,
            device_id=device,
            device_id_type=MESH,
        )

    barrier = pltpu.get_barrier_semaphore()
    for dx, dy in plane:
        pl.semaphore_signal(
            barrier, inc=1, device_id=plane_peer(dx, dy, 1), device_id_type=MESH
        )
    for dz, dc in line:
        pl.semaphore_signal(
            barrier, inc=1, device_id=(y * rows_count + line_row(dz, dc, 1), me), device_id_type=MESH
        )
    blocks = width // 128
    own_count = own_ref.shape[0] // tokens
    per_image = pairs // own_count
    last = (((1,), (1,)), ((), ()))
    lane = lax.broadcasted_iota(jnp.int32, (1, 128), 1)
    first_half = lane < HD

    rows = norm_rows(own_ref[...].astype(jnp.float32))
    projected = lax.dot_general(rows, weights_ref[0], last, preferred_element_type=jnp.float32)
    projected = projected.astype(jnp.bfloat16) * jnp.bfloat16(HD ** (-0.5))
    zero = jnp.zeros((), jnp.bfloat16)
    for image in range(own_count):
        for block in range(blocks):
            part = projected[image * tokens : (image + 1) * tokens, block * 128 : (block + 1) * 128]
            queries[image, block, :tokens] = jnp.where(first_half, part, zero)
            queries[image, block, tokens:] = jnp.where(first_half, zero, part)

    chunk = 4 * tokens

    def project(step, carry):
        span = pl.ds(pl.multiple_of(step * chunk, chunk), chunk)
        part = far_ref[span, :]
        keys[span, :] = lax.dot_general(
            part, weights_ref[1], last, preferred_element_type=jnp.float32
        ).astype(jnp.bfloat16)
        values[span, :] = lax.dot_general(
            part, weights_ref[2], last, preferred_element_type=jnp.float32
        ).astype(jnp.bfloat16)
        return carry

    lax.fori_loop(0, pairs // 4, project, 0, unroll=2)
    pl.semaphore_wait(barrier, len(plane) + len(line))

    def depth_copy(step, slot):
        return remote(
            depth_ref.at[lax.rem(me + step, split)],
            depth_all.at[slot],
            x_send.at[step],
            x_recv.at[step],
            mate(step),
        )

    for step in range(1, split):
        depth_copy(step, me).start()
    depth_all[me] = depth_ref[me]
    staging[...] = jnp.zeros_like(staging)
    members = own_count * split
    group_count, pose_rows, _ = pose_all_ref.shape
    lane_ids = lax.broadcasted_iota(jnp.int32, (pairs, 128), 1)
    chosen = (lane_ids == lax.rem(partner_ref[...], members)).astype(jnp.bfloat16)
    candidates = lax.dot_general(
        pose_all_ref[...].reshape(group_count * pose_rows, 128),
        chosen,
        last,
        preferred_element_type=jnp.float32,
    ).reshape(group_count, pose_rows, pairs)
    owners = lax.broadcasted_iota(jnp.int32, (group_count, pose_rows, pairs), 0)
    held_by = lax.div(partner_row_ref[:1, :pairs], members)
    turned = jnp.sum(jnp.where(owners == held_by[None], candidates, 0.0), axis=0)
    same = lax.broadcasted_iota(jnp.int32, (pose_rows, pose_rows), 0) == lax.broadcasted_iota(
        jnp.int32, (pose_rows, pose_rows), 1
    )
    far_pose = lax.dot_general(
        turned.astype(jnp.bfloat16),
        same.astype(jnp.bfloat16),
        (((0,), (0,)), ((), ())),
        preferred_element_type=jnp.float32,
    )
    ones = jnp.ones((tokens, 128), jnp.bfloat16)

    def attend(pair, carry):
        span = pl.ds(pl.multiple_of(pair * tokens, tokens), tokens)
        image = pair // per_image
        columns = [slice(block * 128, (block + 1) * 128) for block in range(blocks)]
        scores = [
            lax.dot_general(
                queries[image, block], keys[span, part], last, preferred_element_type=jnp.float32
            )
            for block, part in enumerate(columns)
        ]
        expos = [
            jnp.exp(each - jnp.max(each, axis=1, keepdims=True)).astype(jnp.bfloat16)
            for each in scores
        ]
        sums = [
            jnp.dot(
                each,
                jnp.concatenate([values[span, part], ones], axis=1),
                preferred_element_type=jnp.float32,
            )
            for each, part in zip(expos, columns)
        ]
        for each, part in zip(sums, columns):
            got = each[:, :128] / each[:, 128:]
            mixed[span, part] = jnp.where(first_half, got[:tokens], got[tokens:]).astype(
                jnp.bfloat16
            )
        return carry

    lax.fori_loop(0, pairs, attend, 0, unroll=2)

    def finish(step, carry):
        span = pl.ds(pl.multiple_of(step * chunk, chunk), chunk)
        image = step * 4 // per_image
        own = own_ref[pl.ds(pl.multiple_of(image * tokens, tokens), tokens), :].astype(jnp.float32)
        settled = jnp.dot(mixed[span, :], weights_ref[3], preferred_element_type=jnp.float32)
        settled = settled + jnp.concatenate([own] * 4, axis=0)
        heads = lax.dot_general(
            head_ref[...], norm_rows(settled), last, preferred_element_type=jnp.float32
        )
        for part in range(4):
            heads_all[step * 4 + part] = heads[:, part * tokens : (part + 1) * tokens]
        return carry

    lax.fori_loop(0, pairs // 4, finish, 0, unroll=2)
    for step in range(1, split):
        depth_copy(step, behind(step)).wait_recv()

    def widen(offset):
        both = jnp.concatenate(
            [depth_all[q, offset : offset + own_count, :share] for q in range(split)], axis=1
        )
        return jnp.concatenate(
            [
                jnp.broadcast_to(both[image : image + 1], (per_image, tokens))
                for image in range(own_count)
            ],
            axis=0,
        )

    depth = widen(0)
    valid = widen(own_count)
    token = lax.broadcasted_iota(jnp.int32, (1, tokens), 1)
    ray_x = (lax.rem(token, 16).astype(jnp.float32) - 7.5) * 0.125
    ray_y = (lax.div(token, 16).astype(jnp.float32) - (tokens // 16 - 1) * 0.5) * 0.125
    rays = [ray_x, ray_y, jnp.ones_like(ray_x)]
    points = [heads_all[:, component, :] for component in range(3)]
    confidence = 1.0 + jnp.exp(heads_all[:, 3, :])
    weight = valid * confidence * (2.0 / tokens)
    own_pose = pose_own_ref[...]
    lane128 = lax.broadcasted_iota(jnp.int32, (pairs, 128), 1)
    own_grad = jnp.zeros((pairs, 128), jnp.float32)
    far_grad = jnp.zeros((pairs, 128), jnp.float32)
    depth_grad = jnp.zeros((pairs, tokens), jnp.float32)
    for component in range(3):
        base = 4 * component
        direction = sum(own_pose[:, base + k : base + k + 1] * rays[k] for k in range(3))
        world = own_pose[:, base + 3 : base + 4] + depth * direction
        predicted = far_pose[:, base + 3 : base + 4] + sum(
            far_pose[:, base + k : base + k + 1] * points[k] for k in range(3)
        )
        slope = weight * (world - predicted)
        depth_grad = depth_grad + slope * direction
        scaled = slope * depth
        for k in range(4):
            mine = scaled * rays[k] if k < 3 else slope
            other = slope * points[k] if k < 3 else slope
            mine = jnp.sum(mine, axis=1, keepdims=True)
            other = jnp.sum(other, axis=1, keepdims=True)
            own_grad = jnp.where(lane128 == base + k, mine, own_grad)
            far_grad = jnp.where(lane128 == base + k, -other, far_grad)
    total_images = YS * 128
    ids = lax.broadcasted_iota(jnp.int32, (pairs, total_images), 1)
    pair_ids = lax.broadcasted_iota(jnp.int32, (pairs, total_images), 0)
    own_ids = (here * split + me) * own_count + lax.div(pair_ids, per_image)
    hits = jnp.concatenate([ids == own_ids, ids == partner_ref[:, :1]], axis=0)
    table = lax.dot_general(
        jnp.concatenate([own_grad, far_grad], axis=0),
        hits.astype(jnp.float32),
        (((0,), (0,)), ((), ())),
        precision=lax.Precision.HIGHEST,
        preferred_element_type=jnp.float32,
    )
    for part in range(YS):
        dense[part] = table[:16, part * 128 : (part + 1) * 128]

    def plane_copy(number, dx, dy, slot):
        return remote(
            dense.at[lax.rem(y + dy, YS)],
            plane_in.at[slot],
            plane_send.at[number],
            plane_recv.at[number],
            plane_peer(dx, dy, 1),
        )

    for number, (dx, dy) in enumerate(plane):
        plane_copy(number, dx, dy, me * YS + y).start()
    plane_in[me * YS + y] = dense[y]

    old = jnp.concatenate(
        [depth[image * per_image : image * per_image + 1] for image in range(own_count)], axis=0
    )
    change = jnp.concatenate(
        [
            jnp.sum(
                depth_grad[image * per_image : (image + 1) * per_image], axis=0, keepdims=True
            )
            for image in range(own_count)
        ],
        axis=0,
    )
    moved = old - depth_step * change
    for place in range(split):
        span = slice(place * share, (place + 1) * share)
        for component, values_now in enumerate(points + [confidence]):
            staging[place, component * pairs : (component + 1) * pairs, :share] = values_now[:, span]
        staging[place, 4 * pairs : 4 * pairs + own_count, :share] = moved[:, span]

    def result_copy(step, slot):
        return remote(
            staging.at[lax.rem(me + step, split)],
            result_ref.at[slot],
            x_send.at[split + step],
            x_recv.at[split + step],
            mate(step),
        )

    for step in range(1, split):
        result_copy(step, me).start()
    result_ref[me] = staging[me]
    for number, (dx, dy) in enumerate(plane):
        source = lax.rem(me + split - dx, split) * YS + lax.rem(y + YS - dy, YS)
        plane_copy(number, dx, dy, source).wait_recv()
    gathered = jnp.sum(plane_in[...], axis=0)
    part_sum[...] = gathered
    line_in[row] = gathered

    def line_copy(number, dz, dc, slot):
        return remote(
            part_sum,
            line_in.at[slot],
            line_send.at[number],
            line_recv.at[number],
            (y * rows_count + line_row(dz, dc, 1), me),
        )

    for number, (dz, dc) in enumerate(line):
        line_copy(number, dz, dc, row).start()
    for number, (dz, dc) in enumerate(line):
        line_copy(number, dz, dc, line_row(dz, dc, -1)).wait_recv()
    total_ref[...] = jnp.sum(line_in[...], axis=0)
    for step in range(1, split):
        depth_copy(step, me).wait_send()
        result_copy(step, behind(step)).wait_recv()
        result_copy(step, me).wait_send()
    for number, (dx, dy) in enumerate(plane):
        plane_copy(number, dx, dy, me * YS + y).wait_send()
    for number, (dz, dc) in enumerate(line):
        line_copy(number, dz, dc, row).wait_send()


def decode(
    far, own, weights, head_rows, depth_tiles, pose_own, poses, partner_tile, partner_row, pairs
):
    width = own.shape[1]
    tokens = far.shape[0] // pairs
    own_count = own.shape[0] // tokens
    split = depth_tiles.shape[0]
    vmem = pl.BlockSpec(memory_space=pltpu.VMEM)
    result_rows = 4 * pairs + 8
    return pl.pallas_call(
        decode_kernel,
        out_shape=(
            jax.ShapeDtypeStruct((split, result_rows, 128), jnp.float32),
            jax.ShapeDtypeStruct((16, 128), jnp.float32),
        ),
        in_specs=[vmem] * 9,
        out_specs=(vmem, vmem),
        scratch_shapes=[
            pltpu.VMEM((own_count, width // 128, 2 * tokens, 128), jnp.bfloat16),
            pltpu.VMEM(far.shape, jnp.bfloat16),
            pltpu.VMEM(far.shape, jnp.bfloat16),
            pltpu.VMEM(far.shape, jnp.bfloat16),
            pltpu.VMEM((pairs, head_rows.shape[0], tokens), jnp.float32),
            pltpu.VMEM(depth_tiles.shape, jnp.float32),
            pltpu.VMEM((split, result_rows, 128), jnp.float32),
            pltpu.VMEM((YS, 16, 128), jnp.float32),
            pltpu.VMEM((split * YS, 16, 128), jnp.float32),
            pltpu.VMEM((16, 128), jnp.float32),
            pltpu.VMEM((2 * ZS, 16, 128), jnp.float32),
            pltpu.SemaphoreType.DMA((2 * split,)),
            pltpu.SemaphoreType.DMA((2 * split,)),
            pltpu.SemaphoreType.DMA((split * YS,)),
            pltpu.SemaphoreType.DMA((split * YS,)),
            pltpu.SemaphoreType.DMA((2 * ZS,)),
            pltpu.SemaphoreType.DMA((2 * ZS,)),
        ],
        compiler_params=pltpu.CompilerParams(
            collective_id=1, has_side_effects=True, vmem_limit_bytes=48 * 2**20
        ),
        name="decode",
    )(far, own, weights, head_rows, depth_tiles, pose_own, poses, partner_tile, partner_row)


def shards(
    patches,
    encoder_proj,
    encoder_out,
    decoder_embed,
    decoder_proj,
    decoder_out,
    head_weight,
    partners,
    depths,
    camera_poses,
    valid_mask,
):
    images, tokens, model_width = patches.shape
    dec_width = decoder_embed.shape[1]
    enc_local = encoder_proj.shape[2]
    split = lax.axis_size("mp")
    place = lax.axis_index("mp")
    own_count = images // split
    flat_partner = partners.reshape(-1)
    pair_count = flat_partner.shape[0]
    groups = lax.axis_size("img")
    here = lax.axis_index("img")
    weights = jnp.concatenate([jnp.transpose(decoder_proj, (1, 2, 0)), decoder_out[None]], axis=0)
    pose_tile = jnp.pad(
        camera_poses.astype(jnp.bfloat16), ((0, 4), (0, 128 - camera_poses.shape[1]))
    )

    token_share = tokens // split
    owner = flat_partner // images
    shift_y = (here // (2 * ZS) - owner // (2 * ZS)) % YS
    shift_z = ((here // 2) % ZS - (owner // 2) % ZS) % ZS
    shift_core = (here - owner) % 2
    pick = ((shift_core * YS + shift_y) * ZS + shift_z) * images + flat_partner % images
    far_rows, own_rows, weights_full, pose_tiles = exchange(
        pick,
        patches.reshape(images, split, token_share, model_width),
        jnp.transpose(encoder_proj, (1, 0, 2)),
        encoder_out.reshape(4, enc_local // 4, model_width),
        decoder_embed,
        weights,
        pose_tile,
        pair_count,
        groups,
        split,
    )
    head_rows = jnp.pad(head_weight.T, ((0, 12), (0, 0)))
    own_pairs = pair_count // split
    depth_mask = jnp.stack([depths, valid_mask.astype(jnp.float32)], axis=0)
    depth_tiles = depth_mask.reshape(2, split, own_count, token_share).transpose(1, 0, 2, 3)
    depth_tiles = jnp.pad(
        depth_tiles.reshape(split, 2 * own_count, token_share),
        ((0, 0), (0, 8 - 2 * own_count), (0, 128 - token_share)),
    )
    pose_own = lax.dynamic_slice_in_dim(camera_poses, place * own_count, own_count, 1)
    pose_own = jnp.pad(jnp.repeat(pose_own.T, K, axis=0), ((0, 0), (0, 116)))
    own_partner = lax.dynamic_slice_in_dim(flat_partner, place * own_pairs, own_pairs, 0)
    partner_tile = jnp.broadcast_to(own_partner[:, None], (own_pairs, 128))
    partner_row = jnp.broadcast_to(jnp.pad(own_partner, (0, 128 - own_pairs))[None], (8, 128))
    results, total = decode(
        far_rows.reshape(own_pairs * tokens, dec_width),
        own_rows.reshape(own_count * tokens, dec_width),
        weights_full.reshape(4, dec_width, dec_width),
        head_rows,
        depth_tiles,
        pose_own,
        pose_tiles,
        partner_tile,
        partner_row,
        own_pairs,
    )
    pointmap = results[:, : 4 * own_pairs, :token_share].reshape(split, 4, own_pairs, token_share)
    pointmap = pointmap.transpose(1, 0, 2, 3).reshape(4, pair_count, token_share)
    new_depths = results[:, 4 * own_pairs : 4 * own_pairs + own_count, :token_share]
    new_depths = new_depths.reshape(images, token_share)
    grad_pose = lax.dynamic_slice(total, (0, here % (2 * ZS) * images), (12, images))
    new_poses = camera_poses - pose_step * grad_pose
    return (pointmap, new_depths, new_poses)


def solution(mesh):
    placed = (
        P("img", None, None),
        P(None, None, "mp"),
        P("mp", None),
        P(),
        P(None, None, "mp"),
        P("mp", None),
        P(),
        P("img", None),
        P("img", "mp"),
        P(None, "img"),
        P("img", "mp"),
    )
    return jax.shard_map(
        shards,
        mesh=mesh,
        in_specs=placed,
        out_specs=(P(None, "img", "mp"), P("img", "mp"), P(None, "img")),
        check_vma=False,
    )
```

```python
import functools

import jax
import jax.numpy as jnp
from jax import lax
from jax.experimental import pallas as pl
from jax.experimental.pallas import tpu as pltpu
from jax.sharding import PartitionSpec as P

HD = 64
K = 8


epsilon = 1e-06
depth_step = 0.1
pose_step = 0.005


def norm_rows(values):
    average = jnp.mean(values, axis=-1, keepdims=True)
    centred = values - average
    variance = jnp.mean(centred * centred, axis=-1, keepdims=True)
    return (centred * lax.rsqrt(variance + epsilon)).astype(jnp.bfloat16)


YS, ZS, CORES = 4, 8, 2
FIRST = 5
WIDTHS = (384, 384)
RELAY = 18
AHEAD, DELAY = 4.0, 4.0
MESH = pl.DeviceIdType.MESH


def link_plan(images, spans):
    split = {"z": (0, FIRST), "y": (FIRST, images)}
    full = sum(spans)
    waiting = {"y+": [], "y-": [], "z+": [], "z-": []}
    free = {link: 0.0 for link in waiting}
    plan, flight, steps = [], [], []

    def push(now, chunk, link, source, target, span):
        waiting[link].append((chunk, len(waiting[link]) + 1000 * now, source, target, span))

    def issue(now):
        for link, queue in waiting.items():
            while queue and free[link] <= now + AHEAD:
                entry = min(queue)
                queue.remove(entry)
                chunk, _, source, target, span = entry
                free[link] = max(now, free[link]) + (span[1] - span[0]) * spans[chunk] / full
                flight.append((free[link] + DELAY, len(plan)))
                steps.append(("send", len(plan)))
                plan.append((chunk, link, source, target, span))

    def forward(now, chunk, dy, dz, span):
        if span[1] <= FIRST:
            low, high = split["z"]
            half = (low + high + 1) // 2
            if dy == 0:
                if dz in (0, 1, 2):
                    push(now, chunk, "z+", (dy, dz), (dy, dz + 1), span)
                if dz == 3:
                    push(now, chunk, "z+", (dy, dz), (dy, 4), (low, half))
                if dz in (0, 7, 6):
                    push(now, chunk, "z-", (dy, dz), (dy, (dz - 1) % ZS), span)
                if dz == 5:
                    push(now, chunk, "z-", (dy, dz), (dy, 4), (half, high))
                push(now, chunk, "y+", (dy, dz), (1, dz), span)
                push(now, chunk, "y-", (dy, dz), (3, dz), span)
            if dy == 1 and dz % 2 == 0:
                push(now, chunk, "y+", (dy, dz), (2, dz), span)
            if dy == 3 and dz % 2 == 1:
                push(now, chunk, "y-", (dy, dz), (2, dz), span)
        else:
            low, high = split["y"]
            half = (low + high + 1) // 2
            if dz == 0:
                if dy == 0:
                    push(now, chunk, "y+", (0, 0), (1, 0), span)
                    push(now, chunk, "y-", (0, 0), (3, 0), span)
                if dy == 1:
                    push(now, chunk, "y+", (1, 0), (2, 0), (low, half))
                if dy == 3:
                    push(now, chunk, "y-", (3, 0), (2, 0), (half, high))
            if dz in (0, 1, 2):
                push(now, chunk, "z+", (dy, dz), (dy, dz + 1), span)
            if dz == 3 and dy < 2:
                push(now, chunk, "z+", (dy, dz), (dy, 4), span)
            if dz in (0, 7, 6):
                push(now, chunk, "z-", (dy, dz), (dy, (dz - 1) % ZS), span)
            if dz == 5 and dy >= 2:
                push(now, chunk, "z-", (dy, dz), (dy, 4), span)

    for chunk in range(len(spans)):
        forward(0.0, chunk, 0, 0, split["z"])
        forward(0.0, chunk, 0, 0, split["y"])
    issue(0.0)
    while flight:
        entry = min(flight)
        flight.remove(entry)
        now, number = entry
        chunk, _, _, target, span = plan[number]
        steps.append(("wait", number))
        forward(now, chunk, target[0], target[1], span)
        issue(now)
    return steps, plan


def exchange_kernel(
    pick_ref,
    patches_ref,
    enc_proj_ref,
    enc_out_ref,
    embed_ref,
    weights_ref,
    pose_ref,
    head_ref,
    depth_ref,
    pose_own_ref,
    partner_ref,
    partner_row_ref,
    result_ref,
    total_ref,
    far_ref,
    own_ref,
    weights_all,
    pose_all,
    *scratch,
):
    finish, scratch = scratch[:17], scratch[17:]
    chunks = len(WIDTHS)
    held, scratch = scratch[:chunks], scratch[chunks:]
    staged, scratch = scratch[:chunks], scratch[chunks:]
    relay, scratch = scratch[:chunks], scratch[chunks:]
    (
        mixed,
        mixed_all,
        enc_out_all,
        emb_ref,
        enc_send,
        enc_recv,
        ring_send,
        ring_recv,
        twin_send,
        twin_recv,
        line_send,
        line_recv,
        pose_send,
        pose_recv,
        far_send,
        far_recv,
        local_sem,
    ) = scratch
    columns = [slice(sum(WIDTHS[:c]), sum(WIDTHS[: c + 1])) for c in range(chunks)]
    images, share, width = emb_ref.shape
    here = lax.axis_index("img")
    me = lax.axis_index("mp")
    core = lax.rem(here, 2)
    z = lax.rem(here // 2, ZS)
    y = here // (2 * ZS)
    split = far_ref.shape[1]
    per_dev = far_ref.shape[0]
    half_dev = per_dev // 2

    def spot(yy, zz, cc):
        return ((yy * ZS + zz) * 2 + cc, me)

    def mate(step):
        return (here, lax.rem(me + step, split))

    def behind(step):
        return lax.rem(me + split - step, split)

    twin = spot(y, z, 1 - core)
    links = {
        "y+": spot(lax.rem(y + 1, YS), z, core),
        "y-": spot(lax.rem(y + YS - 1, YS), z, core),
        "z+": spot(y, lax.rem(z + 1, ZS), core),
        "z-": spot(y, lax.rem(z + ZS - 1, ZS), core),
    }
    line = [(dz, dc) for dz in range(ZS) for dc in range(CORES) if dz or dc]

    def line_peer(dz, dc, sign):
        return spot(y, lax.rem(z + ZS + sign * dz, ZS), lax.rem(core + dc, 2))

    def y_peer(dy, sign):
        return spot(lax.rem(y + YS + sign * dy, YS), z, core)

    barrier = pltpu.get_barrier_semaphore()
    peers = [line_peer(dz, dc, 1) for dz, dc in line]
    peers += [
        (spot(lax.rem(y + dy, YS), z, core)[0], lax.rem(me + dx, split))
        for dx in range(split)
        for dy in range(YS)
        if dx or dy
    ]
    for peer in peers:
        pl.semaphore_signal(barrier, inc=1, device_id=peer, device_id_type=MESH)
    pose_all[here] = pose_ref[...]
    pl.semaphore_wait(barrier, len(peers))

    def remote(source, target, send, recv, device):
        return pltpu.make_async_remote_copy(
            src_ref=source,
            dst_ref=target,
            send_sem=send,
            recv_sem=recv,
            device_id=device,
            device_id_type=MESH,
        )

    steps, plan = link_plan(images, WIDTHS)

    def block(chunk, side, slot, span):
        first = ((side * YS + slot[0]) * ZS + slot[1]) * images
        return held[chunk].at[pl.ds(first + span[0], span[1] - span[0])]

    def ring(number):
        chunk, link, source, target, span = plan[number]
        return remote(
            block(chunk, 0, source, span),
            block(chunk, 0, target, span),
            ring_send.at[number],
            ring_recv.at[number],
            links[link],
        )

    twins = [(entry[0], entry[3], entry[4]) for entry in plan]
    twins += [(chunk, (0, 0), (0, images)) for chunk in range(chunks)]

    def twin_copy(number):
        chunk, slot, span = twins[number]
        return remote(
            block(chunk, 0, slot, span),
            block(chunk, 1, slot, span),
            twin_send.at[number],
            twin_recv.at[number],
            twin,
        )

    def pose_line(dz, dc, number, slot):
        return remote(
            pose_all.at[slot],
            pose_all.at[slot],
            pose_send.at[number],
            pose_recv.at[number],
            line_peer(dz, dc, 1),
        )

    for number, (dz, dc) in enumerate(line):
        pose_line(dz, dc, number, here).start()

    pair_images = images // split

    def own_copy(step, slot):
        return remote(
            emb_ref.at[pl.ds(pair_images * lax.rem(me + step, split), pair_images)],
            own_ref.at[:, slot],
            line_send.at[step],
            line_recv.at[step],
            mate(step),
        )

    def weight_copy(step, slot):
        return remote(
            weights_ref.at[pl.ds(2 * core, 2)],
            weights_all.at[pl.ds(2 * core, 2), slot],
            line_send.at[split + step],
            line_recv.at[split + step],
            mate(step),
        )

    def weight_relay(step, slot):
        kind = 2 * core + (0 if step == 1 else 1)
        return remote(
            weights_all.at[pl.ds(kind, 1), slot],
            weights_all.at[pl.ds(kind, 1), slot],
            line_send.at[3 * split + step],
            line_recv.at[3 * split + step],
            mate(step),
        )

    def weight_twin(step, half, slot):
        return remote(
            weights_all.at[pl.ds(2 * half, 2), slot],
            weights_all.at[pl.ds(2 * half, 2), slot],
            line_send.at[2 * split + step],
            line_recv.at[2 * split + step],
            twin,
        )

    def far_direct(chunk, step, slot):
        return remote(
            staged[chunk].at[pl.ds(per_dev * lax.rem(me + step, split), per_dev)],
            far_ref.at[:, slot, :, columns[chunk]],
            far_send.at[chunk, step],
            far_recv.at[chunk, step],
            mate(step),
        )

    def far_relay(chunk, step):
        side = 0 if step == 1 else 1
        return remote(
            staged[chunk].at[pl.ds(per_dev * lax.rem(me + 2, split) + side * half_dev, half_dev)],
            relay[chunk].at[side],
            far_send.at[chunk, split + step],
            far_recv.at[chunk, split + step],
            mate(step),
        )

    def far_onward(chunk, step, slot):
        side = 0 if step == 1 else 1
        return remote(
            relay[chunk].at[side],
            far_ref.at[pl.ds(side * half_dev, half_dev), slot, :, columns[chunk]],
            far_send.at[chunk, 2 * split + step],
            far_recv.at[chunk, 2 * split + step],
            mate(step),
        )

    def out_copy(step, slot):
        return remote(
            enc_out_ref.at[pl.ds(2 * core, 2)],
            enc_out_all.at[slot, pl.ds(2 * core, 2)],
            enc_send.at[step],
            enc_recv.at[step],
            mate(step),
        )

    def out_relay(step, slot):
        part = pl.ds(2 * core + (0 if step == 1 else 1), 1)
        return remote(
            enc_out_all.at[slot, part],
            enc_out_all.at[slot, part],
            enc_send.at[3 * split + step],
            enc_recv.at[3 * split + step],
            mate(step),
        )

    def out_twin(step, half, slot):
        return remote(
            enc_out_all.at[slot, pl.ds(2 * half, 2)],
            enc_out_all.at[slot, pl.ds(2 * half, 2)],
            enc_send.at[4 * split + step],
            enc_recv.at[4 * split + step],
            twin,
        )

    def mixed_copy(part, step, slot):
        span = pl.ds(part * (images // 2), images // 2)
        return remote(
            mixed.at[lax.rem(me + step, split), span],
            mixed_all.at[slot, span],
            enc_send.at[split * (1 + part) + step],
            enc_recv.at[split * (1 + part) + step],
            mate(step),
        )

    for step in (1, 3):
        out_copy(step, me).start()
    enc_out_all[me] = enc_out_ref[...]
    tokens = share * split
    local = enc_out_ref.shape[0] * enc_out_ref.shape[1]
    last = (((1,), (1,)), ((), ()))
    first_half = lax.broadcasted_iota(jnp.int32, (1, 128), 1) < HD
    zero = jnp.zeros((), jnp.bfloat16)
    ones = jnp.ones((tokens, 128), jnp.bfloat16)

    def encode(pair, carry):
        picture = patches_ref[pl.ds(2 * pair, 2)].astype(jnp.float32)
        normed = norm_rows(picture.reshape(2 * tokens, -1))
        projected = [
            jnp.dot(normed, enc_proj_ref[kind], preferred_element_type=jnp.float32).astype(
                jnp.bfloat16
            )
            for kind in range(3)
        ]
        places = [(image, first) for image in range(2) for first in range(0, local, 128)]

        def take(kind, image, first):
            lines = slice(image * tokens, (image + 1) * tokens)
            return projected[kind][lines, first : first + 128]

        scores = []
        for image, first in places:
            query = take(0, image, first) * jnp.bfloat16(HD ** (-0.5))
            both = jnp.concatenate(
                [jnp.where(first_half, query, zero), jnp.where(first_half, zero, query)], axis=0
            )
            scores.append(
                lax.dot_general(
                    both, take(1, image, first), last, preferred_element_type=jnp.float32
                )
            )
        expos = [
            jnp.exp(each - jnp.max(each, axis=1, keepdims=True)).astype(jnp.bfloat16)
            for each in scores
        ]
        sums = [
            jnp.dot(
                each,
                jnp.concatenate([take(2, image, first), ones], axis=1),
                preferred_element_type=jnp.float32,
            )
            for each, (image, first) in zip(expos, places)
        ]
        for each, (image, first) in zip(sums, places):
            got = each[:, :128] / each[:, 128:]
            got = jnp.where(first_half, got[:tokens], got[tokens:])
            for place in range(split):
                mixed[place, pair * 2 + image, :, first : first + 128] = got[
                    place * share : (place + 1) * share
                ].astype(jnp.bfloat16)
        return carry

    lax.fori_loop(0, images // 4, encode, 0)
    for step in range(1, split):
        mixed_copy(0, step, me).start()
    for step in (1, 3):
        out_copy(step, behind(step)).wait_recv()
        out_relay(step, behind(step)).start()
        out_twin(step, core, behind(step)).start()
    lax.fori_loop(images // 4, images // 2, encode, 0)
    for step in range(1, split):
        mixed_copy(1, step, me).start()
    for step in (1, 3):
        out_relay(step, behind(2)).wait_recv()
    out_twin(2, core, behind(2)).start()
    for step in (1, 3):
        weight_copy(step, me).start()
    mixed_all[me] = mixed[me]
    encoded = patches_ref[:, me].astype(jnp.float32).reshape(images * share, -1)
    for step in range(split):
        source = behind(step)
        if step:
            out_twin(step, 1 - core, source).wait_recv()
            mixed_copy(0, step, source).wait_recv()
            mixed_copy(1, step, source).wait_recv()
        part = mixed_all[source].astype(jnp.float32).reshape(images * share, local)
        encoded = encoded + jnp.dot(
            part.astype(jnp.bfloat16), enc_out_all[source].reshape(local, -1), preferred_element_type=jnp.float32
        )
    embedded = jnp.dot(norm_rows(encoded), embed_ref[...], preferred_element_type=jnp.float32)
    embedded = embedded.astype(jnp.bfloat16).astype(jnp.float32)
    emb_ref[...] = embedded.reshape(images, share, width).astype(jnp.bfloat16)
    normed_rows = norm_rows(embedded).astype(jnp.float32).reshape(images, share, width)
    for chunk in range(chunks):
        held[chunk][pl.ds(0, images)] = normed_rows[:, :, columns[chunk]].astype(jnp.bfloat16)
    opening = [kind for kind, _ in steps].index("wait")
    for _, number in steps[:opening]:
        ring(number).start()
    for chunk in range(chunks):
        twin_copy(len(plan) + chunk).start()

    for step in range(1, split):
        own_copy(step, me).start()
    own_local = pltpu.make_async_copy(
        emb_ref.at[pl.ds(pair_images * me, pair_images)], own_ref.at[:, me], local_sem.at[0]
    )
    own_local.start()
    weight_local = pltpu.make_async_copy(weights_ref, weights_all.at[:, me], local_sem.at[1])
    weight_local.start()

    def far_local(chunk):
        return pltpu.make_async_copy(
            staged[chunk].at[pl.ds(per_dev * me, per_dev)],
            far_ref.at[:, me, :, columns[chunk]],
            local_sem.at[2 + chunk],
        )

    def choose(chunk):
        for number, entry in enumerate(twins):
            if entry[0] == chunk:
                twin_copy(number).wait_recv()

        def pick(index, carry):
            staged[chunk][index] = held[chunk][pick_ref[index]]
            return carry

        lax.fori_loop(0, per_dev * split, pick, 0, unroll=4)
        for step in (1, 3):
            far_relay(chunk, step).start()
        for step in (1, 3):
            far_direct(chunk, step, me).start()
        far_local(chunk).start()

    def pass_on(chunk):
        for step in (1, 3):
            far_relay(chunk, step).wait_recv()
            far_onward(chunk, step, behind(step)).start()

    def pose_cross(dy, row):
        return remote(
            pose_all.at[pl.ds(row * 2 * ZS, 2 * ZS)],
            pose_all.at[pl.ds(row * 2 * ZS, 2 * ZS)],
            pose_send.at[len(line) + dy - 1],
            pose_recv.at[len(line) + dy - 1],
            y_peer(dy, 1),
        )

    def pose_second():
        for number, (dz, dc) in enumerate(line):
            pose_line(dz, dc, number, line_peer(dz, dc, -1)[0]).wait_recv()
        for dy in range(1, YS):
            pose_cross(dy, y).start()

    def weights_second():
        for step in (1, 3):
            weight_copy(step, behind(step)).wait_recv()
            weight_relay(step, behind(step)).start()
            weight_twin(step, core, behind(step)).start()

    def weights_third():
        for step in (1, 3):
            weight_relay(step, behind(2)).wait_recv()
        weight_twin(2, core, behind(2)).start()

    waits = [number for kind, number in steps if kind == "wait"]
    final = {c: max(i for i, n in enumerate(waits) if plan[n][0] == c) for c in range(chunks)}
    events = {8: pose_second, len(waits) // 4: weights_second, len(waits) // 2: weights_third}
    later, pending, count = {}, [], 0
    for kind, number in steps[opening:]:
        if kind == "send":
            ring(number).start()
            continue
        for action in pending:
            action()
        pending = []
        ring(number).wait_recv()
        twin_copy(number).start()
        count += 1
        if count in events:
            pending.append(events[count])
        for chunk in range(chunks):
            if final[chunk] == count - 1:
                pending.append(functools.partial(choose, chunk))
                later[count + RELAY] = chunk
        if count in later:
            pending.append(functools.partial(pass_on, later.pop(count)))
    for action in pending:
        action()
    for chunk in later.values():
        pass_on(chunk)
    for dy in range(1, YS):
        pose_cross(dy, lax.rem(y + YS - dy, YS)).wait_recv()
    for step in range(1, split):
        own_copy(step, behind(step)).wait_recv()
        weight_twin(step, 1 - core, behind(step)).wait_recv()
    own_local.wait()
    weight_local.wait()
    for number in range(len(plan)):
        ring(number).wait_send()
    for number in range(len(twins)):
        twin_copy(number).wait_send()
    for number, (dz, dc) in enumerate(line):
        pose_line(dz, dc, number, here).wait_send()
    for dy in range(1, YS):
        pose_cross(dy, y).wait_send()
    for step in range(1, split):
        out_twin(step, core, behind(step)).wait_send()
        mixed_copy(0, step, me).wait_send()
        mixed_copy(1, step, me).wait_send()
        own_copy(step, me).wait_send()
        weight_twin(step, core, behind(step)).wait_send()
    for step in (1, 3):
        out_copy(step, me).wait_send()
        out_relay(step, behind(step)).wait_send()
        weight_copy(step, me).wait_send()
        weight_relay(step, behind(step)).wait_send()
    for chunk in range(chunks):
        far_local(chunk).wait()
        for step in (1, 3):
            far_relay(chunk, step).wait_send()
            far_direct(chunk, step, behind(step)).wait_recv()
            far_direct(chunk, step, me).wait_send()
            far_onward(chunk, step, behind(2)).wait_recv()
            far_onward(chunk, step, behind(step)).wait_send()
    decode_part(
        far_ref,
        own_ref,
        weights_all,
        head_ref,
        depth_ref,
        pose_own_ref,
        pose_all,
        partner_ref,
        partner_row_ref,
        result_ref,
        total_ref,
        *finish,
    )


def decode_part(
    far_ref,
    own_ref,
    weights_ref,
    head_ref,
    depth_ref,
    pose_own_ref,
    pose_all_ref,
    partner_ref,
    partner_row_ref,
    result_ref,
    total_ref,
    queries,
    keys,
    values,
    mixed,
    heads_all,
    depth_all,
    staging,
    dense,
    plane_in,
    part_sum,
    line_in,
    x_send,
    x_recv,
    plane_send,
    plane_recv,
    line_send,
    line_recv,
):
    width = own_ref.shape[3]
    pairs, _, tokens = heads_all.shape
    split = depth_all.shape[0]
    share = tokens // split
    here = lax.axis_index("img")
    me = lax.axis_index("mp")
    rows_count = 2 * ZS
    row = lax.rem(here, rows_count)
    y = here // rows_count
    plane = [(dx, dy) for dx in range(split) for dy in range(YS) if dx or dy]
    line = [(dz, dc) for dz in range(ZS) for dc in range(CORES) if dz or dc]

    def plane_peer(dx, dy, sign):
        return (
            lax.rem(y + YS + sign * dy, YS) * rows_count + row,
            lax.rem(me + split + sign * dx, split),
        )

    def line_row(dz, dc, sign):
        z = lax.rem(row // 2 + ZS + sign * dz, ZS)
        return z * 2 + lax.rem(lax.rem(row, 2) + dc, 2)

    def mate(step):
        return (here, lax.rem(me + step, split))

    def behind(step):
        return lax.rem(me + split - step, split)

    def remote(source, target, send, recv, device):
        return pltpu.make_async_remote_copy(
            src_ref=source,
            dst_ref=target,
            send_sem=send,
            recv_sem=recv,
            device_id=device,
            device_id_type=MESH,
        )

    blocks = width // 128
    own_count = own_ref.shape[0]
    per_image = pairs // own_count
    last = (((1,), (1,)), ((), ()))
    lane = lax.broadcasted_iota(jnp.int32, (1, 128), 1)
    first_half = lane < HD

    def weight(kind):
        return weights_ref[kind].reshape(width, width)

    rows = norm_rows(own_ref[...].astype(jnp.float32).reshape(own_count * tokens, width))
    projected = lax.dot_general(rows, weight(0), last, preferred_element_type=jnp.float32)
    projected = projected.astype(jnp.bfloat16) * jnp.bfloat16(HD ** (-0.5))
    zero = jnp.zeros((), jnp.bfloat16)
    for image in range(own_count):
        for block in range(blocks):
            part = projected[image * tokens : (image + 1) * tokens, block * 128 : (block + 1) * 128]
            queries[image, block, :tokens] = jnp.where(first_half, part, zero)
            queries[image, block, tokens:] = jnp.where(first_half, zero, part)

    chunk = 4 * tokens

    def project(step, carry):
        span = pl.ds(pl.multiple_of(step * chunk, chunk), chunk)
        part = far_ref[pl.ds(step * 4, 4)].astype(jnp.float32)
        part = part.reshape(chunk, width).astype(jnp.bfloat16)
        keys[span, :] = lax.dot_general(
            part, weight(1), last, preferred_element_type=jnp.float32
        ).astype(jnp.bfloat16)
        values[span, :] = lax.dot_general(
            part, weight(2), last, preferred_element_type=jnp.float32
        ).astype(jnp.bfloat16)
        return carry

    lax.fori_loop(0, pairs // 4, project, 0, unroll=2)
    def depth_copy(step, slot):
        return remote(
            depth_ref.at[lax.rem(me + step, split)],
            depth_all.at[slot],
            x_send.at[step],
            x_recv.at[step],
            mate(step),
        )

    for step in range(1, split):
        depth_copy(step, me).start()
    depth_all[me] = depth_ref[me]
    staging[...] = jnp.zeros_like(staging)
    members = own_count * split
    group_count, pose_rows, _ = pose_all_ref.shape
    lane_ids = lax.broadcasted_iota(jnp.int32, (pairs, 128), 1)
    chosen = (lane_ids == lax.rem(partner_ref[...], members)).astype(jnp.bfloat16)
    candidates = lax.dot_general(
        pose_all_ref[...].reshape(group_count * pose_rows, 128),
        chosen,
        last,
        preferred_element_type=jnp.float32,
    ).reshape(group_count, pose_rows, pairs)
    owners = lax.broadcasted_iota(jnp.int32, (group_count, pose_rows, pairs), 0)
    held_by = lax.div(partner_row_ref[:1, :pairs], members)
    turned = jnp.sum(jnp.where(owners == held_by[None], candidates, 0.0), axis=0)
    same = lax.broadcasted_iota(jnp.int32, (pose_rows, pose_rows), 0) == lax.broadcasted_iota(
        jnp.int32, (pose_rows, pose_rows), 1
    )
    far_pose = lax.dot_general(
        turned.astype(jnp.bfloat16),
        same.astype(jnp.bfloat16),
        (((0,), (0,)), ((), ())),
        preferred_element_type=jnp.float32,
    )
    ones = jnp.ones((tokens, 128), jnp.bfloat16)

    def attend(pair, carry):
        span = pl.ds(pl.multiple_of(pair * tokens, tokens), tokens)
        image = pair // per_image
        columns = [slice(block * 128, (block + 1) * 128) for block in range(blocks)]
        scores = [
            lax.dot_general(
                queries[image, block], keys[span, part], last, preferred_element_type=jnp.float32
            )
            for block, part in enumerate(columns)
        ]
        expos = [
            jnp.exp(each - jnp.max(each, axis=1, keepdims=True)).astype(jnp.bfloat16)
            for each in scores
        ]
        sums = [
            jnp.dot(
                each,
                jnp.concatenate([values[span, part], ones], axis=1),
                preferred_element_type=jnp.float32,
            )
            for each, part in zip(expos, columns)
        ]
        for each, part in zip(sums, columns):
            got = each[:, :128] / each[:, 128:]
            mixed[span, part] = jnp.where(first_half, got[:tokens], got[tokens:]).astype(
                jnp.bfloat16
            )
        return carry

    lax.fori_loop(0, pairs, attend, 0, unroll=2)

    def finish(step, carry):
        span = pl.ds(pl.multiple_of(step * chunk, chunk), chunk)
        image = step * 4 // per_image
        own = own_ref[image].astype(jnp.float32).reshape(tokens, width)
        settled = jnp.dot(mixed[span, :], weight(3), preferred_element_type=jnp.float32)
        settled = settled + jnp.concatenate([own] * 4, axis=0)
        heads = lax.dot_general(
            head_ref[...], norm_rows(settled), last, preferred_element_type=jnp.float32
        )
        for part in range(4):
            heads_all[step * 4 + part] = heads[:, part * tokens : (part + 1) * tokens]
        return carry

    lax.fori_loop(0, pairs // 4, finish, 0, unroll=2)
    for step in range(1, split):
        depth_copy(step, behind(step)).wait_recv()

    def widen(offset):
        both = jnp.concatenate(
            [depth_all[q, offset : offset + own_count, :share] for q in range(split)], axis=1
        )
        return jnp.concatenate(
            [
                jnp.broadcast_to(both[image : image + 1], (per_image, tokens))
                for image in range(own_count)
            ],
            axis=0,
        )

    depth = widen(0)
    valid = widen(own_count)
    token = lax.broadcasted_iota(jnp.int32, (1, tokens), 1)
    ray_x = (lax.rem(token, 16).astype(jnp.float32) - 7.5) * 0.125
    ray_y = (lax.div(token, 16).astype(jnp.float32) - (tokens // 16 - 1) * 0.5) * 0.125
    rays = [ray_x, ray_y, jnp.ones_like(ray_x)]
    points = [heads_all[:, component, :] for component in range(3)]
    confidence = 1.0 + jnp.exp(heads_all[:, 3, :])
    weight = valid * confidence * (2.0 / tokens)
    own_pose = pose_own_ref[...]
    lane128 = lax.broadcasted_iota(jnp.int32, (pairs, 128), 1)
    own_grad = jnp.zeros((pairs, 128), jnp.float32)
    far_grad = jnp.zeros((pairs, 128), jnp.float32)
    depth_grad = jnp.zeros((pairs, tokens), jnp.float32)
    for component in range(3):
        base = 4 * component
        direction = sum(own_pose[:, base + k : base + k + 1] * rays[k] for k in range(3))
        world = own_pose[:, base + 3 : base + 4] + depth * direction
        predicted = far_pose[:, base + 3 : base + 4] + sum(
            far_pose[:, base + k : base + k + 1] * points[k] for k in range(3)
        )
        slope = weight * (world - predicted)
        depth_grad = depth_grad + slope * direction
        scaled = slope * depth
        for k in range(4):
            mine = scaled * rays[k] if k < 3 else slope
            other = slope * points[k] if k < 3 else slope
            mine = jnp.sum(mine, axis=1, keepdims=True)
            other = jnp.sum(other, axis=1, keepdims=True)
            own_grad = jnp.where(lane128 == base + k, mine, own_grad)
            far_grad = jnp.where(lane128 == base + k, -other, far_grad)
    total_images = YS * 128
    ids = lax.broadcasted_iota(jnp.int32, (pairs, total_images), 1)
    pair_ids = lax.broadcasted_iota(jnp.int32, (pairs, total_images), 0)
    own_ids = (here * split + me) * own_count + lax.div(pair_ids, per_image)
    hits = jnp.concatenate([ids == own_ids, ids == partner_ref[:, :1]], axis=0)
    table = lax.dot_general(
        jnp.concatenate([own_grad, far_grad], axis=0),
        hits.astype(jnp.float32),
        (((0,), (0,)), ((), ())),
        precision=lax.Precision.HIGHEST,
        preferred_element_type=jnp.float32,
    )
    for part in range(YS):
        dense[part] = table[:16, part * 128 : (part + 1) * 128]

    def plane_copy(number, dx, dy, slot):
        return remote(
            dense.at[lax.rem(y + dy, YS)],
            plane_in.at[slot],
            plane_send.at[number],
            plane_recv.at[number],
            plane_peer(dx, dy, 1),
        )

    for number, (dx, dy) in enumerate(plane):
        plane_copy(number, dx, dy, me * YS + y).start()
    plane_in[me * YS + y] = dense[y]

    old = jnp.concatenate(
        [depth[image * per_image : image * per_image + 1] for image in range(own_count)], axis=0
    )
    change = jnp.concatenate(
        [
            jnp.sum(
                depth_grad[image * per_image : (image + 1) * per_image], axis=0, keepdims=True
            )
            for image in range(own_count)
        ],
        axis=0,
    )
    moved = old - depth_step * change
    for place in range(split):
        span = slice(place * share, (place + 1) * share)
        for component, values_now in enumerate(points + [confidence]):
            staging[place, component * pairs : (component + 1) * pairs, :share] = values_now[:, span]
        staging[place, 4 * pairs : 4 * pairs + own_count, :share] = moved[:, span]

    def result_copy(step, slot):
        return remote(
            staging.at[lax.rem(me + step, split)],
            result_ref.at[slot],
            x_send.at[split + step],
            x_recv.at[split + step],
            mate(step),
        )

    for step in range(1, split):
        result_copy(step, me).start()
    result_ref[me] = staging[me]
    for number, (dx, dy) in enumerate(plane):
        source = lax.rem(me + split - dx, split) * YS + lax.rem(y + YS - dy, YS)
        plane_copy(number, dx, dy, source).wait_recv()
    gathered = jnp.sum(plane_in[...], axis=0)
    part_sum[...] = gathered
    line_in[row] = gathered

    def line_copy(number, dz, dc, slot):
        return remote(
            part_sum,
            line_in.at[slot],
            line_send.at[number],
            line_recv.at[number],
            (y * rows_count + line_row(dz, dc, 1), me),
        )

    for number, (dz, dc) in enumerate(line):
        line_copy(number, dz, dc, row).start()
    for number, (dz, dc) in enumerate(line):
        line_copy(number, dz, dc, line_row(dz, dc, -1)).wait_recv()
    total_ref[...] = jnp.sum(line_in[...], axis=0)
    for step in range(1, split):
        depth_copy(step, me).wait_send()
        result_copy(step, behind(step)).wait_recv()
        result_copy(step, me).wait_send()
    for number, (dx, dy) in enumerate(plane):
        plane_copy(number, dx, dy, me * YS + y).wait_send()
    for number, (dz, dc) in enumerate(line):
        line_copy(number, dz, dc, row).wait_send()


def pair_step(
    pick,
    patches,
    enc_proj,
    enc_out,
    embed,
    weights,
    pose,
    head_rows,
    depth_tiles,
    pose_own,
    partner_tile,
    partner_row,
    pairs,
    groups,
):
    images, split, share, _ = patches.shape
    tokens = share * split
    own_count = images // split
    local = enc_out.shape[0] * enc_out.shape[1]
    width = embed.shape[1]
    chunks = len(WIDTHS)
    count = len(link_plan(images, WIDTHS)[1])
    vmem = pl.BlockSpec(memory_space=pltpu.VMEM)
    per_dev = pairs // split
    result_rows = 4 * per_dev + 8
    rows = per_dev * tokens
    b16, f32, dma = jnp.bfloat16, jnp.float32, pltpu.SemaphoreType.DMA
    return pl.pallas_call(
        exchange_kernel,
        out_shape=(
            jax.ShapeDtypeStruct((split, result_rows, 128), f32),
            jax.ShapeDtypeStruct((16, 128), f32),
        ),
        in_specs=[pl.BlockSpec(memory_space=pltpu.SMEM)] + [vmem] * 11,
        out_specs=(vmem, vmem),
        scratch_shapes=[
            pltpu.VMEM((per_dev, split, share, width), b16),
            pltpu.VMEM((own_count, split, share, width), b16),
            pltpu.VMEM((4, split) + weights.shape[1:], b16),
            pltpu.VMEM((groups,) + pose.shape, b16),
            pltpu.VMEM((own_count, width // 128, 2 * tokens, 128), b16),
            pltpu.VMEM((rows, width), b16),
            pltpu.VMEM((rows, width), b16),
            pltpu.VMEM((rows, width), b16),
            pltpu.VMEM((per_dev, head_rows.shape[0], tokens), f32),
            pltpu.VMEM(depth_tiles.shape, f32),
            pltpu.VMEM((split, result_rows, 128), f32),
            pltpu.VMEM((YS, 16, 128), f32),
            pltpu.VMEM((split * YS, 16, 128), f32),
            pltpu.VMEM((16, 128), f32),
            pltpu.VMEM((2 * ZS, 16, 128), f32),
            dma((2 * split,)),
            dma((2 * split,)),
            dma((split * YS,)),
            dma((split * YS,)),
            dma((2 * ZS,)),
            dma((2 * ZS,)),
        ]
        + [pltpu.VMEM((groups * images, share, w), b16) for w in WIDTHS]
        + [pltpu.VMEM((pairs, share, w), b16) for w in WIDTHS]
        + [pltpu.VMEM((2, per_dev // 2, share, w), b16) for w in WIDTHS]
        + [
            pltpu.VMEM((split, images, share, local), b16),
            pltpu.VMEM((split, images, share, local), b16),
            pltpu.VMEM((split,) + enc_out.shape, b16),
            pltpu.VMEM((images, share, width), b16),
            dma((5 * split,)),
            dma((5 * split,)),
            dma((count,)),
            dma((count,)),
            dma((count + chunks,)),
            dma((count + chunks,)),
            dma((4 * split,)),
            dma((4 * split,)),
            dma((2 * ZS + YS,)),
            dma((2 * ZS + YS,)),
            dma((chunks, 3 * split)),
            dma((chunks, 3 * split)),
            dma((2 + chunks,)),
        ],
        compiler_params=pltpu.CompilerParams(
            collective_id=0, has_side_effects=True, vmem_limit_bytes=61 * 2**20
        ),
        name="pair_step",
    )(
        pick,
        patches,
        enc_proj,
        enc_out,
        embed,
        weights,
        pose,
        head_rows,
        depth_tiles,
        pose_own,
        partner_tile,
        partner_row,
    )


def shards(
    patches,
    encoder_proj,
    encoder_out,
    decoder_embed,
    decoder_proj,
    decoder_out,
    head_weight,
    partners,
    depths,
    camera_poses,
    valid_mask,
):
    images, tokens, model_width = patches.shape
    dec_width = decoder_embed.shape[1]
    enc_local = encoder_proj.shape[2]
    split = lax.axis_size("mp")
    place = lax.axis_index("mp")
    own_count = images // split
    flat_partner = partners.reshape(-1)
    pair_count = flat_partner.shape[0]
    groups = lax.axis_size("img")
    here = lax.axis_index("img")
    weights = jnp.concatenate([jnp.transpose(decoder_proj, (1, 2, 0)), decoder_out[None]], axis=0)
    pose_tile = jnp.pad(
        camera_poses.astype(jnp.bfloat16), ((0, 4), (0, 128 - camera_poses.shape[1]))
    )

    token_share = tokens // split
    owner = flat_partner // images
    shift_y = (here // (2 * ZS) - owner // (2 * ZS)) % YS
    shift_z = ((here // 2) % ZS - (owner // 2) % ZS) % ZS
    shift_core = (here - owner) % 2
    pick = ((shift_core * YS + shift_y) * ZS + shift_z) * images + flat_partner % images
    head_rows = jnp.pad(head_weight.T, ((0, 12), (0, 0)))
    own_pairs = pair_count // split
    depth_mask = jnp.stack([depths, valid_mask.astype(jnp.float32)], axis=0)
    depth_tiles = depth_mask.reshape(2, split, own_count, token_share).transpose(1, 0, 2, 3)
    depth_tiles = jnp.pad(
        depth_tiles.reshape(split, 2 * own_count, token_share),
        ((0, 0), (0, 8 - 2 * own_count), (0, 128 - token_share)),
    )
    pose_own = lax.dynamic_slice_in_dim(camera_poses, place * own_count, own_count, 1)
    pose_own = jnp.pad(jnp.repeat(pose_own.T, K, axis=0), ((0, 0), (0, 116)))
    own_partner = lax.dynamic_slice_in_dim(flat_partner, place * own_pairs, own_pairs, 0)
    partner_tile = jnp.broadcast_to(own_partner[:, None], (own_pairs, 128))
    partner_row = jnp.broadcast_to(jnp.pad(own_partner, (0, 128 - own_pairs))[None], (8, 128))
    results, total = pair_step(
        pick,
        patches.reshape(images, split, token_share, model_width),
        jnp.transpose(encoder_proj, (1, 0, 2)),
        encoder_out.reshape(4, enc_local // 4, model_width),
        decoder_embed,
        weights,
        pose_tile,
        head_rows,
        depth_tiles,
        pose_own,
        partner_tile,
        partner_row,
        pair_count,
        groups,
    )
    pointmap = results[:, : 4 * own_pairs, :token_share].reshape(split, 4, own_pairs, token_share)
    pointmap = pointmap.transpose(1, 0, 2, 3).reshape(4, pair_count, token_share)
    new_depths = results[:, 4 * own_pairs : 4 * own_pairs + own_count, :token_share]
    new_depths = new_depths.reshape(images, token_share)
    grad_pose = lax.dynamic_slice(total, (0, here % (2 * ZS) * images), (12, images))
    new_poses = camera_poses - pose_step * grad_pose
    return (pointmap, new_depths, new_poses)


def solution(mesh):
    placed = (
        P("img", None, None),
        P(None, None, "mp"),
        P("mp", None),
        P(),
        P(None, None, "mp"),
        P("mp", None),
        P(),
        P("img", None),
        P("img", "mp"),
        P(None, "img"),
        P("img", "mp"),
    )
    return jax.shard_map(
        shards,
        mesh=mesh,
        in_specs=placed,
        out_specs=(P(None, "img", "mp"), P("img", "mp"), P(None, "img")),
        check_vma=False,
    )
```

```python
import functools

import jax
import jax.numpy as jnp
from jax import lax
from jax.experimental import pallas as pl
from jax.experimental.pallas import tpu as pltpu
from jax.sharding import PartitionSpec as P

HD = 64
K = 8


epsilon = 1e-06
depth_step = 0.1
pose_step = 0.005


def norm_rows(values):
    average = jnp.mean(values, axis=-1, keepdims=True)
    centred = values - average
    variance = jnp.mean(centred * centred, axis=-1, keepdims=True)
    return (centred * lax.rsqrt(variance + epsilon)).astype(jnp.bfloat16)


YS, ZS, CORES = 4, 8, 2
FIRST = 5
WIDTHS = (384, 384)
RELAY = 18
AHEAD, DELAY = 4.0, 4.0
MESH = pl.DeviceIdType.MESH


def link_plan(images, spans):
    split = {"z": (0, FIRST), "y": (FIRST, images)}
    full = sum(spans)
    waiting = {"y+": [], "y-": [], "z+": [], "z-": []}
    free = {link: 0.0 for link in waiting}
    plan, flight, steps = [], [], []

    def push(now, chunk, link, source, target, span):
        waiting[link].append((chunk, len(waiting[link]) + 1000 * now, source, target, span))

    def issue(now):
        for link, queue in waiting.items():
            while queue and free[link] <= now + AHEAD:
                entry = min(queue)
                queue.remove(entry)
                chunk, _, source, target, span = entry
                free[link] = max(now, free[link]) + (span[1] - span[0]) * spans[chunk] / full
                flight.append((free[link] + DELAY, len(plan)))
                steps.append(("send", len(plan)))
                plan.append((chunk, link, source, target, span))

    def forward(now, chunk, dy, dz, span):
        if span[1] <= FIRST:
            low, high = split["z"]
            half = (low + high + 1) // 2
            if dy == 0:
                if dz in (0, 1, 2):
                    push(now, chunk, "z+", (dy, dz), (dy, dz + 1), span)
                if dz == 3:
                    push(now, chunk, "z+", (dy, dz), (dy, 4), (low, half))
                if dz in (0, 7, 6):
                    push(now, chunk, "z-", (dy, dz), (dy, (dz - 1) % ZS), span)
                if dz == 5:
                    push(now, chunk, "z-", (dy, dz), (dy, 4), (half, high))
                push(now, chunk, "y+", (dy, dz), (1, dz), span)
                push(now, chunk, "y-", (dy, dz), (3, dz), span)
            if dy == 1 and dz % 2 == 0:
                push(now, chunk, "y+", (dy, dz), (2, dz), span)
            if dy == 3 and dz % 2 == 1:
                push(now, chunk, "y-", (dy, dz), (2, dz), span)
        else:
            low, high = split["y"]
            half = (low + high + 1) // 2
            if dz == 0:
                if dy == 0:
                    push(now, chunk, "y+", (0, 0), (1, 0), span)
                    push(now, chunk, "y-", (0, 0), (3, 0), span)
                if dy == 1:
                    push(now, chunk, "y+", (1, 0), (2, 0), (low, half))
                if dy == 3:
                    push(now, chunk, "y-", (3, 0), (2, 0), (half, high))
            if dz in (0, 1, 2):
                push(now, chunk, "z+", (dy, dz), (dy, dz + 1), span)
            if dz == 3 and dy < 2:
                push(now, chunk, "z+", (dy, dz), (dy, 4), span)
            if dz in (0, 7, 6):
                push(now, chunk, "z-", (dy, dz), (dy, (dz - 1) % ZS), span)
            if dz == 5 and dy >= 2:
                push(now, chunk, "z-", (dy, dz), (dy, 4), span)

    for chunk in range(len(spans)):
        forward(0.0, chunk, 0, 0, split["z"])
        forward(0.0, chunk, 0, 0, split["y"])
    issue(0.0)
    while flight:
        entry = min(flight)
        flight.remove(entry)
        now, number = entry
        chunk, _, _, target, span = plan[number]
        steps.append(("wait", number))
        forward(now, chunk, target[0], target[1], span)
        issue(now)
    return steps, plan


def exchange_kernel(
    pick_ref,
    patches_ref,
    enc_proj_ref,
    enc_out_ref,
    embed_ref,
    weights_ref,
    head_ref,
    floats_ref,
    ints_ref,
    result_ref,
    total_ref,
    far_ref,
    own_ref,
    weights_all,
    pose_all,
    *scratch,
):
    finish, scratch = scratch[:17], scratch[17:]
    chunks = len(WIDTHS)
    held, scratch = scratch[:chunks], scratch[chunks:]
    staged, scratch = scratch[:chunks], scratch[chunks:]
    relay, scratch = scratch[:chunks], scratch[chunks:]
    (
        mixed,
        mixed_all,
        enc_out_all,
        emb_ref,
        enc_send,
        enc_recv,
        ring_send,
        ring_recv,
        twin_send,
        twin_recv,
        line_send,
        line_recv,
        pose_send,
        pose_recv,
        far_send,
        far_recv,
        local_sem,
    ) = scratch
    columns = [slice(sum(WIDTHS[:c]), sum(WIDTHS[: c + 1])) for c in range(chunks)]
    images, share, width = emb_ref.shape
    here = lax.axis_index("img")
    me = lax.axis_index("mp")
    core = lax.rem(here, 2)
    z = lax.rem(here // 2, ZS)
    y = here // (2 * ZS)
    split = far_ref.shape[1]
    per_dev = far_ref.shape[0]
    half_dev = per_dev // 2

    def spot(yy, zz, cc):
        return ((yy * ZS + zz) * 2 + cc, me)

    def mate(step):
        return (here, lax.rem(me + step, split))

    def behind(step):
        return lax.rem(me + split - step, split)

    twin = spot(y, z, 1 - core)
    links = {
        "y+": spot(lax.rem(y + 1, YS), z, core),
        "y-": spot(lax.rem(y + YS - 1, YS), z, core),
        "z+": spot(y, lax.rem(z + 1, ZS), core),
        "z-": spot(y, lax.rem(z + ZS - 1, ZS), core),
    }
    line = [(dz, dc) for dz in range(ZS) for dc in range(CORES) if dz or dc]

    def line_peer(dz, dc, sign):
        return spot(y, lax.rem(z + ZS + sign * dz, ZS), lax.rem(core + dc, 2))

    def y_peer(dy, sign):
        return spot(lax.rem(y + YS + sign * dy, YS), z, core)

    barrier = pltpu.get_barrier_semaphore()
    peers = [line_peer(dz, dc, 1) for dz, dc in line]
    peers += [
        (spot(lax.rem(y + dy, YS), z, core)[0], lax.rem(me + dx, split))
        for dx in range(split)
        for dy in range(YS)
        if dx or dy
    ]
    for peer in peers:
        pl.semaphore_signal(barrier, inc=1, device_id=peer, device_id_type=MESH)
    pose_all[here] = floats_ref[2 * split].astype(jnp.bfloat16)
    pl.semaphore_wait(barrier, len(peers))

    def remote(source, target, send, recv, device):
        return pltpu.make_async_remote_copy(
            src_ref=source,
            dst_ref=target,
            send_sem=send,
            recv_sem=recv,
            device_id=device,
            device_id_type=MESH,
        )

    steps, plan = link_plan(images, WIDTHS)

    def block(chunk, side, slot, span):
        first = ((side * YS + slot[0]) * ZS + slot[1]) * images
        return held[chunk].at[pl.ds(first + span[0], span[1] - span[0])]

    def ring(number):
        chunk, link, source, target, span = plan[number]
        return remote(
            block(chunk, 0, source, span),
            block(chunk, 0, target, span),
            ring_send.at[number],
            ring_recv.at[number],
            links[link],
        )

    twins = [(entry[0], entry[3], entry[4]) for entry in plan]
    twins += [(chunk, (0, 0), (0, images)) for chunk in range(chunks)]

    def twin_copy(number):
        chunk, slot, span = twins[number]
        return remote(
            block(chunk, 0, slot, span),
            block(chunk, 1, slot, span),
            twin_send.at[number],
            twin_recv.at[number],
            twin,
        )

    def pose_line(dz, dc, number, slot):
        return remote(
            pose_all.at[slot],
            pose_all.at[slot],
            pose_send.at[number],
            pose_recv.at[number],
            line_peer(dz, dc, 1),
        )

    for number, (dz, dc) in enumerate(line):
        pose_line(dz, dc, number, here).start()

    pair_images = images // split

    def own_copy(step, slot):
        return remote(
            emb_ref.at[pl.ds(pair_images * lax.rem(me + step, split), pair_images)],
            own_ref.at[:, slot],
            line_send.at[step],
            line_recv.at[step],
            mate(step),
        )

    def weight_copy(step, slot):
        return remote(
            weights_ref.at[pl.ds(2 * core, 2)],
            weights_all.at[pl.ds(2 * core, 2), slot],
            line_send.at[split + step],
            line_recv.at[split + step],
            mate(step),
        )

    def weight_relay(step, slot):
        kind = 2 * core + (0 if step == 1 else 1)
        return remote(
            weights_all.at[pl.ds(kind, 1), slot],
            weights_all.at[pl.ds(kind, 1), slot],
            line_send.at[3 * split + step],
            line_recv.at[3 * split + step],
            mate(step),
        )

    def weight_twin(step, half, slot):
        return remote(
            weights_all.at[pl.ds(2 * half, 2), slot],
            weights_all.at[pl.ds(2 * half, 2), slot],
            line_send.at[2 * split + step],
            line_recv.at[2 * split + step],
            twin,
        )

    def far_direct(chunk, step, slot):
        return remote(
            staged[chunk].at[pl.ds(per_dev * lax.rem(me + step, split), per_dev)],
            far_ref.at[:, slot, :, columns[chunk]],
            far_send.at[chunk, step],
            far_recv.at[chunk, step],
            mate(step),
        )

    def far_relay(chunk, step):
        side = 0 if step == 1 else 1
        return remote(
            staged[chunk].at[pl.ds(per_dev * lax.rem(me + 2, split) + side * half_dev, half_dev)],
            relay[chunk].at[side],
            far_send.at[chunk, split + step],
            far_recv.at[chunk, split + step],
            mate(step),
        )

    def far_onward(chunk, step, slot):
        side = 0 if step == 1 else 1
        return remote(
            relay[chunk].at[side],
            far_ref.at[pl.ds(side * half_dev, half_dev), slot, :, columns[chunk]],
            far_send.at[chunk, 2 * split + step],
            far_recv.at[chunk, 2 * split + step],
            mate(step),
        )

    def out_copy(step, slot):
        return remote(
            enc_out_ref.at[pl.ds(2 * core, 2)],
            enc_out_all.at[slot, pl.ds(2 * core, 2)],
            enc_send.at[step],
            enc_recv.at[step],
            mate(step),
        )

    def out_relay(step, slot):
        part = pl.ds(2 * core + (0 if step == 1 else 1), 1)
        return remote(
            enc_out_all.at[slot, part],
            enc_out_all.at[slot, part],
            enc_send.at[3 * split + step],
            enc_recv.at[3 * split + step],
            mate(step),
        )

    def out_twin(step, half, slot):
        return remote(
            enc_out_all.at[slot, pl.ds(2 * half, 2)],
            enc_out_all.at[slot, pl.ds(2 * half, 2)],
            enc_send.at[4 * split + step],
            enc_recv.at[4 * split + step],
            twin,
        )

    def mixed_copy(part, step, slot):
        span = pl.ds(part * (images // 2), images // 2)
        return remote(
            mixed.at[lax.rem(me + step, split), span],
            mixed_all.at[slot, span],
            enc_send.at[split * (1 + part) + step],
            enc_recv.at[split * (1 + part) + step],
            mate(step),
        )

    for step in (1, 3):
        out_copy(step, me).start()
    enc_out_all[me] = enc_out_ref[...]
    tokens = share * split
    local = enc_out_ref.shape[0] * enc_out_ref.shape[1]
    last = (((1,), (1,)), ((), ()))
    first_half = lax.broadcasted_iota(jnp.int32, (1, 128), 1) < HD
    zero = jnp.zeros((), jnp.bfloat16)
    ones = jnp.ones((tokens, 128), jnp.bfloat16)

    def encode(pair, carry):
        picture = patches_ref[pl.ds(2 * pair, 2)].astype(jnp.float32)
        normed = norm_rows(picture.reshape(2 * tokens, -1))
        projected = [
            jnp.dot(normed, enc_proj_ref[kind], preferred_element_type=jnp.float32).astype(
                jnp.bfloat16
            )
            for kind in range(3)
        ]
        places = [(image, first) for image in range(2) for first in range(0, local, 128)]

        def take(kind, image, first):
            lines = slice(image * tokens, (image + 1) * tokens)
            return projected[kind][lines, first : first + 128]

        scores = []
        for image, first in places:
            query = take(0, image, first) * jnp.bfloat16(HD ** (-0.5))
            both = jnp.concatenate(
                [jnp.where(first_half, query, zero), jnp.where(first_half, zero, query)], axis=0
            )
            scores.append(
                lax.dot_general(
                    both, take(1, image, first), last, preferred_element_type=jnp.float32
                )
            )
        expos = [
            jnp.exp(each - jnp.max(each, axis=1, keepdims=True)).astype(jnp.bfloat16)
            for each in scores
        ]
        sums = [
            jnp.dot(
                each,
                jnp.concatenate([take(2, image, first), ones], axis=1),
                preferred_element_type=jnp.float32,
            )
            for each, (image, first) in zip(expos, places)
        ]
        for each, (image, first) in zip(sums, places):
            got = each[:, :128] / each[:, 128:]
            got = jnp.where(first_half, got[:tokens], got[tokens:])
            for place in range(split):
                mixed[place, pair * 2 + image, :, first : first + 128] = got[
                    place * share : (place + 1) * share
                ].astype(jnp.bfloat16)
        return carry

    lax.fori_loop(0, images // 4, encode, 0)
    for step in range(1, split):
        mixed_copy(0, step, me).start()
    for step in (1, 3):
        out_copy(step, behind(step)).wait_recv()
        out_relay(step, behind(step)).start()
        out_twin(step, core, behind(step)).start()
    lax.fori_loop(images // 4, images // 2, encode, 0)
    for step in range(1, split):
        mixed_copy(1, step, me).start()
    for step in (1, 3):
        out_relay(step, behind(2)).wait_recv()
    out_twin(2, core, behind(2)).start()
    for step in (1, 3):
        weight_copy(step, me).start()
    mixed_all[me] = mixed[me]
    encoded = patches_ref[:, me].astype(jnp.float32).reshape(images * share, -1)
    for step in range(split):
        source = behind(step)
        if step:
            out_twin(step, 1 - core, source).wait_recv()
            mixed_copy(0, step, source).wait_recv()
            mixed_copy(1, step, source).wait_recv()
        part = mixed_all[source].astype(jnp.float32).reshape(images * share, local)
        encoded = encoded + jnp.dot(
            part.astype(jnp.bfloat16), enc_out_all[source].reshape(local, -1), preferred_element_type=jnp.float32
        )
    embedded = jnp.dot(norm_rows(encoded), embed_ref[...], preferred_element_type=jnp.float32)
    embedded = embedded.astype(jnp.bfloat16).astype(jnp.float32)
    emb_ref[...] = embedded.reshape(images, share, width).astype(jnp.bfloat16)
    normed_rows = norm_rows(embedded).astype(jnp.float32).reshape(images, share, width)
    for chunk in range(chunks):
        held[chunk][pl.ds(0, images)] = normed_rows[:, :, columns[chunk]].astype(jnp.bfloat16)
    opening = [kind for kind, _ in steps].index("wait")
    for _, number in steps[:opening]:
        ring(number).start()
    for chunk in range(chunks):
        twin_copy(len(plan) + chunk).start()

    for step in range(1, split):
        own_copy(step, me).start()
    own_local = pltpu.make_async_copy(
        emb_ref.at[pl.ds(pair_images * me, pair_images)], own_ref.at[:, me], local_sem.at[0]
    )
    own_local.start()
    weight_local = pltpu.make_async_copy(weights_ref, weights_all.at[:, me], local_sem.at[1])
    weight_local.start()

    def far_local(chunk):
        return pltpu.make_async_copy(
            staged[chunk].at[pl.ds(per_dev * me, per_dev)],
            far_ref.at[:, me, :, columns[chunk]],
            local_sem.at[2 + chunk],
        )

    def choose(chunk):
        for number, entry in enumerate(twins):
            if entry[0] == chunk:
                twin_copy(number).wait_recv()

        def pick(index, carry):
            staged[chunk][index] = held[chunk][pick_ref[index]]
            return carry

        lax.fori_loop(0, per_dev * split, pick, 0, unroll=4)
        for step in (1, 3):
            far_relay(chunk, step).start()
        for step in (1, 3):
            far_direct(chunk, step, me).start()
        far_local(chunk).start()

    def pass_on(chunk):
        for step in (1, 3):
            far_relay(chunk, step).wait_recv()
            far_onward(chunk, step, behind(step)).start()

    def pose_cross(dy, row):
        return remote(
            pose_all.at[pl.ds(row * 2 * ZS, 2 * ZS)],
            pose_all.at[pl.ds(row * 2 * ZS, 2 * ZS)],
            pose_send.at[len(line) + dy - 1],
            pose_recv.at[len(line) + dy - 1],
            y_peer(dy, 1),
        )

    def pose_second():
        for number, (dz, dc) in enumerate(line):
            pose_line(dz, dc, number, line_peer(dz, dc, -1)[0]).wait_recv()
        for dy in range(1, YS):
            pose_cross(dy, y).start()

    def weights_second():
        for step in (1, 3):
            weight_copy(step, behind(step)).wait_recv()
            weight_relay(step, behind(step)).start()
            weight_twin(step, core, behind(step)).start()

    def weights_third():
        for step in (1, 3):
            weight_relay(step, behind(2)).wait_recv()
        weight_twin(2, core, behind(2)).start()

    waits = [number for kind, number in steps if kind == "wait"]
    final = {c: max(i for i, n in enumerate(waits) if plan[n][0] == c) for c in range(chunks)}
    events = {8: pose_second, len(waits) // 4: weights_second, len(waits) // 2: weights_third}
    later, pending, count = {}, [], 0
    for kind, number in steps[opening:]:
        if kind == "send":
            ring(number).start()
            continue
        for action in pending:
            action()
        pending = []
        ring(number).wait_recv()
        twin_copy(number).start()
        count += 1
        if count in events:
            pending.append(events[count])
        for chunk in range(chunks):
            if final[chunk] == count - 1:
                pending.append(functools.partial(choose, chunk))
                later[count + RELAY] = chunk
        if count in later:
            pending.append(functools.partial(pass_on, later.pop(count)))
    for action in pending:
        action()
    for chunk in later.values():
        pass_on(chunk)
    for dy in range(1, YS):
        pose_cross(dy, lax.rem(y + YS - dy, YS)).wait_recv()
    for step in range(1, split):
        own_copy(step, behind(step)).wait_recv()
        weight_twin(step, 1 - core, behind(step)).wait_recv()
    own_local.wait()
    weight_local.wait()
    for number in range(len(plan)):
        ring(number).wait_send()
    for number in range(len(twins)):
        twin_copy(number).wait_send()
    for number, (dz, dc) in enumerate(line):
        pose_line(dz, dc, number, here).wait_send()
    for dy in range(1, YS):
        pose_cross(dy, y).wait_send()
    for step in range(1, split):
        out_twin(step, core, behind(step)).wait_send()
        mixed_copy(0, step, me).wait_send()
        mixed_copy(1, step, me).wait_send()
        own_copy(step, me).wait_send()
        weight_twin(step, core, behind(step)).wait_send()
    for step in (1, 3):
        out_copy(step, me).wait_send()
        out_relay(step, behind(step)).wait_send()
        weight_copy(step, me).wait_send()
        weight_relay(step, behind(step)).wait_send()
    rest = decode_part(
        far_ref,
        own_ref,
        weights_all,
        head_ref,
        floats_ref,
        pose_all,
        ints_ref,
        result_ref,
        total_ref,
        *finish,
    )
    for chunk in range(chunks):
        far_local(chunk).wait()
        for step in (1, 3):
            far_relay(chunk, step).wait_send()
            far_direct(chunk, step, behind(step)).wait_recv()
            far_direct(chunk, step, me).wait_send()
            far_onward(chunk, step, behind(2)).wait_recv()
            far_onward(chunk, step, behind(step)).wait_send()
    rest()


def decode_part(
    far_ref,
    own_ref,
    weights_ref,
    head_ref,
    floats_ref,
    pose_all_ref,
    ints_ref,
    result_ref,
    total_ref,
    queries,
    keys,
    values,
    mixed,
    heads_all,
    depth_all,
    staging,
    dense,
    plane_in,
    part_sum,
    line_in,
    x_send,
    x_recv,
    plane_send,
    plane_recv,
    line_send,
    line_recv,
):
    width = own_ref.shape[3]
    pairs, _, tokens = heads_all.shape
    split = depth_all.shape[0]
    share = tokens // split
    here = lax.axis_index("img")
    me = lax.axis_index("mp")
    rows_count = 2 * ZS
    row = lax.rem(here, rows_count)
    y = here // rows_count
    plane = [(dx, dy) for dx in range(split) for dy in range(YS) if dx or dy]
    line = [(dz, dc) for dz in range(ZS) for dc in range(CORES) if dz or dc]

    def plane_peer(dx, dy, sign):
        return (
            lax.rem(y + YS + sign * dy, YS) * rows_count + row,
            lax.rem(me + split + sign * dx, split),
        )

    def line_row(dz, dc, sign):
        z = lax.rem(row // 2 + ZS + sign * dz, ZS)
        return z * 2 + lax.rem(lax.rem(row, 2) + dc, 2)

    def mate(step):
        return (here, lax.rem(me + step, split))

    def behind(step):
        return lax.rem(me + split - step, split)

    def remote(source, target, send, recv, device):
        return pltpu.make_async_remote_copy(
            src_ref=source,
            dst_ref=target,
            send_sem=send,
            recv_sem=recv,
            device_id=device,
            device_id_type=MESH,
        )

    blocks = width // 128
    own_count = own_ref.shape[0]
    per_image = pairs // own_count
    last = (((1,), (1,)), ((), ()))
    lane = lax.broadcasted_iota(jnp.int32, (1, 128), 1)
    first_half = lane < HD

    def weight(kind):
        return weights_ref[kind].reshape(width, width)

    rows = norm_rows(own_ref[...].astype(jnp.float32).reshape(own_count * tokens, width))
    projected = lax.dot_general(rows, weight(0), last, preferred_element_type=jnp.float32)
    projected = projected.astype(jnp.bfloat16) * jnp.bfloat16(HD ** (-0.5))
    zero = jnp.zeros((), jnp.bfloat16)
    for image in range(own_count):
        for block in range(blocks):
            part = projected[image * tokens : (image + 1) * tokens, block * 128 : (block + 1) * 128]
            queries[image, block, :tokens] = jnp.where(first_half, part, zero)
            queries[image, block, tokens:] = jnp.where(first_half, zero, part)

    def depth_copy(step, slot):
        return remote(
            floats_ref.at[split + lax.rem(me + step, split)],
            depth_all.at[slot],
            x_send.at[step],
            x_recv.at[step],
            mate(step),
        )

    for step in range(1, split):
        depth_copy(step, me).start()
    depth_all[me] = floats_ref[split + me]
    own_partner = ints_ref[me, :pairs]
    staging[...] = jnp.zeros_like(staging)
    members = own_count * split
    group_count, pose_rows, _ = pose_all_ref.shape
    lane_ids = lax.broadcasted_iota(jnp.int32, (pairs, 128), 1)
    chosen = (lane_ids == lax.rem(own_partner, members)).astype(jnp.bfloat16)
    candidates = lax.dot_general(
        pose_all_ref[...].reshape(group_count * pose_rows, 128),
        chosen,
        last,
        preferred_element_type=jnp.float32,
    ).reshape(group_count, pose_rows, pairs)
    owners = lax.broadcasted_iota(jnp.int32, (group_count, pose_rows, pairs), 0)
    held_by = lax.div(ints_ref[me, pairs : pairs + 1, :pairs], members)
    turned = jnp.sum(jnp.where(owners == held_by[None], candidates, 0.0), axis=0)
    same = lax.broadcasted_iota(jnp.int32, (pose_rows, pose_rows), 0) == lax.broadcasted_iota(
        jnp.int32, (pose_rows, pose_rows), 1
    )
    far_pose = lax.dot_general(
        turned.astype(jnp.bfloat16),
        same.astype(jnp.bfloat16),
        (((0,), (0,)), ((), ())),
        preferred_element_type=jnp.float32,
    )

    def rest():
        chunk = 4 * tokens

        def project(step, carry):
            span = pl.ds(pl.multiple_of(step * chunk, chunk), chunk)
            part = far_ref[pl.ds(step * 4, 4)].astype(jnp.float32)
            part = part.reshape(chunk, width).astype(jnp.bfloat16)
            keys[span, :] = lax.dot_general(
                part, weight(1), last, preferred_element_type=jnp.float32
            ).astype(jnp.bfloat16)
            values[span, :] = lax.dot_general(
                part, weight(2), last, preferred_element_type=jnp.float32
            ).astype(jnp.bfloat16)
            return carry

        lax.fori_loop(0, pairs // 4, project, 0, unroll=2)
        ones = jnp.ones((tokens, 128), jnp.bfloat16)

        def attend(pair, carry):
            span = pl.ds(pl.multiple_of(pair * tokens, tokens), tokens)
            image = pair // per_image
            columns = [slice(block * 128, (block + 1) * 128) for block in range(blocks)]
            scores = [
                lax.dot_general(
                    queries[image, block], keys[span, part], last, preferred_element_type=jnp.float32
                )
                for block, part in enumerate(columns)
            ]
            expos = [
                jnp.exp(each - jnp.max(each, axis=1, keepdims=True)).astype(jnp.bfloat16)
                for each in scores
            ]
            sums = [
                jnp.dot(
                    each,
                    jnp.concatenate([values[span, part], ones], axis=1),
                    preferred_element_type=jnp.float32,
                )
                for each, part in zip(expos, columns)
            ]
            for each, part in zip(sums, columns):
                got = each[:, :128] / each[:, 128:]
                mixed[span, part] = jnp.where(first_half, got[:tokens], got[tokens:]).astype(
                    jnp.bfloat16
                )
            return carry

        lax.fori_loop(0, pairs, attend, 0, unroll=2)

        def finish(step, carry):
            span = pl.ds(pl.multiple_of(step * chunk, chunk), chunk)
            image = step * 4 // per_image
            own = own_ref[image].astype(jnp.float32).reshape(tokens, width)
            settled = jnp.dot(mixed[span, :], weight(3), preferred_element_type=jnp.float32)
            settled = settled + jnp.concatenate([own] * 4, axis=0)
            heads = lax.dot_general(
                head_ref[...], norm_rows(settled), last, preferred_element_type=jnp.float32
            )
            for part in range(4):
                heads_all[step * 4 + part] = heads[:, part * tokens : (part + 1) * tokens]
            return carry

        lax.fori_loop(0, pairs // 4, finish, 0, unroll=2)
        for step in range(1, split):
            depth_copy(step, behind(step)).wait_recv()

        def widen(offset):
            both = jnp.concatenate(
                [depth_all[q, offset : offset + own_count, :share] for q in range(split)], axis=1
            )
            return jnp.concatenate(
                [
                    jnp.broadcast_to(both[image : image + 1], (per_image, tokens))
                    for image in range(own_count)
                ],
                axis=0,
            )

        depth = widen(0)
        valid = widen(own_count)
        token = lax.broadcasted_iota(jnp.int32, (1, tokens), 1)
        ray_x = (lax.rem(token, 16).astype(jnp.float32) - 7.5) * 0.125
        ray_y = (lax.div(token, 16).astype(jnp.float32) - (tokens // 16 - 1) * 0.5) * 0.125
        rays = [ray_x, ray_y, jnp.ones_like(ray_x)]
        points = [heads_all[:, component, :] for component in range(3)]
        confidence = 1.0 + jnp.exp(heads_all[:, 3, :])
        factor = valid * confidence * (2.0 / tokens)
        own_pose = floats_ref[me]
        lane128 = lax.broadcasted_iota(jnp.int32, (pairs, 128), 1)
        own_grad = jnp.zeros((pairs, 128), jnp.float32)
        far_grad = jnp.zeros((pairs, 128), jnp.float32)
        depth_grad = jnp.zeros((pairs, tokens), jnp.float32)
        for component in range(3):
            base = 4 * component
            direction = sum(own_pose[:, base + k : base + k + 1] * rays[k] for k in range(3))
            world = own_pose[:, base + 3 : base + 4] + depth * direction
            predicted = far_pose[:, base + 3 : base + 4] + sum(
                far_pose[:, base + k : base + k + 1] * points[k] for k in range(3)
            )
            slope = factor * (world - predicted)
            depth_grad = depth_grad + slope * direction
            scaled = slope * depth
            for k in range(4):
                mine = scaled * rays[k] if k < 3 else slope
                other = slope * points[k] if k < 3 else slope
                mine = jnp.sum(mine, axis=1, keepdims=True)
                other = jnp.sum(other, axis=1, keepdims=True)
                own_grad = jnp.where(lane128 == base + k, mine, own_grad)
                far_grad = jnp.where(lane128 == base + k, -other, far_grad)
        total_images = YS * 128
        ids = lax.broadcasted_iota(jnp.int32, (pairs, total_images), 1)
        pair_ids = lax.broadcasted_iota(jnp.int32, (pairs, total_images), 0)
        own_ids = (here * split + me) * own_count + lax.div(pair_ids, per_image)
        hits = jnp.concatenate([ids == own_ids, ids == own_partner[:, :1]], axis=0)
        table = lax.dot_general(
            jnp.concatenate([own_grad, far_grad], axis=0),
            hits.astype(jnp.float32),
            (((0,), (0,)), ((), ())),
            precision=lax.Precision.HIGHEST,
            preferred_element_type=jnp.float32,
        )
        for part in range(YS):
            dense[part] = table[:16, part * 128 : (part + 1) * 128]

        def plane_copy(number, dx, dy, slot):
            return remote(
                dense.at[lax.rem(y + dy, YS)],
                plane_in.at[slot],
                plane_send.at[number],
                plane_recv.at[number],
                plane_peer(dx, dy, 1),
            )

        for number, (dx, dy) in enumerate(plane):
            plane_copy(number, dx, dy, me * YS + y).start()
        plane_in[me * YS + y] = dense[y]

        old = jnp.concatenate(
            [depth[image * per_image : image * per_image + 1] for image in range(own_count)], axis=0
        )
        change = jnp.concatenate(
            [
                jnp.sum(
                    depth_grad[image * per_image : (image + 1) * per_image], axis=0, keepdims=True
                )
                for image in range(own_count)
            ],
            axis=0,
        )
        moved = old - depth_step * change
        for place in range(split):
            span = slice(place * share, (place + 1) * share)
            for component, values_now in enumerate(points + [confidence]):
                staging[place, component * pairs : (component + 1) * pairs, :share] = values_now[:, span]
            staging[place, 4 * pairs : 4 * pairs + own_count, :share] = moved[:, span]

        def result_copy(step, slot):
            return remote(
                staging.at[lax.rem(me + step, split)],
                result_ref.at[slot],
                x_send.at[split + step],
                x_recv.at[split + step],
                mate(step),
            )

        for step in range(1, split):
            result_copy(step, me).start()
        result_ref[me] = staging[me]
        for number, (dx, dy) in enumerate(plane):
            source = lax.rem(me + split - dx, split) * YS + lax.rem(y + YS - dy, YS)
            plane_copy(number, dx, dy, source).wait_recv()
        gathered = jnp.sum(plane_in[...], axis=0)
        part_sum[...] = gathered
        line_in[row] = gathered

        def line_copy(number, dz, dc, slot):
            return remote(
                part_sum,
                line_in.at[slot],
                line_send.at[number],
                line_recv.at[number],
                (y * rows_count + line_row(dz, dc, 1), me),
            )

        for number, (dz, dc) in enumerate(line):
            line_copy(number, dz, dc, row).start()
        for number, (dz, dc) in enumerate(line):
            line_copy(number, dz, dc, line_row(dz, dc, -1)).wait_recv()
        total_ref[...] = jnp.sum(line_in[...], axis=0)
        for step in range(1, split):
            depth_copy(step, me).wait_send()
            result_copy(step, behind(step)).wait_recv()
            result_copy(step, me).wait_send()
        for number, (dx, dy) in enumerate(plane):
            plane_copy(number, dx, dy, me * YS + y).wait_send()
        for number, (dz, dc) in enumerate(line):
            line_copy(number, dz, dc, row).wait_send()

    return rest


def pair_step(
    pick,
    patches,
    enc_proj,
    enc_out,
    embed,
    weights,
    head_rows,
    floats,
    ints,
    pairs,
    groups,
):
    images, split, share, _ = patches.shape
    tokens = share * split
    own_count = images // split
    local = enc_out.shape[0] * enc_out.shape[1]
    width = embed.shape[1]
    chunks = len(WIDTHS)
    count = len(link_plan(images, WIDTHS)[1])
    vmem = pl.BlockSpec(memory_space=pltpu.VMEM)
    per_dev = pairs // split
    result_rows = 4 * per_dev + 8
    rows = per_dev * tokens
    b16, f32, dma = jnp.bfloat16, jnp.float32, pltpu.SemaphoreType.DMA
    return pl.pallas_call(
        exchange_kernel,
        out_shape=(
            jax.ShapeDtypeStruct((split, result_rows, 128), f32),
            jax.ShapeDtypeStruct((16, 128), f32),
        ),
        in_specs=[pl.BlockSpec(memory_space=pltpu.SMEM)] + [vmem] * 8,
        out_specs=(vmem, vmem),
        scratch_shapes=[
            pltpu.VMEM((per_dev, split, share, width), b16),
            pltpu.VMEM((own_count, split, share, width), b16),
            pltpu.VMEM((4, split) + weights.shape[1:], b16),
            pltpu.VMEM((groups, 16, 128), b16),
            pltpu.VMEM((own_count, width // 128, 2 * tokens, 128), b16),
            pltpu.VMEM((rows, width), b16),
            pltpu.VMEM((rows, width), b16),
            pltpu.VMEM((rows, width), b16),
            pltpu.VMEM((per_dev, head_rows.shape[0], tokens), f32),
            pltpu.VMEM((split, 16, 128), f32),
            pltpu.VMEM((split, result_rows, 128), f32),
            pltpu.VMEM((YS, 16, 128), f32),
            pltpu.VMEM((split * YS, 16, 128), f32),
            pltpu.VMEM((16, 128), f32),
            pltpu.VMEM((2 * ZS, 16, 128), f32),
            dma((2 * split,)),
            dma((2 * split,)),
            dma((split * YS,)),
            dma((split * YS,)),
            dma((2 * ZS,)),
            dma((2 * ZS,)),
        ]
        + [pltpu.VMEM((groups * images, share, w), b16) for w in WIDTHS]
        + [pltpu.VMEM((pairs, share, w), b16) for w in WIDTHS]
        + [pltpu.VMEM((2, per_dev // 2, share, w), b16) for w in WIDTHS]
        + [
            pltpu.VMEM((split, images, share, local), b16),
            pltpu.VMEM((split, images, share, local), b16),
            pltpu.VMEM((split,) + enc_out.shape, b16),
            pltpu.VMEM((images, share, width), b16),
            dma((5 * split,)),
            dma((5 * split,)),
            dma((count,)),
            dma((count,)),
            dma((count + chunks,)),
            dma((count + chunks,)),
            dma((4 * split,)),
            dma((4 * split,)),
            dma((2 * ZS + YS,)),
            dma((2 * ZS + YS,)),
            dma((chunks, 3 * split)),
            dma((chunks, 3 * split)),
            dma((2 + chunks,)),
        ],
        compiler_params=pltpu.CompilerParams(
            collective_id=0, has_side_effects=True, vmem_limit_bytes=61 * 2**20
        ),
        name="pair_step",
    )(
        pick,
        patches,
        enc_proj,
        enc_out,
        embed,
        weights,
        head_rows,
        floats,
        ints,
    )


def shards(
    patches,
    encoder_proj,
    encoder_out,
    decoder_embed,
    decoder_proj,
    decoder_out,
    head_weight,
    partners,
    depths,
    camera_poses,
    valid_mask,
):
    images, tokens, model_width = patches.shape
    dec_width = decoder_embed.shape[1]
    enc_local = encoder_proj.shape[2]
    split = lax.axis_size("mp")
    own_count = images // split
    flat_partner = partners.reshape(-1)
    pair_count = flat_partner.shape[0]
    groups = lax.axis_size("img")
    here = lax.axis_index("img")
    weights = jnp.concatenate([jnp.transpose(decoder_proj, (1, 2, 0)), decoder_out[None]], axis=0)
    token_share = tokens // split
    owner = flat_partner // images
    shift_y = (here // (2 * ZS) - owner // (2 * ZS)) % YS
    shift_z = ((here // 2) % ZS - (owner // 2) % ZS) % ZS
    shift_core = (here - owner) % 2
    pick = ((shift_core * YS + shift_y) * ZS + shift_z) * images + flat_partner % images
    head_rows = jnp.pad(head_weight.T, ((0, 12), (0, 0)))
    own_pairs = pair_count // split
    depth_mask = jnp.stack([depths, valid_mask.astype(jnp.float32)], axis=0)
    depth_tiles = depth_mask.reshape(2, split, own_count, token_share).transpose(1, 0, 2, 3)
    depth_tiles = jnp.pad(
        depth_tiles.reshape(split, 2 * own_count, token_share),
        ((0, 0), (0, 16 - 2 * own_count), (0, 128 - token_share)),
    )
    pose_own = jnp.repeat(camera_poses.T, K, axis=0).reshape(split, own_pairs, 12)
    pose_own = jnp.pad(pose_own, ((0, 0), (0, 0), (0, 116)))
    pose_tile = jnp.pad(camera_poses, ((0, 4), (0, 128 - images)))[None]
    floats = jnp.concatenate([pose_own, depth_tiles, pose_tile], axis=0)
    parted = flat_partner.reshape(split, own_pairs)
    columns = jnp.broadcast_to(parted[:, :, None], (split, own_pairs, 128))
    lines = jnp.broadcast_to(jnp.pad(parted, ((0, 0), (0, 112)))[:, None], (split, 8, 128))
    ints = jnp.concatenate([columns, lines], axis=1)
    results, total = pair_step(
        pick,
        patches.reshape(images, split, token_share, model_width),
        jnp.transpose(encoder_proj, (1, 0, 2)),
        encoder_out.reshape(4, enc_local // 4, model_width),
        decoder_embed,
        weights,
        head_rows,
        floats,
        ints,
        pair_count,
        groups,
    )
    pointmap = results[:, : 4 * own_pairs, :token_share].reshape(split, 4, own_pairs, token_share)
    pointmap = pointmap.transpose(1, 0, 2, 3).reshape(4, pair_count, token_share)
    new_depths = results[:, 4 * own_pairs : 4 * own_pairs + own_count, :token_share]
    new_depths = new_depths.reshape(images, token_share)
    grad_pose = lax.dynamic_slice(total, (0, here % (2 * ZS) * images), (12, images))
    new_poses = camera_poses - pose_step * grad_pose
    return (pointmap, new_depths, new_poses)


def solution(mesh):
    placed = (
        P("img", None, None),
        P(None, None, "mp"),
        P("mp", None),
        P(),
        P(None, None, "mp"),
        P("mp", None),
        P(),
        P("img", None),
        P("img", "mp"),
        P(None, "img"),
        P("img", "mp"),
    )
    return jax.shard_map(
        shards,
        mesh=mesh,
        in_specs=placed,
        out_specs=(P(None, "img", "mp"), P("img", "mp"), P(None, "img")),
        check_vma=False,
    )
```

```python
import functools

import jax
import jax.numpy as jnp
from jax import lax
from jax.experimental import pallas as pl
from jax.experimental.pallas import tpu as pltpu
from jax.sharding import PartitionSpec as P

HD = 64
K = 8


epsilon = 1e-06
depth_step = 0.1
pose_step = 0.005


def norm_rows(values):
    average = jnp.mean(values, axis=-1, keepdims=True)
    centred = values - average
    variance = jnp.mean(centred * centred, axis=-1, keepdims=True)
    return (centred * lax.rsqrt(variance + epsilon)).astype(jnp.bfloat16)


YS, ZS, CORES = 4, 8, 2
FIRST = 5
WIDTHS = (384, 384)
RELAY = 18
AHEAD, DELAY = 4.0, 4.0
MESH = pl.DeviceIdType.MESH


def link_plan(images, spans):
    split = {"z": (0, FIRST), "y": (FIRST, images)}
    full = sum(spans)
    waiting = {"y+": [], "y-": [], "z+": [], "z-": []}
    free = {link: 0.0 for link in waiting}
    plan, flight, steps = [], [], []

    def push(now, chunk, link, source, target, span):
        waiting[link].append((chunk, len(waiting[link]) + 1000 * now, source, target, span))

    def issue(now):
        for link, queue in waiting.items():
            while queue and free[link] <= now + AHEAD:
                entry = min(queue)
                queue.remove(entry)
                chunk, _, source, target, span = entry
                free[link] = max(now, free[link]) + (span[1] - span[0]) * spans[chunk] / full
                flight.append((free[link] + DELAY, len(plan)))
                steps.append(("send", len(plan)))
                plan.append((chunk, link, source, target, span))

    def forward(now, chunk, dy, dz, span):
        if span[1] <= FIRST:
            low, high = split["z"]
            half = (low + high + 1) // 2
            if dy == 0:
                if dz in (0, 1, 2):
                    push(now, chunk, "z+", (dy, dz), (dy, dz + 1), span)
                if dz == 3:
                    push(now, chunk, "z+", (dy, dz), (dy, 4), (low, half))
                if dz in (0, 7, 6):
                    push(now, chunk, "z-", (dy, dz), (dy, (dz - 1) % ZS), span)
                if dz == 5:
                    push(now, chunk, "z-", (dy, dz), (dy, 4), (half, high))
                push(now, chunk, "y+", (dy, dz), (1, dz), span)
                push(now, chunk, "y-", (dy, dz), (3, dz), span)
            if dy == 1 and dz % 2 == 0:
                push(now, chunk, "y+", (dy, dz), (2, dz), span)
            if dy == 3 and dz % 2 == 1:
                push(now, chunk, "y-", (dy, dz), (2, dz), span)
        else:
            low, high = split["y"]
            half = (low + high + 1) // 2
            if dz == 0:
                if dy == 0:
                    push(now, chunk, "y+", (0, 0), (1, 0), span)
                    push(now, chunk, "y-", (0, 0), (3, 0), span)
                if dy == 1:
                    push(now, chunk, "y+", (1, 0), (2, 0), (low, half))
                if dy == 3:
                    push(now, chunk, "y-", (3, 0), (2, 0), (half, high))
            if dz in (0, 1, 2):
                push(now, chunk, "z+", (dy, dz), (dy, dz + 1), span)
            if dz == 3 and dy < 2:
                push(now, chunk, "z+", (dy, dz), (dy, 4), span)
            if dz in (0, 7, 6):
                push(now, chunk, "z-", (dy, dz), (dy, (dz - 1) % ZS), span)
            if dz == 5 and dy >= 2:
                push(now, chunk, "z-", (dy, dz), (dy, 4), span)

    for chunk in range(len(spans)):
        forward(0.0, chunk, 0, 0, split["z"])
        forward(0.0, chunk, 0, 0, split["y"])
    issue(0.0)
    while flight:
        entry = min(flight)
        flight.remove(entry)
        now, number = entry
        chunk, _, _, target, span = plan[number]
        steps.append(("wait", number))
        forward(now, chunk, target[0], target[1], span)
        issue(now)
    return steps, plan


def exchange_kernel(
    pick_ref,
    patches_ref,
    enc_proj_ref,
    enc_out_ref,
    embed_ref,
    weights_ref,
    head_ref,
    depth_ref,
    valid_ref,
    poses_ref,
    ints_ref,
    result_ref,
    total_ref,
    far_ref,
    own_ref,
    weights_all,
    pose_all,
    *scratch,
):
    finish, scratch = scratch[:17], scratch[17:]
    floats_ref, scratch = scratch[0], scratch[1:]
    chunks = len(WIDTHS)
    held, scratch = scratch[:chunks], scratch[chunks:]
    staged, scratch = scratch[:chunks], scratch[chunks:]
    relay, scratch = scratch[:chunks], scratch[chunks:]
    (
        mixed,
        mixed_all,
        enc_out_all,
        emb_ref,
        enc_send,
        enc_recv,
        ring_send,
        ring_recv,
        twin_send,
        twin_recv,
        line_send,
        line_recv,
        pose_send,
        pose_recv,
        far_send,
        far_recv,
        local_sem,
    ) = scratch
    columns = [slice(sum(WIDTHS[:c]), sum(WIDTHS[: c + 1])) for c in range(chunks)]
    images, share, width = emb_ref.shape
    here = lax.axis_index("img")
    me = lax.axis_index("mp")
    core = lax.rem(here, 2)
    z = lax.rem(here // 2, ZS)
    y = here // (2 * ZS)
    split = far_ref.shape[1]
    per_dev = far_ref.shape[0]
    half_dev = per_dev // 2

    def spot(yy, zz, cc):
        return ((yy * ZS + zz) * 2 + cc, me)

    def mate(step):
        return (here, lax.rem(me + step, split))

    def behind(step):
        return lax.rem(me + split - step, split)

    twin = spot(y, z, 1 - core)
    links = {
        "y+": spot(lax.rem(y + 1, YS), z, core),
        "y-": spot(lax.rem(y + YS - 1, YS), z, core),
        "z+": spot(y, lax.rem(z + 1, ZS), core),
        "z-": spot(y, lax.rem(z + ZS - 1, ZS), core),
    }
    line = [(dz, dc) for dz in range(ZS) for dc in range(CORES) if dz or dc]

    def line_peer(dz, dc, sign):
        return spot(y, lax.rem(z + ZS + sign * dz, ZS), lax.rem(core + dc, 2))

    def y_peer(dy, sign):
        return spot(lax.rem(y + YS + sign * dy, YS), z, core)

    barrier = pltpu.get_barrier_semaphore()
    peers = [line_peer(dz, dc, 1) for dz, dc in line]
    peers += [
        (spot(lax.rem(y + dy, YS), z, core)[0], lax.rem(me + dx, split))
        for dx in range(split)
        for dy in range(YS)
        if dx or dy
    ]
    for peer in peers:
        pl.semaphore_signal(barrier, inc=1, device_id=peer, device_id_type=MESH)
    floats_ref[...] = jnp.zeros_like(floats_ref)
    floats_ref[split, : poses_ref.shape[0], : poses_ref.shape[1]] = poses_ref[...]
    pair_count = images // split
    for quarter in range(split):
        lines = slice(quarter * pair_count, (quarter + 1) * pair_count)
        floats_ref[quarter, :pair_count, :share] = depth_ref[lines, :]
        floats_ref[quarter, pair_count : 2 * pair_count, :share] = valid_ref[lines, :].astype(
            jnp.float32
        )
    pose_all[here] = floats_ref[split].astype(jnp.bfloat16)
    pl.semaphore_wait(barrier, len(peers))

    def remote(source, target, send, recv, device):
        return pltpu.make_async_remote_copy(
            src_ref=source,
            dst_ref=target,
            send_sem=send,
            recv_sem=recv,
            device_id=device,
            device_id_type=MESH,
        )

    steps, plan = link_plan(images, WIDTHS)

    def block(chunk, side, slot, span):
        first = ((side * YS + slot[0]) * ZS + slot[1]) * images
        return held[chunk].at[pl.ds(first + span[0], span[1] - span[0])]

    def ring(number):
        chunk, link, source, target, span = plan[number]
        return remote(
            block(chunk, 0, source, span),
            block(chunk, 0, target, span),
            ring_send.at[number],
            ring_recv.at[number],
            links[link],
        )

    twins = [(entry[0], entry[3], entry[4]) for entry in plan]
    twins += [(chunk, (0, 0), (0, images)) for chunk in range(chunks)]

    def twin_copy(number):
        chunk, slot, span = twins[number]
        return remote(
            block(chunk, 0, slot, span),
            block(chunk, 1, slot, span),
            twin_send.at[number],
            twin_recv.at[number],
            twin,
        )

    def pose_line(dz, dc, number, slot):
        return remote(
            pose_all.at[slot],
            pose_all.at[slot],
            pose_send.at[number],
            pose_recv.at[number],
            line_peer(dz, dc, 1),
        )

    for number, (dz, dc) in enumerate(line):
        pose_line(dz, dc, number, here).start()

    pair_images = images // split

    def own_copy(step, slot):
        return remote(
            emb_ref.at[pl.ds(pair_images * lax.rem(me + step, split), pair_images)],
            own_ref.at[:, slot],
            line_send.at[step],
            line_recv.at[step],
            mate(step),
        )

    def weight_copy(step, slot):
        return remote(
            weights_ref.at[pl.ds(2 * core, 2)],
            weights_all.at[pl.ds(2 * core, 2), slot],
            line_send.at[split + step],
            line_recv.at[split + step],
            mate(step),
        )

    def weight_relay(step, slot):
        kind = 2 * core + (0 if step == 1 else 1)
        return remote(
            weights_all.at[pl.ds(kind, 1), slot],
            weights_all.at[pl.ds(kind, 1), slot],
            line_send.at[3 * split + step],
            line_recv.at[3 * split + step],
            mate(step),
        )

    def weight_twin(step, half, slot):
        return remote(
            weights_all.at[pl.ds(2 * half, 2), slot],
            weights_all.at[pl.ds(2 * half, 2), slot],
            line_send.at[2 * split + step],
            line_recv.at[2 * split + step],
            twin,
        )

    def far_direct(chunk, step, slot):
        return remote(
            staged[chunk].at[pl.ds(per_dev * lax.rem(me + step, split), per_dev)],
            far_ref.at[:, slot, :, columns[chunk]],
            far_send.at[chunk, step],
            far_recv.at[chunk, step],
            mate(step),
        )

    def far_relay(chunk, step):
        side = 0 if step == 1 else 1
        return remote(
            staged[chunk].at[pl.ds(per_dev * lax.rem(me + 2, split) + side * half_dev, half_dev)],
            relay[chunk].at[side],
            far_send.at[chunk, split + step],
            far_recv.at[chunk, split + step],
            mate(step),
        )

    def far_onward(chunk, step, slot):
        side = 0 if step == 1 else 1
        return remote(
            relay[chunk].at[side],
            far_ref.at[pl.ds(side * half_dev, half_dev), slot, :, columns[chunk]],
            far_send.at[chunk, 2 * split + step],
            far_recv.at[chunk, 2 * split + step],
            mate(step),
        )

    def out_copy(step, slot):
        return remote(
            enc_out_ref.at[pl.ds(2 * core, 2)],
            enc_out_all.at[slot, pl.ds(2 * core, 2)],
            enc_send.at[step],
            enc_recv.at[step],
            mate(step),
        )

    def out_relay(step, slot):
        part = pl.ds(2 * core + (0 if step == 1 else 1), 1)
        return remote(
            enc_out_all.at[slot, part],
            enc_out_all.at[slot, part],
            enc_send.at[3 * split + step],
            enc_recv.at[3 * split + step],
            mate(step),
        )

    def out_twin(step, half, slot):
        return remote(
            enc_out_all.at[slot, pl.ds(2 * half, 2)],
            enc_out_all.at[slot, pl.ds(2 * half, 2)],
            enc_send.at[4 * split + step],
            enc_recv.at[4 * split + step],
            twin,
        )

    def mixed_copy(part, step, slot):
        span = pl.ds(part * (images // 2), images // 2)
        return remote(
            mixed.at[lax.rem(me + step, split), span],
            mixed_all.at[slot, span],
            enc_send.at[split * (1 + part) + step],
            enc_recv.at[split * (1 + part) + step],
            mate(step),
        )

    for step in (1, 3):
        out_copy(step, me).start()
    enc_out_all[me] = enc_out_ref[...]
    tokens = share * split
    local = enc_out_ref.shape[0] * enc_out_ref.shape[1]
    last = (((1,), (1,)), ((), ()))
    first_half = lax.broadcasted_iota(jnp.int32, (1, 128), 1) < HD
    zero = jnp.zeros((), jnp.bfloat16)
    ones = jnp.ones((tokens, 128), jnp.bfloat16)

    def encode(pair, carry):
        picture = patches_ref[pl.ds(2 * pair, 2)].astype(jnp.float32)
        normed = norm_rows(picture.reshape(2 * tokens, -1))
        projected = [
            jnp.dot(normed, enc_proj_ref[kind], preferred_element_type=jnp.float32).astype(
                jnp.bfloat16
            )
            for kind in range(3)
        ]
        places = [(image, first) for image in range(2) for first in range(0, local, 128)]

        def take(kind, image, first):
            lines = slice(image * tokens, (image + 1) * tokens)
            return projected[kind][lines, first : first + 128]

        scores = []
        for image, first in places:
            query = take(0, image, first) * jnp.bfloat16(HD ** (-0.5))
            both = jnp.concatenate(
                [jnp.where(first_half, query, zero), jnp.where(first_half, zero, query)], axis=0
            )
            scores.append(
                lax.dot_general(
                    both, take(1, image, first), last, preferred_element_type=jnp.float32
                )
            )
        expos = [
            jnp.exp(each - jnp.max(each, axis=1, keepdims=True)).astype(jnp.bfloat16)
            for each in scores
        ]
        sums = [
            jnp.dot(
                each,
                jnp.concatenate([take(2, image, first), ones], axis=1),
                preferred_element_type=jnp.float32,
            )
            for each, (image, first) in zip(expos, places)
        ]
        for each, (image, first) in zip(sums, places):
            got = each[:, :128] / each[:, 128:]
            got = jnp.where(first_half, got[:tokens], got[tokens:])
            for place in range(split):
                mixed[place, pair * 2 + image, :, first : first + 128] = got[
                    place * share : (place + 1) * share
                ].astype(jnp.bfloat16)
        return carry

    lax.fori_loop(0, images // 4, encode, 0)
    for step in range(1, split):
        mixed_copy(0, step, me).start()
    for step in (1, 3):
        out_copy(step, behind(step)).wait_recv()
        out_relay(step, behind(step)).start()
        out_twin(step, core, behind(step)).start()
    lax.fori_loop(images // 4, images // 2, encode, 0)
    for step in range(1, split):
        mixed_copy(1, step, me).start()
    for step in (1, 3):
        out_relay(step, behind(2)).wait_recv()
    out_twin(2, core, behind(2)).start()
    for step in (1, 3):
        weight_copy(step, me).start()
    mixed_all[me] = mixed[me]
    encoded = patches_ref[:, me].astype(jnp.float32).reshape(images * share, -1)
    for step in range(split):
        source = behind(step)
        if step:
            out_twin(step, 1 - core, source).wait_recv()
            mixed_copy(0, step, source).wait_recv()
            mixed_copy(1, step, source).wait_recv()
        part = mixed_all[source].astype(jnp.float32).reshape(images * share, local)
        encoded = encoded + jnp.dot(
            part.astype(jnp.bfloat16), enc_out_all[source].reshape(local, -1), preferred_element_type=jnp.float32
        )
    embedded = jnp.dot(norm_rows(encoded), embed_ref[...], preferred_element_type=jnp.float32)
    embedded = embedded.astype(jnp.bfloat16).astype(jnp.float32)
    emb_ref[...] = embedded.reshape(images, share, width).astype(jnp.bfloat16)
    normed_rows = norm_rows(embedded).astype(jnp.float32).reshape(images, share, width)
    for chunk in range(chunks):
        held[chunk][pl.ds(0, images)] = normed_rows[:, :, columns[chunk]].astype(jnp.bfloat16)
    opening = [kind for kind, _ in steps].index("wait")
    for _, number in steps[:opening]:
        ring(number).start()
    for chunk in range(chunks):
        twin_copy(len(plan) + chunk).start()

    for step in range(1, split):
        own_copy(step, me).start()
    own_local = pltpu.make_async_copy(
        emb_ref.at[pl.ds(pair_images * me, pair_images)], own_ref.at[:, me], local_sem.at[0]
    )
    own_local.start()
    weight_local = pltpu.make_async_copy(weights_ref, weights_all.at[:, me], local_sem.at[1])
    weight_local.start()

    def far_local(chunk):
        return pltpu.make_async_copy(
            staged[chunk].at[pl.ds(per_dev * me, per_dev)],
            far_ref.at[:, me, :, columns[chunk]],
            local_sem.at[2 + chunk],
        )

    def choose(chunk):
        for number, entry in enumerate(twins):
            if entry[0] == chunk:
                twin_copy(number).wait_recv()

        def pick(index, carry):
            staged[chunk][index] = held[chunk][pick_ref[index]]
            return carry

        lax.fori_loop(0, per_dev * split, pick, 0, unroll=4)
        for step in (1, 3):
            far_relay(chunk, step).start()
        for step in (1, 3):
            far_direct(chunk, step, me).start()
        far_local(chunk).start()

    def pass_on(chunk):
        for step in (1, 3):
            far_relay(chunk, step).wait_recv()
            far_onward(chunk, step, behind(step)).start()

    def pose_cross(dy, row):
        return remote(
            pose_all.at[pl.ds(row * 2 * ZS, 2 * ZS)],
            pose_all.at[pl.ds(row * 2 * ZS, 2 * ZS)],
            pose_send.at[len(line) + dy - 1],
            pose_recv.at[len(line) + dy - 1],
            y_peer(dy, 1),
        )

    def pose_second():
        for number, (dz, dc) in enumerate(line):
            pose_line(dz, dc, number, line_peer(dz, dc, -1)[0]).wait_recv()
        for dy in range(1, YS):
            pose_cross(dy, y).start()

    def weights_second():
        for step in (1, 3):
            weight_copy(step, behind(step)).wait_recv()
            weight_relay(step, behind(step)).start()
            weight_twin(step, core, behind(step)).start()

    def weights_third():
        for step in (1, 3):
            weight_relay(step, behind(2)).wait_recv()
        weight_twin(2, core, behind(2)).start()

    waits = [number for kind, number in steps if kind == "wait"]
    final = {c: max(i for i, n in enumerate(waits) if plan[n][0] == c) for c in range(chunks)}
    events = {8: pose_second, len(waits) // 4: weights_second, len(waits) // 2: weights_third}
    later, pending, count = {}, [], 0
    for kind, number in steps[opening:]:
        if kind == "send":
            ring(number).start()
            continue
        for action in pending:
            action()
        pending = []
        ring(number).wait_recv()
        twin_copy(number).start()
        count += 1
        if count in events:
            pending.append(events[count])
        for chunk in range(chunks):
            if final[chunk] == count - 1:
                pending.append(functools.partial(choose, chunk))
                later[count + RELAY] = chunk
        if count in later:
            pending.append(functools.partial(pass_on, later.pop(count)))
    for action in pending:
        action()
    for chunk in later.values():
        pass_on(chunk)
    for dy in range(1, YS):
        pose_cross(dy, lax.rem(y + YS - dy, YS)).wait_recv()
    for step in range(1, split):
        own_copy(step, behind(step)).wait_recv()
        weight_twin(step, 1 - core, behind(step)).wait_recv()
    own_local.wait()
    weight_local.wait()
    for number in range(len(plan)):
        ring(number).wait_send()
    for number in range(len(twins)):
        twin_copy(number).wait_send()
    for number, (dz, dc) in enumerate(line):
        pose_line(dz, dc, number, here).wait_send()
    for dy in range(1, YS):
        pose_cross(dy, y).wait_send()
    for step in range(1, split):
        out_twin(step, core, behind(step)).wait_send()
        mixed_copy(0, step, me).wait_send()
        mixed_copy(1, step, me).wait_send()
        own_copy(step, me).wait_send()
        weight_twin(step, core, behind(step)).wait_send()
    for step in (1, 3):
        out_copy(step, me).wait_send()
        out_relay(step, behind(step)).wait_send()
        weight_copy(step, me).wait_send()
        weight_relay(step, behind(step)).wait_send()
    rest = decode_part(
        far_ref,
        own_ref,
        weights_all,
        head_ref,
        floats_ref,
        pose_all,
        ints_ref,
        result_ref,
        total_ref,
        *finish,
    )
    for chunk in range(chunks):
        far_local(chunk).wait()
        for step in (1, 3):
            far_relay(chunk, step).wait_send()
            far_direct(chunk, step, behind(step)).wait_recv()
            far_direct(chunk, step, me).wait_send()
            far_onward(chunk, step, behind(2)).wait_recv()
            far_onward(chunk, step, behind(step)).wait_send()
    rest()


def decode_part(
    far_ref,
    own_ref,
    weights_ref,
    head_ref,
    floats_ref,
    pose_all_ref,
    ints_ref,
    result_ref,
    total_ref,
    queries,
    keys,
    values,
    mixed,
    heads_all,
    depth_all,
    staging,
    dense,
    plane_in,
    part_sum,
    line_in,
    x_send,
    x_recv,
    plane_send,
    plane_recv,
    line_send,
    line_recv,
):
    width = own_ref.shape[3]
    pairs, _, tokens = heads_all.shape
    split = depth_all.shape[0]
    share = tokens // split
    here = lax.axis_index("img")
    me = lax.axis_index("mp")
    rows_count = 2 * ZS
    row = lax.rem(here, rows_count)
    y = here // rows_count
    plane = [(dx, dy) for dx in range(split) for dy in range(YS) if dx or dy]
    line = [(dz, dc) for dz in range(ZS) for dc in range(CORES) if dz or dc]

    def plane_peer(dx, dy, sign):
        return (
            lax.rem(y + YS + sign * dy, YS) * rows_count + row,
            lax.rem(me + split + sign * dx, split),
        )

    def line_row(dz, dc, sign):
        z = lax.rem(row // 2 + ZS + sign * dz, ZS)
        return z * 2 + lax.rem(lax.rem(row, 2) + dc, 2)

    def mate(step):
        return (here, lax.rem(me + step, split))

    def behind(step):
        return lax.rem(me + split - step, split)

    def remote(source, target, send, recv, device):
        return pltpu.make_async_remote_copy(
            src_ref=source,
            dst_ref=target,
            send_sem=send,
            recv_sem=recv,
            device_id=device,
            device_id_type=MESH,
        )

    blocks = width // 128
    own_count = own_ref.shape[0]
    per_image = pairs // own_count
    last = (((1,), (1,)), ((), ()))
    lane = lax.broadcasted_iota(jnp.int32, (1, 128), 1)
    first_half = lane < HD

    def weight(kind):
        return weights_ref[kind].reshape(width, width)

    rows = norm_rows(own_ref[...].astype(jnp.float32).reshape(own_count * tokens, width))
    projected = lax.dot_general(rows, weight(0), last, preferred_element_type=jnp.float32)
    projected = projected.astype(jnp.bfloat16) * jnp.bfloat16(HD ** (-0.5))
    zero = jnp.zeros((), jnp.bfloat16)
    for image in range(own_count):
        for block in range(blocks):
            part = projected[image * tokens : (image + 1) * tokens, block * 128 : (block + 1) * 128]
            queries[image, block, :tokens] = jnp.where(first_half, part, zero)
            queries[image, block, tokens:] = jnp.where(first_half, zero, part)

    def depth_copy(step, slot):
        return remote(
            floats_ref.at[lax.rem(me + step, split)],
            depth_all.at[slot],
            x_send.at[step],
            x_recv.at[step],
            mate(step),
        )

    for step in range(1, split):
        depth_copy(step, me).start()
    depth_all[me] = floats_ref[me]
    own_partner = ints_ref[me, :pairs]
    staging[...] = jnp.zeros_like(staging)
    members = own_count * split
    group_count, pose_rows, _ = pose_all_ref.shape
    lane_ids = lax.broadcasted_iota(jnp.int32, (pairs, 128), 1)
    chosen = (lane_ids == lax.rem(own_partner, members)).astype(jnp.bfloat16)
    candidates = lax.dot_general(
        pose_all_ref[...].reshape(group_count * pose_rows, 128),
        chosen,
        last,
        preferred_element_type=jnp.float32,
    ).reshape(group_count, pose_rows, pairs)
    owners = lax.broadcasted_iota(jnp.int32, (group_count, pose_rows, pairs), 0)
    held_by = lax.div(ints_ref[me, pairs : pairs + 1, :pairs], members)
    turned = jnp.sum(jnp.where(owners == held_by[None], candidates, 0.0), axis=0)
    same = lax.broadcasted_iota(jnp.int32, (pose_rows, pose_rows), 0) == lax.broadcasted_iota(
        jnp.int32, (pose_rows, pose_rows), 1
    )
    far_pose = lax.dot_general(
        turned.astype(jnp.bfloat16),
        same.astype(jnp.bfloat16),
        (((0,), (0,)), ((), ())),
        preferred_element_type=jnp.float32,
    )

    def rest():
        chunk = 4 * tokens

        def project(step, carry):
            span = pl.ds(pl.multiple_of(step * chunk, chunk), chunk)
            part = far_ref[pl.ds(step * 4, 4)].astype(jnp.float32)
            part = part.reshape(chunk, width).astype(jnp.bfloat16)
            keys[span, :] = lax.dot_general(
                part, weight(1), last, preferred_element_type=jnp.float32
            ).astype(jnp.bfloat16)
            values[span, :] = lax.dot_general(
                part, weight(2), last, preferred_element_type=jnp.float32
            ).astype(jnp.bfloat16)
            return carry

        lax.fori_loop(0, pairs // 4, project, 0, unroll=2)
        ones = jnp.ones((tokens, 128), jnp.bfloat16)

        def attend(pair, carry):
            span = pl.ds(pl.multiple_of(pair * tokens, tokens), tokens)
            image = pair // per_image
            columns = [slice(block * 128, (block + 1) * 128) for block in range(blocks)]
            scores = [
                lax.dot_general(
                    queries[image, block], keys[span, part], last, preferred_element_type=jnp.float32
                )
                for block, part in enumerate(columns)
            ]
            expos = [
                jnp.exp(each - jnp.max(each, axis=1, keepdims=True)).astype(jnp.bfloat16)
                for each in scores
            ]
            sums = [
                jnp.dot(
                    each,
                    jnp.concatenate([values[span, part], ones], axis=1),
                    preferred_element_type=jnp.float32,
                )
                for each, part in zip(expos, columns)
            ]
            for each, part in zip(sums, columns):
                got = each[:, :128] / each[:, 128:]
                mixed[span, part] = jnp.where(first_half, got[:tokens], got[tokens:]).astype(
                    jnp.bfloat16
                )
            return carry

        lax.fori_loop(0, pairs, attend, 0, unroll=2)

        def finish(step, carry):
            span = pl.ds(pl.multiple_of(step * chunk, chunk), chunk)
            image = step * 4 // per_image
            own = own_ref[image].astype(jnp.float32).reshape(tokens, width)
            settled = jnp.dot(mixed[span, :], weight(3), preferred_element_type=jnp.float32)
            settled = settled + jnp.concatenate([own] * 4, axis=0)
            heads = lax.dot_general(
                head_ref[...], norm_rows(settled), last, preferred_element_type=jnp.float32
            )
            for part in range(4):
                heads_all[step * 4 + part] = heads[:, part * tokens : (part + 1) * tokens]
            return carry

        lax.fori_loop(0, pairs // 4, finish, 0, unroll=2)
        for step in range(1, split):
            depth_copy(step, behind(step)).wait_recv()

        def widen(offset):
            both = jnp.concatenate(
                [depth_all[q, offset : offset + own_count, :share] for q in range(split)], axis=1
            )
            return jnp.concatenate(
                [
                    jnp.broadcast_to(both[image : image + 1], (per_image, tokens))
                    for image in range(own_count)
                ],
                axis=0,
            )

        depth = widen(0)
        valid = widen(own_count)
        token = lax.broadcasted_iota(jnp.int32, (1, tokens), 1)
        ray_x = (lax.rem(token, 16).astype(jnp.float32) - 7.5) * 0.125
        ray_y = (lax.div(token, 16).astype(jnp.float32) - (tokens // 16 - 1) * 0.5) * 0.125
        rays = [ray_x, ray_y, jnp.ones_like(ray_x)]
        points = [heads_all[:, component, :] for component in range(3)]
        confidence = 1.0 + jnp.exp(heads_all[:, 3, :])
        factor = valid * confidence * (2.0 / tokens)
        lane128 = lax.broadcasted_iota(jnp.int32, (pairs, 128), 1)
        mine_ids = me * own_count + lax.div(lax.broadcasted_iota(jnp.int32, (pairs, 128), 0), per_image)
        own_pose = lax.dot_general(
            (lane128 == mine_ids).astype(jnp.float32),
            floats_ref[split],
            last,
            precision=lax.Precision.HIGHEST,
            preferred_element_type=jnp.float32,
        )
        own_grad = jnp.zeros((pairs, 128), jnp.float32)
        far_grad = jnp.zeros((pairs, 128), jnp.float32)
        depth_grad = jnp.zeros((pairs, tokens), jnp.float32)
        for component in range(3):
            base = 4 * component
            direction = sum(own_pose[:, base + k : base + k + 1] * rays[k] for k in range(3))
            world = own_pose[:, base + 3 : base + 4] + depth * direction
            predicted = far_pose[:, base + 3 : base + 4] + sum(
                far_pose[:, base + k : base + k + 1] * points[k] for k in range(3)
            )
            slope = factor * (world - predicted)
            depth_grad = depth_grad + slope * direction
            scaled = slope * depth
            for k in range(4):
                mine = scaled * rays[k] if k < 3 else slope
                other = slope * points[k] if k < 3 else slope
                mine = jnp.sum(mine, axis=1, keepdims=True)
                other = jnp.sum(other, axis=1, keepdims=True)
                own_grad = jnp.where(lane128 == base + k, mine, own_grad)
                far_grad = jnp.where(lane128 == base + k, -other, far_grad)
        total_images = YS * 128
        ids = lax.broadcasted_iota(jnp.int32, (pairs, total_images), 1)
        pair_ids = lax.broadcasted_iota(jnp.int32, (pairs, total_images), 0)
        own_ids = (here * split + me) * own_count + lax.div(pair_ids, per_image)
        hits = jnp.concatenate([ids == own_ids, ids == own_partner[:, :1]], axis=0)
        table = lax.dot_general(
            jnp.concatenate([own_grad, far_grad], axis=0),
            hits.astype(jnp.float32),
            (((0,), (0,)), ((), ())),
            precision=lax.Precision.HIGHEST,
            preferred_element_type=jnp.float32,
        )
        for part in range(YS):
            dense[part] = table[:16, part * 128 : (part + 1) * 128]

        def plane_copy(number, dx, dy, slot):
            return remote(
                dense.at[lax.rem(y + dy, YS)],
                plane_in.at[slot],
                plane_send.at[number],
                plane_recv.at[number],
                plane_peer(dx, dy, 1),
            )

        for number, (dx, dy) in enumerate(plane):
            plane_copy(number, dx, dy, me * YS + y).start()
        plane_in[me * YS + y] = dense[y]

        old = jnp.concatenate(
            [depth[image * per_image : image * per_image + 1] for image in range(own_count)], axis=0
        )
        change = jnp.concatenate(
            [
                jnp.sum(
                    depth_grad[image * per_image : (image + 1) * per_image], axis=0, keepdims=True
                )
                for image in range(own_count)
            ],
            axis=0,
        )
        moved = old - depth_step * change
        for place in range(split):
            span = slice(place * share, (place + 1) * share)
            for component, values_now in enumerate(points + [confidence]):
                staging[place, component * pairs : (component + 1) * pairs, :share] = values_now[:, span]
            staging[place, 4 * pairs : 4 * pairs + own_count, :share] = moved[:, span]

        def result_copy(step, slot):
            return remote(
                staging.at[lax.rem(me + step, split)],
                result_ref.at[slot],
                x_send.at[split + step],
                x_recv.at[split + step],
                mate(step),
            )

        for step in range(1, split):
            result_copy(step, me).start()
        result_ref[me] = staging[me]
        for number, (dx, dy) in enumerate(plane):
            source = lax.rem(me + split - dx, split) * YS + lax.rem(y + YS - dy, YS)
            plane_copy(number, dx, dy, source).wait_recv()
        gathered = jnp.sum(plane_in[...], axis=0)
        part_sum[...] = gathered
        line_in[row] = gathered

        def line_copy(number, dz, dc, slot):
            return remote(
                part_sum,
                line_in.at[slot],
                line_send.at[number],
                line_recv.at[number],
                (y * rows_count + line_row(dz, dc, 1), me),
            )

        for number, (dz, dc) in enumerate(line):
            line_copy(number, dz, dc, row).start()
        for number, (dz, dc) in enumerate(line):
            line_copy(number, dz, dc, line_row(dz, dc, -1)).wait_recv()
        total_ref[...] = jnp.sum(line_in[...], axis=0)
        for step in range(1, split):
            depth_copy(step, me).wait_send()
            result_copy(step, behind(step)).wait_recv()
            result_copy(step, me).wait_send()
        for number, (dx, dy) in enumerate(plane):
            plane_copy(number, dx, dy, me * YS + y).wait_send()
        for number, (dz, dc) in enumerate(line):
            line_copy(number, dz, dc, row).wait_send()

    return rest


def pair_step(
    pick,
    patches,
    enc_proj,
    enc_out,
    embed,
    weights,
    head_rows,
    depths,
    valid,
    poses,
    ints,
    pairs,
    groups,
):
    images, split, share, _ = patches.shape
    tokens = share * split
    own_count = images // split
    local = enc_out.shape[0] * enc_out.shape[1]
    width = embed.shape[1]
    chunks = len(WIDTHS)
    count = len(link_plan(images, WIDTHS)[1])
    vmem = pl.BlockSpec(memory_space=pltpu.VMEM)
    per_dev = pairs // split
    result_rows = 4 * per_dev + 8
    rows = per_dev * tokens
    b16, f32, dma = jnp.bfloat16, jnp.float32, pltpu.SemaphoreType.DMA
    return pl.pallas_call(
        exchange_kernel,
        out_shape=(
            jax.ShapeDtypeStruct((split, result_rows, 128), f32),
            jax.ShapeDtypeStruct((16, 128), f32),
        ),
        in_specs=[pl.BlockSpec(memory_space=pltpu.SMEM)] + [vmem] * 10,
        out_specs=(vmem, vmem),
        scratch_shapes=[
            pltpu.VMEM((per_dev, split, share, width), b16),
            pltpu.VMEM((own_count, split, share, width), b16),
            pltpu.VMEM((4, split) + weights.shape[1:], b16),
            pltpu.VMEM((groups, 16, 128), b16),
            pltpu.VMEM((own_count, width // 128, 2 * tokens, 128), b16),
            pltpu.VMEM((rows, width), b16),
            pltpu.VMEM((rows, width), b16),
            pltpu.VMEM((rows, width), b16),
            pltpu.VMEM((per_dev, head_rows.shape[0], tokens), f32),
            pltpu.VMEM((split, 16, 128), f32),
            pltpu.VMEM((split, result_rows, 128), f32),
            pltpu.VMEM((YS, 16, 128), f32),
            pltpu.VMEM((split * YS, 16, 128), f32),
            pltpu.VMEM((16, 128), f32),
            pltpu.VMEM((2 * ZS, 16, 128), f32),
            dma((2 * split,)),
            dma((2 * split,)),
            dma((split * YS,)),
            dma((split * YS,)),
            dma((2 * ZS,)),
            dma((2 * ZS,)),
        ]
        + [pltpu.VMEM((split + 1, 16, 128), f32)]
        + [pltpu.VMEM((groups * images, share, w), b16) for w in WIDTHS]
        + [pltpu.VMEM((pairs, share, w), b16) for w in WIDTHS]
        + [pltpu.VMEM((2, per_dev // 2, share, w), b16) for w in WIDTHS]
        + [
            pltpu.VMEM((split, images, share, local), b16),
            pltpu.VMEM((split, images, share, local), b16),
            pltpu.VMEM((split,) + enc_out.shape, b16),
            pltpu.VMEM((images, share, width), b16),
            dma((5 * split,)),
            dma((5 * split,)),
            dma((count,)),
            dma((count,)),
            dma((count + chunks,)),
            dma((count + chunks,)),
            dma((4 * split,)),
            dma((4 * split,)),
            dma((2 * ZS + YS,)),
            dma((2 * ZS + YS,)),
            dma((chunks, 3 * split)),
            dma((chunks, 3 * split)),
            dma((2 + chunks,)),
        ],
        compiler_params=pltpu.CompilerParams(
            collective_id=0, has_side_effects=True, vmem_limit_bytes=61 * 2**20
        ),
        name="pair_step",
    )(
        pick,
        patches,
        enc_proj,
        enc_out,
        embed,
        weights,
        head_rows,
        depths,
        valid,
        poses,
        ints,
    )


def shards(
    patches,
    encoder_proj,
    encoder_out,
    decoder_embed,
    decoder_proj,
    decoder_out,
    head_weight,
    partners,
    depths,
    camera_poses,
    valid_mask,
):
    images, tokens, model_width = patches.shape
    dec_width = decoder_embed.shape[1]
    enc_local = encoder_proj.shape[2]
    split = lax.axis_size("mp")
    own_count = images // split
    flat_partner = partners.reshape(-1)
    pair_count = flat_partner.shape[0]
    groups = lax.axis_size("img")
    here = lax.axis_index("img")
    weights = jnp.concatenate([jnp.transpose(decoder_proj, (1, 2, 0)), decoder_out[None]], axis=0)
    token_share = tokens // split
    owner = flat_partner // images
    shift_y = (here // (2 * ZS) - owner // (2 * ZS)) % YS
    shift_z = ((here // 2) % ZS - (owner // 2) % ZS) % ZS
    shift_core = (here - owner) % 2
    pick = ((shift_core * YS + shift_y) * ZS + shift_z) * images + flat_partner % images
    head_rows = jnp.pad(head_weight.T, ((0, 12), (0, 0)))
    own_pairs = pair_count // split
    parted = flat_partner.reshape(split, own_pairs)
    columns = jnp.broadcast_to(parted[:, :, None], (split, own_pairs, 128))
    lines = jnp.broadcast_to(jnp.pad(parted, ((0, 0), (0, 112)))[:, None], (split, 8, 128))
    ints = jnp.concatenate([columns, lines], axis=1)
    results, total = pair_step(
        pick,
        patches.reshape(images, split, token_share, model_width),
        jnp.transpose(encoder_proj, (1, 0, 2)),
        encoder_out.reshape(4, enc_local // 4, model_width),
        decoder_embed,
        weights,
        head_rows,
        depths,
        valid_mask,
        camera_poses,
        ints,
        pair_count,
        groups,
    )
    pointmap = results[:, : 4 * own_pairs, :token_share].reshape(split, 4, own_pairs, token_share)
    pointmap = pointmap.transpose(1, 0, 2, 3).reshape(4, pair_count, token_share)
    new_depths = results[:, 4 * own_pairs : 4 * own_pairs + own_count, :token_share]
    new_depths = new_depths.reshape(images, token_share)
    grad_pose = lax.dynamic_slice(total, (0, here % (2 * ZS) * images), (12, images))
    new_poses = camera_poses - pose_step * grad_pose
    return (pointmap, new_depths, new_poses)


def solution(mesh):
    placed = (
        P("img", None, None),
        P(None, None, "mp"),
        P("mp", None),
        P(),
        P(None, None, "mp"),
        P("mp", None),
        P(),
        P("img", None),
        P("img", "mp"),
        P(None, "img"),
        P("img", "mp"),
    )
    return jax.shard_map(
        shards,
        mesh=mesh,
        in_specs=placed,
        out_specs=(P(None, "img", "mp"), P("img", "mp"), P(None, "img")),
        check_vma=False,
    )
```
